32 devices in a mesh: head: 2 (over y), seq: 16 (over z, x, core).
Axes of the slice: x: 2, y: 2, z: 4, core: 2. Of those that a mesh axis runs over, the one named last changes fastest.
Arguments:
- inputs: bfloat16 [2, 16, 512, 1024], P(None, 'seq'), may hold values from -6 to 6
- lengths: int32 [2, 16], replicated, may hold values from 128 to 512
- query_weight: bfloat16 [1024, 1024], P('seq', 'head'), may hold values from -0.1875 to 0.1875
- key_weight: bfloat16 [1024, 1024], P('seq', 'head'), may hold values from -0.1875 to 0.1875
- value_weight: bfloat16 [1024, 1024], P('seq', 'head'), may hold values from -0.1875 to 0.1875
- position_weight: bfloat16 [1024, 1024], P('seq', 'head'), may hold values from -0.1875 to 0.1875
- content_bias: bfloat16 [1024], P(('head', 'seq')), may hold values from -3 to 3
- position_bias: bfloat16 [1024], P(('head', 'seq')), may hold values from -3 to 3
- output_weight: bfloat16 [1024, 1024], P(('head', 'seq')), may hold values from -0.5 to 0.5
- output_bias: bfloat16 [1024], P('seq'), may hold values from -2 to 2
- first_gain: bfloat16 [1024], P('seq'), may hold values from 0.5 to 1.5
- first_shift: bfloat16 [1024], P('seq'), may hold values from -2 to 2
- up_weight: bfloat16 [1024, 4096], P(None, ('head', 'seq')), may hold values from -0.1875 to 0.1875
- up_bias: bfloat16 [4096], P(('head', 'seq')), may hold values from -2 to 2
- down_weight: bfloat16 [4096, 1024], P(('head', 'seq')), may hold values from -0.09375 to 0.09375
- down_bias: bfloat16 [1024], P('seq'), may hold values from -2 to 2
- second_gain: bfloat16 [1024], P('seq'), may hold values from 0.5 to 1.5
- second_shift: bfloat16 [1024], P('seq'), may hold values from -2 to 2
- squeeze_weight: bfloat16 [3072, 1024], P(None, ('head', 'seq')), may hold values from -0.109375 to 0.109375
- squeeze_bias: bfloat16 [1024], P(('head', 'seq')), may hold values from -2 to 2
- cotangent: bfloat16 [2, 16, 512, 1024], P(None, 'seq'), may hold values from -6 to 6
Outputs:
- outputs: bfloat16 [2, 16, 512, 1024], P(None, 'seq', 'head')
- input_grad: bfloat16 [2, 16, 512, 1024], P(None, 'seq', 'head')
- query_grad: float32 [1024, 1024], P('seq', 'head')
- key_grad: float32 [1024, 1024], P('seq', 'head')
- value_grad: float32 [1024, 1024], P('seq', 'head')
- position_grad: float32 [1024, 1024], P('seq', 'head')
- content_bias_grad: float32 [1024], P(('head', 'seq'))
- position_bias_grad: float32 [1024], P(('head', 'seq'))
- output_weight_grad: float32 [1024, 1024], P(('head', 'seq'))
- output_bias_grad: float32 [1024], P(('head', 'seq'))
- first_gain_grad: float32 [1024], P(('head', 'seq'))
- first_shift_grad: float32 [1024], P(('head', 'seq'))
- up_weight_grad: float32 [1024, 4096], P(None, ('head', 'seq'))
- up_bias_grad: float32 [4096], P(('head', 'seq'))
- down_weight_grad: float32 [4096, 1024], P(('head', 'seq'))
- down_bias_grad: float32 [1024], P(('head', 'seq'))
- second_gain_grad: float32 [1024], P(('head', 'seq'))
- second_shift_grad: float32 [1024], P(('head', 'seq'))
- squeeze_weight_grad: float32 [3072, 1024], P(None, ('head', 'seq'))
- squeeze_bias_grad: float32 [1024], P(('head', 'seq'))
The draws below stay inside these ranges and needn't reach their ends.
All inputs are finite; a program needn't handle non-finite values.
Results may differ from the reference program's by a relative error of at most 0.017.
Values may be sent and summed in bfloat16 or wider, within the bound.
A program may use at most 320 MiB of HBM per device.

```python
import jax
import jax.numpy as jnp
from jax import lax

D = 1024
HEADS = 8
HD = 128
FF = 4096
SEG = 512
BOOKS = 2
SEGS = 16


def plant(values, key, least, top_value):
    extent = values.shape
    spot = [jax.random.randint(jax.random.fold_in(key, axis), (), 0, extent[axis]) for axis in range(len(extent))]
    values = values.at[tuple(spot)].set(least)
    longest = extent.index(max(extent))
    spot[longest] = (spot[longest] + 1) % extent[longest]
    return values.at[tuple(spot)].set(top_value)


def block_scale(rng, shape, cuts, least, high):
    def one(axis_at, shards_of):
        heights = jax.random.uniform(jax.random.fold_in(jax.random.fold_in(rng, 6), axis_at), (shards_of,), jnp.float32, least / len(cuts), high / len(cuts))
        return jnp.repeat(jnp.exp(heights), shape[axis_at] // shards_of).reshape((-1,) + (1,) * (len(shape) - axis_at - 1))

    loudness = one(*cuts[0])
    for cut in cuts[1:]:
        loudness = loudness * one(*cut)
    return loudness


def centred(key, dims, deviation, reach, split=(), kind=jnp.bfloat16):
    result = jax.random.normal(key, dims, jnp.float32) * deviation
    if len(split) > 0:
        result = block_scale(key, dims, split, -0.22, 0.18) * result
    return jnp.clip(result, min=-reach, max=reach).astype(kind)


def setup_inputs(seed: int = 0) -> dict:
    key_of = jax.random.split(jax.random.key(seed), 22)
    inputs = centred(key_of[0], (BOOKS, SEGS, SEG, D), 1.0, 6.0, ((1, 16),))
    lengths = plant(jax.random.randint(key_of[1], (BOOKS, SEGS), SEG // 4, SEG + 1), jax.random.fold_in(key_of[1], 1), SEG // 4, SEG).astype(jnp.int32)
    query_weight = centred(key_of[2], (D, HEADS * HD), D ** -0.5, 0.1875, ((0, 16), (1, 2)))
    key_weight = centred(key_of[3], (D, HEADS * HD), D ** -0.5, 0.1875, ((0, 16), (1, 2)))
    value_weight = centred(key_of[4], (D, HEADS * HD), D ** -0.5, 0.1875, ((0, 16), (1, 2)))
    position_weight = centred(key_of[5], (D, HEADS * HD), D ** -0.5, 0.1875, ((0, 16), (1, 2)))
    content_bias = centred(key_of[6], (HEADS * HD,), 0.5, 3.0, ((0, 32),))
    position_bias = centred(key_of[7], (HEADS * HD,), 0.5, 3.0, ((0, 32),))
    output_weight = centred(key_of[8], (HEADS * HD, D), HD ** -0.5, 0.5, ((0, 32),))
    output_bias = centred(key_of[9], (D,), 0.3, 2.0, ((0, 16),))
    first_gain = jnp.clip(1.0 + 0.1 * jax.random.normal(key_of[10], (D,), jnp.float32), 0.5, 1.5).astype(jnp.bfloat16)
    first_shift = centred(key_of[11], (D,), 0.3, 2.0, ((0, 16),))
    up_weight = centred(key_of[12], (D, FF), D ** -0.5, 0.1875, ((1, 32),))
    up_bias = centred(key_of[13], (FF,), 0.3, 2.0, ((0, 32),))
    down_weight = centred(key_of[14], (FF, D), FF ** -0.5, 0.09375, ((0, 32),))
    down_bias = centred(key_of[15], (D,), 0.3, 2.0, ((0, 16),))
    second_gain = jnp.clip(1.0 + 0.1 * jax.random.normal(key_of[16], (D,), jnp.float32), 0.5, 1.5).astype(jnp.bfloat16)
    second_shift = centred(key_of[17], (D,), 0.3, 2.0, ((0, 16),))
    squeeze_weight = centred(key_of[18], (3 * D, D), (3 * D) ** -0.5, 0.109375, ((1, 32),))
    squeeze_bias = centred(key_of[19], (D,), 0.3, 2.0, ((0, 32),))
    cotangent = centred(key_of[20], (BOOKS, SEGS, SEG, D), 1.0, 6.0, ((1, 16),))
    return {"inputs": inputs, "lengths": lengths, "query_weight": query_weight, "key_weight": key_weight, "value_weight": value_weight, "position_weight": position_weight, "content_bias": content_bias, "position_bias": position_bias, "output_weight": output_weight, "output_bias": output_bias, "first_gain": first_gain, "first_shift": first_shift, "up_weight": up_weight, "up_bias": up_bias, "down_weight": down_weight, "down_bias": down_bias, "second_gain": second_gain, "second_shift": second_shift, "squeeze_weight": squeeze_weight, "squeeze_bias": squeeze_bias, "cotangent": cotangent}


@jax.custom_vjp
def low(v):
    return lax.optimization_barrier(v.astype(jnp.bfloat16)).astype(jnp.float32)

@jax.custom_vjp
def low_back(v):
    return v

def low_keep(v):
    return (low(v), None)

def low_pass(kept, grad):
    return (grad,)

def back_keep(v):
    return (v, None)

def back_low(kept, grad):
    return (low(grad),)
low.defvjp(low_keep, low_pass)
low_back.defvjp(back_keep, back_low)
highest = lax.Precision.HIGHEST
epsilon = 1e-05

def matmul(left, right):
    return jnp.dot(left, right, precision=highest)

def table_rows(width, count):
    distance = jnp.arange(count - 1, -1, -1).astype(jnp.float32)[:, None]
    frequency = 10000.0 ** (-jnp.arange(0, width, 2).astype(jnp.float32) / width)
    angles = distance * frequency[None, :]
    return jnp.concatenate([jnp.sin(angles), jnp.cos(angles)], axis=1)

def normalize(values, norm_gain, norm_bias):
    centre = values - lax.optimization_barrier(jnp.mean(values, axis=-1, keepdims=True))
    spread = lax.optimization_barrier(jnp.mean(centre * centre, axis=-1, keepdims=True))
    return centre * lax.rsqrt(spread + epsilon) * norm_gain + norm_bias

def realign(scores):
    head_count, row_count, col_count = scores.shape
    padded = jnp.pad(scores, ((0, 0), (0, 0), (0, row_count)))
    flattened = padded.reshape(head_count, row_count * (col_count + row_count))
    flattened = lax.slice_in_dim(flattened, row_count - 1, row_count - 1 + row_count * (col_count + row_count - 1), axis=1)
    return flattened.reshape(head_count, row_count, col_count + row_count - 1)[:, :, :col_count]

def rows_valid(window_lengths, row_count):
    positions = jnp.arange(3 * row_count).astype(jnp.int32)
    blocks = positions // row_count
    chosen = jnp.arange(3).astype(jnp.int32)
    row_limit = lax.optimization_barrier(jnp.sum(jnp.where(blocks[:, None] == chosen[None, :], window_lengths[None, :3], 0), axis=1))
    return positions % row_count < row_limit

def keys_valid(window_lengths, row_count):
    history_ok = rows_valid(window_lengths, row_count)
    places = jnp.arange(row_count).astype(jnp.int32)
    return jnp.concatenate([history_ok[::3], places < window_lengths[3], places < window_lengths[4]])

def squeeze(grouped, squeeze_weight, squeeze_bias):
    return low(low_back(matmul(grouped, squeeze_weight) + squeeze_bias))

def attend(squeezed, memory, current, allowed_keys, query_weight, key_weight, value_weight, position_weight, content_bias, position_bias):
    row_count, width = current.shape
    head_count = query_weight.shape[1] // HD
    scaling = HD ** (-0.5)
    keys_in = jnp.concatenate([squeezed, memory, current], axis=0)
    query = low_back(matmul(current, query_weight))
    content_query = low((query + content_bias) * scaling).reshape(row_count, head_count, HD)
    place_query = low((query + position_bias) * scaling).reshape(row_count, head_count, HD)
    key_rows = low(low_back(matmul(keys_in, key_weight))).reshape(3 * row_count, head_count, HD)
    value_rows = low(low_back(matmul(keys_in, value_weight))).reshape(3 * row_count, head_count, HD)
    places = low(low_back(matmul(low(table_rows(width, 3 * row_count)), position_weight))).reshape(3 * row_count, head_count, HD)
    content = jnp.einsum('ihd,jhd->hij', content_query, key_rows, precision=highest)
    located = realign(jnp.einsum('ihd,chd->hic', place_query, places, precision=highest))
    scores = low_back(content + located)
    key_index = jnp.arange(3 * row_count).astype(jnp.int32)
    query_index = jnp.arange(row_count).astype(jnp.int32)
    allowed = allowed_keys[None, :] & (key_index[None, :] <= 2 * row_count + query_index[:, None])
    scores = jnp.where(allowed[None], scores, -1e+30)
    largest = lax.optimization_barrier(jnp.max(scores, axis=-1, keepdims=True))
    exp_scores = jnp.exp(scores - largest)
    probability = low(exp_scores / lax.optimization_barrier(jnp.sum(exp_scores, axis=-1, keepdims=True)))
    blended = jnp.einsum('hij,jhd->ihd', probability, value_rows, precision=highest)
    return low(low_back(blended.reshape(row_count, head_count * HD)))

def finish(attended, residual, output_weight, output_bias, first_gain, first_shift, up_weight, up_bias, down_weight, down_bias, second_gain, second_shift):
    blended = residual + low_back(matmul(attended, output_weight)) + output_bias
    normed = low(normalize(blended, first_gain, first_shift))
    hidden = low(jax.nn.gelu(low_back(matmul(normed, up_weight) + up_bias), approximate=True))
    return normalize(normed + low_back(matmul(hidden, down_weight)) + down_bias, second_gain, second_shift)

def segment_layer(window, window_lengths, weights):
    query_weight, key_weight, value_weight, position_weight, content_bias, position_bias, output_weight, output_bias, first_gain, first_shift, up_weight, up_bias, down_weight, down_bias, second_gain, second_shift, squeeze_weight, squeeze_bias = weights
    row_count = window.shape[1]
    width = window.shape[2]
    history_ok = rows_valid(window_lengths, row_count).astype(jnp.float32)
    stacked = window[:3].reshape(3 * row_count, width) * history_ok[:, None]
    squeezed = squeeze(stacked.reshape(row_count, 3 * width), squeeze_weight, squeeze_bias)
    attended = attend(squeezed, window[3], window[4], keys_valid(window_lengths, row_count), query_weight, key_weight, value_weight, position_weight, content_bias, position_bias)
    return finish(attended, window[4], output_weight, output_bias, first_gain, first_shift, up_weight, up_bias, down_weight, down_bias, second_gain, second_shift)

def reference(inputs, lengths, query_weight, key_weight, value_weight, position_weight, content_bias, position_bias, output_weight, output_bias, first_gain, first_shift, up_weight, up_bias, down_weight, down_bias, second_gain, second_shift, squeeze_weight, squeeze_bias, cotangent):
    weights = tuple((weight.astype(jnp.float32) for weight in (query_weight, key_weight, value_weight, position_weight, content_bias, position_bias, output_weight, output_bias, first_gain, first_shift, up_weight, up_bias, down_weight, down_bias, second_gain, second_shift, squeeze_weight, squeeze_bias)))
    padded_lengths = jnp.concatenate([jnp.zeros((BOOKS, 4), jnp.int32), lengths.astype(jnp.int32)], axis=1)

    def forward(inputs_float, *weight_float):
        padded = jnp.concatenate([jnp.zeros((BOOKS, 4, SEG, D), jnp.float32), inputs_float], axis=1)

        def per_segment(index):
            book_id = index // SEGS
            segment_id = index % SEGS
            book_rows = lax.dynamic_index_in_dim(padded, book_id, 0, keepdims=False)
            window = lax.dynamic_slice_in_dim(book_rows, segment_id, 5, 0)
            book_lengths = lax.dynamic_index_in_dim(padded_lengths, book_id, 0, keepdims=False)
            window_lengths = lax.dynamic_slice_in_dim(book_lengths, segment_id, 5, 0)
            return segment_layer(window, window_lengths, weight_float)
        mapped = lax.map(jax.checkpoint(per_segment), jnp.arange(BOOKS * SEGS).astype(jnp.int32))
        return mapped.reshape(BOOKS, SEGS, SEG, D)
    outputs, pullback = jax.vjp(forward, inputs.astype(jnp.float32), *weights)
    gradients = pullback(cotangent.astype(jnp.float32))
    return (outputs.astype(jnp.bfloat16), gradients[0].astype(jnp.bfloat16), gradients[1], gradients[2], gradients[3], gradients[4], gradients[5], gradients[6], gradients[7], gradients[8], gradients[9], gradients[10], gradients[11], gradients[12], gradients[13], gradients[14], gradients[15], gradients[16], gradients[17], gradients[18])
```

```python
import functools

import jax
import jax.numpy as jnp
import numpy as np
from jax import lax
from jax.experimental import pallas as pl
from jax.experimental.pallas import tpu as pltpu
from jax.sharding import PartitionSpec as P

HD = 128
BF = jnp.bfloat16
F32 = jnp.float32
epsilon = 1e-05
MIB = 1024 * 1024


def mm(left, right, contract=((1,), (0,)), out=F32):
    return lax.dot_general(left, right, (contract, ((), ())), preferred_element_type=F32).astype(out)


def mm_nt(left, right, out=F32):
    return mm(left, right, ((1,), (1,)), out)


def mm_tn(left, right, out=F32):
    return mm(left, right, ((0,), (0,)), out)


def shifted(array, axis, by):
    count = lax.axis_size(axis)
    pairs = [(i, i + by) for i in range(count) if 0 <= i + by < count]
    return lax.ppermute(array, axis, pairs)


def table_rows(width, count):
    distance = np.arange(count - 1, -1, -1).astype(np.float32)[:, None]
    exponent = -np.arange(0, width, 2).astype(np.float32) / np.float32(width)
    frequency = np.power(np.float32(10000.0), exponent).astype(np.float32)
    angles = (distance * frequency[None, :]).astype(np.float32)
    return np.concatenate([np.sin(angles), np.cos(angles)], axis=1).astype(BF)


def squeeze_layout(rows):
    pad = -(-(rows // 3 + 2) // 16) * 16
    taps = np.zeros((3, rows, 3 * pad), np.float32)
    collect = np.zeros((rows, 3 * pad), np.float32)
    biased = np.zeros((3 * pad, 1), np.float32)
    for role in range(3):
        first = role * rows // 3
        for i in range(rows):
            flat = role * rows + i
            taps[flat % 3, i, role * pad + flat // 3 - first] = 1.0
            collect[flat // 3, role * pad + flat // 3 - first] = 1.0
        for c in range(first, ((role + 1) * rows - 1) // 3 + 1):
            if role == 0 or 3 * c >= role * rows:
                biased[role * pad + c - first] = 1.0
    return pad, taps.astype(BF), collect.astype(BF), biased


def attend_forward_kernel(bias_ref, cb_ref, pb_ref, q_ref, k_ref, v_ref, pl_ref, out_ref, p_ref, s_scr, x_scr):
    rows = q_ref.shape[0]
    keys = k_ref.shape[0]
    scale = HD ** (-0.5)
    q = q_ref[...]
    content_query = ((q + cb_ref[...]) * scale).astype(BF)
    place_query = ((q + pb_ref[...]) * scale).astype(BF)
    s_scr[...] = mm_nt(content_query, k_ref[...])
    x_scr[...] = mm_nt(place_query, pl_ref[...])
    step = 32
    bias = bias_ref[...]
    for start in range(0, rows, step):
        here = slice(start, start + step)
        located = pltpu.roll(
            x_scr[here], (start + keys - rows + 1) % keys, 1, stride=1, stride_axis=0
        )
        scores = s_scr[here] + located + bias
        row = start + lax.broadcasted_iota(jnp.int32, scores.shape, 0)
        col = lax.broadcasted_iota(jnp.int32, scores.shape, 1)
        scores = jnp.where(col <= 2 * rows + row, scores, -1e30)
        top = jnp.max(scores, axis=1, keepdims=True)
        weights = jnp.exp(scores - top)
        total = jnp.sum(weights, axis=1, keepdims=True)
        p_ref[0, here] = (weights * (1.0 / total)).astype(BF)
    out_ref[...] = mm(p_ref[0], v_ref[...]).astype(BF)


def attend_backward_kernel(
    cb_ref, pb_ref, q_ref, k_ref, v_ref, pl_ref, p_ref, do_ref,
    dq_ref, dcb_ref, dpb_ref, dk_ref, dv_ref, dpl_ref,
    dp_scr, ds_scr, dx_scr,
):
    rows = q_ref.shape[0]
    keys = k_ref.shape[0]
    scale = HD ** (-0.5)
    q = q_ref[...]
    content_query = ((q + cb_ref[...]) * scale).astype(BF)
    place_query = ((q + pb_ref[...]) * scale).astype(BF)
    block = 128
    flip = (
        lax.broadcasted_iota(jnp.int32, (block, block), 0)
        + lax.broadcasted_iota(jnp.int32, (block, block), 1)
        == block - 1
    ).astype(BF)
    dp_scr[...] = mm_nt(do_ref[...], v_ref[...])
    step = 32
    for start in range(0, rows, step):
        here = slice(start, start + step)
        prob = p_ref[0, here].astype(F32)
        dprob = dp_scr[here]
        delta = jnp.sum(prob * dprob, axis=1, keepdims=True)
        ds_scr[here] = (prob * (dprob - delta)).astype(BF)
    dv_ref[...] = mm_tn(do_ref[...], p_ref[0]).T.astype(BF)
    dk_ref[...] = mm_tn(content_query, ds_scr[...]).T.astype(BF)
    dcq = mm(ds_scr[...], k_ref[...]) * scale
    flipped = []
    for start in range(0, rows, block):
        here = slice(start, start + block)
        dp_scr[here] = mm(flip, ds_scr[here])
        flipped.append(mm(flip, place_query[here]).astype(BF))
        dx_scr[here] = pltpu.roll(
            dp_scr[here], rows - block - start, 1, stride=1, stride_axis=0
        ).astype(BF)
    dpl_ref[...] = mm_tn(jnp.concatenate(flipped, axis=0), dx_scr[...]).T.astype(BF)
    dpq_flipped = mm(dx_scr[...], pl_ref[...]) * scale
    dpq = []
    for start in range(0, rows, block):
        piece = dpq_flipped[start : start + block]
        high = piece.astype(BF)
        dpq.append(mm(flip, high) + mm(flip, (piece - high.astype(F32)).astype(BF)))
    dpq = jnp.concatenate(dpq, axis=0)
    dq_ref[...] = (dcq + dpq).astype(BF)
    dcb_ref[...] = jnp.sum(dcq, axis=0, keepdims=True)
    dpb_ref[...] = jnp.sum(dpq, axis=0, keepdims=True)


def attend_forward(key_bias, content_bias, position_bias, query, keys, values, places):
    rows, width = query.shape
    count = keys.shape[0]
    heads = width // HD
    row_spec = pl.BlockSpec((rows, HD), lambda h: (0, h))
    key_spec = pl.BlockSpec((count, HD), lambda h: (0, h))
    vec_spec = pl.BlockSpec((1, HD), lambda h: (0, h))
    return pl.pallas_call(
        attend_forward_kernel,
        grid=(heads,),
        in_specs=[pl.BlockSpec((1, count), lambda h: (0, 0)), vec_spec, vec_spec, row_spec, key_spec, key_spec, key_spec],
        out_specs=[row_spec, pl.BlockSpec((1, rows, count), lambda h: (h, 0, 0))],
        out_shape=[
            jax.ShapeDtypeStruct((rows, width), BF),
            jax.ShapeDtypeStruct((heads, rows, count), BF),
        ],
        scratch_shapes=[pltpu.VMEM((rows, count), F32), pltpu.VMEM((rows, count), F32)],
        compiler_params=pltpu.CompilerParams(vmem_limit_bytes=48 * MIB),
        cost_estimate=pl.CostEstimate(
            flops=6 * rows * count * width, bytes_accessed=2 * heads * rows * count, transcendentals=heads * rows * count
        ),
        name="attend_forward",
    )(key_bias, content_bias, position_bias, query, keys, values, places)


def attend_backward(content_bias, position_bias, query, keys, values, places, probs, d_out):
    rows, width = query.shape
    count = keys.shape[0]
    heads = width // HD
    row_spec = pl.BlockSpec((rows, HD), lambda h: (0, h))
    key_spec = pl.BlockSpec((count, HD), lambda h: (0, h))
    vec_spec = pl.BlockSpec((1, HD), lambda h: (0, h))
    p_spec = pl.BlockSpec((1, rows, count), lambda h: (h, 0, 0))
    return pl.pallas_call(
        attend_backward_kernel,
        grid=(heads,),
        in_specs=[vec_spec, vec_spec, row_spec, key_spec, key_spec, key_spec, p_spec, row_spec],
        out_specs=[row_spec, vec_spec, vec_spec, key_spec, key_spec, key_spec],
        out_shape=[
            jax.ShapeDtypeStruct((rows, width), BF),
            jax.ShapeDtypeStruct((1, width), F32),
            jax.ShapeDtypeStruct((1, width), F32),
            jax.ShapeDtypeStruct((count, width), BF),
            jax.ShapeDtypeStruct((count, width), BF),
            jax.ShapeDtypeStruct((count, width), BF),
        ],
        scratch_shapes=[
            pltpu.VMEM((rows, count), F32),
            pltpu.VMEM((rows, count), BF),
            pltpu.VMEM((rows, count), BF),
        ],
        compiler_params=pltpu.CompilerParams(vmem_limit_bytes=48 * MIB),
        cost_estimate=pl.CostEstimate(
            flops=12 * rows * count * width, bytes_accessed=2 * heads * rows * count, transcendentals=0
        ),
        name="attend_backward",
    )(content_bias, position_bias, query, keys, values, places, probs, d_out)


MESH = pl.DeviceIdType.MESH
CORE, XFLIP, YFLIP, UP, DOWN = range(5)


class Place:
    def __init__(self, count):
        self.count = count
        self.line_size = count // 4
        self.h = lax.axis_index("head")
        self.s = lax.axis_index("seq")
        self.a = self.s // 4
        self.b = (self.s // 2) % 2
        self.c = self.s % 2

    def seq_of(self, a, b, c):
        return a * 4 + b * 2 + c

    def neighbour(self, kind):
        s, h = self.s, self.h
        if kind == CORE:
            return (h, s + 1 - 2 * self.c)
        if kind == XFLIP:
            return (h, s + 2 - 4 * self.b)
        if kind == YFLIP:
            return (1 - h, s)
        return (h, s + 4) if kind == UP else (h, s - 4)

    def when(self, kind):
        if kind == UP:
            return pl.when(self.a < self.line_size - 1)
        if kind == DOWN:
            return pl.when(self.a > 0)
        return lambda run: run()

    def barrier(self):
        barrier = pltpu.get_barrier_semaphore()
        for kind in range(5):
            @self.when(kind)
            def _(kind=kind):
                pl.semaphore_signal(barrier, inc=1, device_id=self.neighbour(kind), device_id_type=MESH)
        ends = jnp.where(self.a == 0, 1, 0) + jnp.where(self.a == self.line_size - 1, 1, 0)
        pl.semaphore_wait(barrier, 5 - ends)


class Gather:
    def __init__(self, place, shards, fulls, views, orders, local_sem, send_sem, recv_sem):
        self.place, self.shards, self.fulls, self.views, self.orders = place, shards, fulls, views, orders
        self.local_sem, self.send_sem, self.recv_sem = local_sem, send_sem, recv_sem

    def view(self, u, h, s):
        return self.views[u](self.fulls[u], h, s)

    def copy(self, u, kind, h, s, own=False):
        slot = h * self.place.count + s
        line, plane = s // 4, slot // 2
        size = self.place.line_size
        sent = {UP: line, DOWN: size + line, XFLIP: 2 * size + plane, YFLIP: 6 * size + plane, CORE: 10 * size + plane}
        there = self.view(u, h, s)
        return pltpu.make_async_remote_copy(
            src_ref=self.shards[u] if own else there,
            dst_ref=there,
            send_sem=self.send_sem.at[u, sent[kind]],
            recv_sem=self.recv_sem.at[u, slot],
            device_id=self.place.neighbour(kind),
            device_id_type=MESH,
        )

    def local(self, u):
        return pltpu.make_async_copy(self.shards[u], self.view(u, self.place.h, self.place.s), self.local_sem.at[u])

    def sources(self):
        p = self.place
        found = []
        for t in range(p.line_size):
            for sign in ((1, -1) if t else (0,)):
                o = p.a - sign * t
                valid = None if not t else (o >= 0 if sign > 0 else o <= p.line_size - 1)
                for one in (0, 1):
                    for two in (0, 1):
                        if t or one or two:
                            found.append((t + one + two, o, sign, one, two, valid))
        return sorted(found, key=lambda e: e[0])

    def slot_of(self, u, o, one, two):
        p = self.place
        x, y = (one, two) if self.orders[u] == 0 else (two, one)
        h = 1 - p.h if y else p.h
        b = 1 - p.b if x else p.b
        return h, p.seq_of(o, b, p.c)

    def flips(self, u):
        return (XFLIP, YFLIP) if self.orders[u] == 0 else (YFLIP, XFLIP)

    def onward(self, u, sign, one, two):
        first, second = self.flips(u)
        kinds = []
        if not one and not two:
            kinds += [UP] if sign > 0 else [DOWN] if sign < 0 else [UP, DOWN]
            kinds += [first]
        if not two:
            kinds += [second]
        return kinds + [CORE]

    def send(self, u, kind, h, s, own, wait):
        @self.place.when(kind)
        def _():
            copy = self.copy(u, kind, h, s, own)
            if wait:
                copy.wait_send()
            else:
                copy.start()

    def steps(self):
        p = self.place
        units = range(len(self.shards))

        def begin(wait=False):
            for u in units:
                if wait:
                    self.local(u).wait()
                else:
                    self.local(u).start()
                for kind in self.onward(u, 0, 0, 0):
                    self.send(u, kind, p.h, p.s, True, wait)

        def pass_on(entry, wait):
            depth, o, sign, one, two, valid = entry

            def run():
                for u in units:
                    h, s = self.slot_of(u, o, one, two)
                    if not wait:
                        self.copy(u, CORE, h, s).wait_recv()
                    for kind in self.onward(u, sign, one, two):
                        self.send(u, kind, h, s, False, wait)

            if valid is None:
                run()
            else:
                pl.when(valid)(run)

        def finish():
            for h in (0, 1):
                for a in range(p.line_size):
                    for b in (0, 1):
                        for u in units:
                            self.copy(u, CORE, h, p.seq_of(a, b, 1 - p.c)).wait_recv()
            begin(True)
            for entry in self.sources():
                pass_on(entry, True)

        return [begin] + [functools.partial(pass_on, entry, False) for entry in self.sources()] + [finish]


def gather_kernel(count, small_names, *refs):
    (qkvp, sq, o, up, down, small), refs = refs[:6], refs[6:]
    (qkvp_f, sq_f, o_f, up_f, down_f, vec, vec_up), refs = refs[:7], refs[7:]
    small_f, local_sem, send_sem, recv_sem = refs
    place = Place(count)
    place.barrier()
    r, w = qkvp.shape[1:]

    def qkvp_view(ref, h, s):
        return ref.at[:, pl.ds(pl.multiple_of(s * r, r), r), pl.ds(pl.multiple_of(h * w, w), w)]

    def block_view(rows):
        return lambda ref, h, s: ref.at[pl.ds(pl.multiple_of((h * count + s) * rows, rows), rows)]

    shards = [qkvp, sq, up, down, o, small]
    fulls = [qkvp_f, sq_f, up_f, down_f, o_f, small_f]
    views = [qkvp_view] + [block_view(s.shape[0]) for s in shards[1:]]
    gather = Gather(place, shards, fulls, views, (0, 1, 0, 1, 1, 0), local_sem, send_sem, recv_sem)
    for step in gather.steps():
        step()
    for slot in range(2 * count):
        for name, row, at, size, target in small_names:
            if size * 2 * count > vec.shape[1] * (4 if name == "ub" else 1) and slot >= count:
                continue
            ref = vec_up if name == "ub" else vec
            ref[target : target + 1, slot * size : (slot + 1) * size] = small_f[slot * 8 + row : slot * 8 + row + 1, at : at + size]


def small_layout(both, seq):
    names = []
    for i, name in enumerate(("cb", "pb", "sb")):
        names.append((name, 0, i * both, both, i))
    names.append(("ub", 1, 0, 4 * both, 0))
    for i, name in enumerate(("ob", "g1", "s1", "db", "g2", "s2")):
        names.append((name, 2 + i // 2, (i % 2) * seq, seq, 3 + i))
    return names


def gather_all(w):
    count = lax.axis_size("seq")
    both, seq = w["cb"].shape[0], w["ob"].shape[0]
    width = both * 2 * count
    layout = small_layout(both, seq)
    lines = [[] for _ in range(8)]
    for name, row, at, size, target in layout:
        lines[row].append(w[name].astype(F32))
    lines = [jnp.concatenate(parts) if parts else jnp.zeros((128,), F32) for parts in lines]
    small = jnp.stack([jnp.pad(line, (0, 128 - line.shape[0])) for line in lines])
    qkvp = jnp.stack([w["q"], w["k"], w["v"], w["p"]])
    shards = [qkvp, w["sq"], w["o"], w["up"], w["down"], small]
    any_spec = pl.BlockSpec(memory_space=pl.ANY)
    vmem_spec = pl.BlockSpec(memory_space=pltpu.VMEM)
    units = len(shards)
    outs = pl.pallas_call(
        functools.partial(gather_kernel, count, layout),
        in_specs=[any_spec] * 6,
        out_specs=[any_spec] * 5 + [vmem_spec] * 2,
        out_shape=[
            jax.ShapeDtypeStruct((4, qkvp.shape[1] * count, qkvp.shape[2] * 2), BF),
            *[jax.ShapeDtypeStruct((s.shape[0] * 2 * count, s.shape[1]), BF) for s in shards[1:5]],
            jax.ShapeDtypeStruct((16, width), F32),
            jax.ShapeDtypeStruct((1, 4 * width), F32),
        ],
        scratch_shapes=[
            pltpu.VMEM((8 * 2 * count, 128), F32),
            pltpu.SemaphoreType.DMA((units,)),
            pltpu.SemaphoreType.DMA((units, 14 * (count // 4))),
            pltpu.SemaphoreType.DMA((units, 2 * count)),
        ],
        compiler_params=pltpu.CompilerParams(collective_id=0, has_side_effects=True, vmem_limit_bytes=16 * MIB),
        name="gather_weights",
    )(*shards)
    full = dict(zip(("q", "k", "v", "p"), outs[0]))
    full.update(zip(("sq", "o", "up", "down"), outs[1:5]))
    for name, row, at, size, target in layout:
        full[name] = outs[6] if name == "ub" else outs[5][target : target + 1]
    return full


class Scatter:
    def __init__(self, place, view, order, mine, core, first, second, line, local_sem, send_sem, recv_sem):
        self.place, self.view, self.order = place, view, order
        self.mine, self.core, self.first, self.second, self.line = mine, core, first, second, line
        self.local_sem, self.send_sem, self.recv_sem = local_sem, send_sem, recv_sem
        self.f, self.g = (place.h, place.b) if order == 0 else (place.b, place.h)
        self.flips = (YFLIP, XFLIP) if order == 0 else (XFLIP, YFLIP)

    def index(self, f, g, a):
        return (f * 2 + g) * self.place.line_size + a

    def slot(self, f, g, a, c):
        h, b = (f, g) if self.order == 0 else (g, f)
        return h, self.place.seq_of(a, b, c)

    def remote(self, source, target, kind, send_at, recv_at):
        return pltpu.make_async_remote_copy(
            src_ref=source,
            dst_ref=target,
            send_sem=self.send_sem.at[send_at],
            recv_sem=self.recv_sem.at[recv_at],
            device_id=self.place.neighbour(kind),
            device_id_type=MESH,
        )

    def core_copy(self, f, g, a):
        i = self.index(f, g, a)
        return self.remote(self.core.at[i], self.core.at[i], CORE, i, i)

    def first_copy(self, g, a):
        n = self.place.line_size
        to = g * n + a
        return self.remote(self.mine.at[self.index(1 - self.f, g, a)], self.first.at[to], self.flips[0], 4 * n + to, 4 * n + to)

    def second_copy(self, a):
        n = self.place.line_size
        return self.remote(self.mine.at[self.index(self.f, 1 - self.g, a)], self.second.at[a], self.flips[1], 6 * n + a, 6 * n + a)

    def line_copy(self, kind, a):
        n = self.place.line_size
        way = 0 if kind == UP else 1
        at = (7 + way) * n + a
        return self.remote(self.mine.at[self.index(self.f, self.g, a)], self.line.at[way * n + a], kind, at, at)

    def start(self, f, g, a):
        p = self.place
        i = self.index(f, g, a)
        for source, target in self.view(*self.slot(f, g, a, 1 - p.c), self.core.at[i]):
            self.remote(source, target, CORE, i, i).start()
        for source, target in self.view(*self.slot(f, g, a, p.c), self.mine.at[i]):
            pltpu.make_async_copy(source, target, self.local_sem.at[i]).start()

    def arrive(self, f, g, a):
        i = self.index(f, g, a)
        pltpu.make_async_copy(self.mine.at[i], self.mine.at[i], self.local_sem.at[i]).wait()
        self.core_copy(f, g, a).wait_recv()

    def add(self, i, *refs):
        total = self.mine[i].astype(F32)
        for ref, at in refs:
            total = total + ref[at].astype(F32)
        self.mine[i] = total.astype(self.mine.dtype)

    def loop(self, count, run):
        def body(i, carry):
            run(i)
            return carry

        lax.fori_loop(0, count, body, 0)

    def begin(self):
        n = self.place.line_size
        self.loop(2 * n, lambda i: self.start(1 - self.f, i // n, i % n))
        self.loop(n, lambda i: self.start(self.f, 1 - self.g, i))
        self.loop(n, lambda i: self.start(self.f, self.g, i))

    def flip_first(self):
        n = self.place.line_size

        def run(i):
            g, a = i // n, i % n
            self.arrive(1 - self.f, g, a)
            at = self.index(1 - self.f, g, a)
            self.add(at, (self.core, at))
            self.first_copy(g, a).start()

        self.loop(2 * n, run)

    def flip_second(self):
        n = self.place.line_size

        def run(a):
            self.arrive(self.f, 1 - self.g, a)
            self.first_copy(1 - self.g, a).wait_recv()
            at = self.index(self.f, 1 - self.g, a)
            self.add(at, (self.core, at), (self.first, (1 - self.g) * n + a))
            self.second_copy(a).start()

        self.loop(n, run)

    def settle(self, a):
        n = self.place.line_size
        self.arrive(self.f, self.g, a)
        self.first_copy(self.g, a).wait_recv()
        self.second_copy(a).wait_recv()
        at = self.index(self.f, self.g, a)
        return at, [(self.core, at), (self.first, self.g * n + a), (self.second, a)]

    def along(self):
        p = self.place
        n = p.line_size
        for d in range(n - 1, 0, -1):
            for kind, way, a, inside, fed in (
                (UP, 0, p.a + d, p.a + d <= n - 1, p.a > 0),
                (DOWN, 1, p.a - d, p.a - d >= 0, p.a < n - 1),
            ):
                @pl.when(inside)
                def _(kind=kind, way=way, a=a, fed=fed):
                    at, refs = self.settle(a)

                    @pl.when(fed)
                    def _():
                        self.line_copy(kind, a).wait_recv()
                        self.add(at, *refs, (self.line, way * n + a))

                    @pl.when(jnp.logical_not(fed))
                    def _():
                        self.add(at, *refs)

                    self.line_copy(kind, a).start()

    def finish(self, store):
        p = self.place
        n = p.line_size
        at, refs = self.settle(p.a)
        self.add(at, *refs)
        for kind, way, fed in ((UP, 0, p.a > 0), (DOWN, 1, p.a < n - 1)):
            @pl.when(fed)
            def _(kind=kind, way=way):
                self.line_copy(kind, p.a).wait_recv()
                self.add(at, (self.line, way * n + p.a))
        store(self.mine[at].astype(F32))
        self.loop(4 * n, lambda i: self.core_copy(i // (2 * n), (i // n) % 2, i % n).wait_send())
        self.loop(2 * n, lambda i: self.first_copy(i // n, i % n).wait_send())
        self.loop(n, lambda a: self.second_copy(a).wait_send())

        def line_done(a):
            for kind, inside in ((UP, a > p.a), (DOWN, a < p.a)):
                @pl.when(inside)
                def _(kind=kind):
                    self.line_copy(kind, a).wait_send()

        self.loop(n, line_done)


def scatter_scratch(count, shape, dtype=BF):
    n = count // 4
    return [
        *[pltpu.VMEM((k * n, *shape), dtype) for k in (4, 4, 2, 1, 2)],
        pltpu.SemaphoreType.DMA((4 * n,)),
        pltpu.SemaphoreType.DMA((9 * n,)),
        pltpu.SemaphoreType.DMA((9 * n,)),
    ]


def block_pairs(ref, rows, count):
    def view(h, s, target):
        return [(ref.at[pl.ds(pl.multiple_of((h * count + s) * rows, rows), rows)], target)]

    return view


def square_pairs(refs, r, w):
    def view(h, s, target):
        here = (pl.ds(pl.multiple_of(s * r, r), r), pl.ds(pl.multiple_of(h * w, w), w))
        return [(ref.at[here], target.at[i]) for i, ref in enumerate(refs)]

    return view


def run_scatters(units, stores, between=lambda at: None):
    for unit in units:
        unit.begin()
    between(0)
    for unit in units:
        unit.flip_first()
    between(1)
    for unit in units:
        unit.flip_second()
    between(2)
    for unit in units:
        unit.along()
    between(3)
    for unit, store in zip(units, stores):
        unit.finish(store)
    between(4)


def scatter_dense_kernel(count, up, down, o, up_out, down_out, o_out, *scratch):
    place = Place(count)
    place.barrier()
    units, stores = [], []
    for i, (ref, out, order) in enumerate(((up, up_out, 0), (down, down_out, 1), (o, o_out, 1))):
        units.append(Scatter(place, block_pairs(ref, out.shape[0], count), order, *scratch[8 * i : 8 * i + 8]))

        def store(value, out=out):
            out[...] = value

        stores.append(store)
    run_scatters(units, stores)


def scatter_attention_kernel(
    count, q, k, v, p, sq, vec, q_out, k_out, v_out, p_out, sq_out, vec_out, ub_out, sums, parts, vec_send, vec_recv, *scratch
):
    place = Place(count)
    place.barrier()
    r, w = q_out.shape
    units = [
        Scatter(place, square_pairs((q, k, v, p), r, w), 0, *scratch[:8]),
        Scatter(place, block_pairs(sq, sq_out.shape[0], count), 1, *scratch[8:]),
    ]

    def store_square(value):
        for i, out in enumerate((q_out, k_out, v_out, p_out)):
            out[...] = value[i]

    def store_sq(value):
        sq_out[...] = value

    def vec_copy(kind):
        return pltpu.make_async_remote_copy(
            src_ref=sums.at[kind],
            dst_ref=parts.at[kind],
            send_sem=vec_send.at[kind],
            recv_sem=vec_recv.at[kind],
            device_id=place.neighbour(kind),
            device_id_type=MESH,
        )

    def between(at):
        kinds = (CORE, XFLIP, YFLIP)
        if at == 0:
            sums[CORE] = vec[...]
            vec_copy(CORE).start()
        elif at < 3:
            vec_copy(kinds[at - 1]).wait_recv()
            sums[kinds[at]] = sums[kinds[at - 1]] + parts[kinds[at - 1]]
            vec_copy(kinds[at]).start()
        elif at == 3:
            vec_copy(YFLIP).wait_recv()
            total = sums[YFLIP] + parts[YFLIP]
            ends = (place.a > 0, place.a < place.line_size - 1)
            sums[UP] = total
            sums[DOWN] = total
            for kind, fed in ((UP, ends[0]), (DOWN, ends[1])):
                @pl.when(fed)
                def _(kind=kind):
                    vec_copy(kind).wait_recv()
                    sums[kind] = sums[kind] + parts[kind]

                @place.when(kind)
                def _(kind=kind):
                    vec_copy(kind).start()
        else:
            total = sums[UP] + sums[DOWN] - (sums[YFLIP] + parts[YFLIP])
            width = total.shape[1]
            both = vec_out.shape[1]
            k = place.h * count + place.s
            mine = pltpu.roll(total, lax.rem(width - k * both, width), 1)
            vec_out[...] = mine[:, :both]
            wide = ub_out.shape[1]
            flat = k * wide
            lanes = lax.rem(flat, width)
            mine = pltpu.roll(total, lax.rem(width - lanes, width), 1)[:, :wide]
            row = lax.broadcasted_iota(jnp.int32, mine.shape, 0)
            ub_out[...] = jnp.sum(jnp.where(row == 12 + flat // width, mine, 0.0), axis=0, keepdims=True)
            for kind in range(5):
                @place.when(kind)
                def _(kind=kind):
                    vec_copy(kind).wait_send()

    run_scatters(units, (store_square, store_sq), between)


def scatter_dense(g):
    count = lax.axis_size("seq")
    names = ("up", "down", "o")
    shapes = [(g[n].shape[0] // (2 * count), g[n].shape[1]) for n in names]
    scratch = []
    for shape in shapes:
        scratch += scatter_scratch(count, shape)
    outs = pl.pallas_call(
        functools.partial(scatter_dense_kernel, count),
        in_specs=[pl.BlockSpec(memory_space=pl.ANY)] * 3,
        out_specs=[pl.BlockSpec(memory_space=pltpu.VMEM)] * 3,
        out_shape=[jax.ShapeDtypeStruct(shape, F32) for shape in shapes],
        scratch_shapes=scratch,
        compiler_params=pltpu.CompilerParams(collective_id=1, has_side_effects=True, vmem_limit_bytes=48 * MIB),
        name="scatter_dense",
    )(*[g[n] for n in names])
    return dict(zip(names, outs))


VECTORS = ("cb", "pb", "sb", "ob", "g1", "s1", "db", "g2", "s2")


def scatter_attention(g):
    count = lax.axis_size("seq")
    width = g["q"].shape[0]
    both = width // (2 * count)
    lines = [g[n].reshape(1, width) for n in VECTORS]
    vec = jnp.concatenate(lines + [jnp.zeros((12 - len(lines), width), F32), g["ub"].reshape(-1, width)], axis=0)
    square = (width // count, width // 2)
    narrow = (both, g["sq"].shape[1])
    vmem = pl.BlockSpec(memory_space=pltpu.VMEM)
    outs = pl.pallas_call(
        functools.partial(scatter_attention_kernel, count),
        in_specs=[pl.BlockSpec(memory_space=pl.ANY)] * 5 + [vmem],
        out_specs=[vmem] * 7,
        out_shape=[jax.ShapeDtypeStruct(square, F32)] * 4
        + [jax.ShapeDtypeStruct(s, F32) for s in (narrow, (16, both), (1, 4 * both))],
        scratch_shapes=[
            pltpu.VMEM((5, 16, width), F32),
            pltpu.VMEM((5, 16, width), F32),
            pltpu.SemaphoreType.DMA((5,)),
            pltpu.SemaphoreType.DMA((5,)),
            *scatter_scratch(count, (4, *square)),
            *scatter_scratch(count, narrow),
        ],
        compiler_params=pltpu.CompilerParams(collective_id=2, has_side_effects=True, vmem_limit_bytes=48 * MIB),
        name="scatter_attention",
    )(g["q"], g["k"], g["v"], g["p"], g["sq"], vec)
    final = dict(zip(("q", "k", "v", "p", "sq"), outs[:5]))
    final.update({n: outs[5][i] for i, n in enumerate(VECTORS)})
    final["ub"] = outs[6].reshape(4 * both)
    return final


def normalize(values):
    centre = values - jnp.mean(values, axis=-1, keepdims=True)
    spread = jnp.mean(centre * centre, axis=-1, keepdims=True)
    scale = lax.rsqrt(spread + epsilon)
    return centre * scale, scale


def normalize_back(grad, gain, unit, scale):
    pulled = grad * gain
    return scale * (
        pulled
        - jnp.mean(pulled, axis=-1, keepdims=True)
        - unit * jnp.mean(pulled * unit, axis=-1, keepdims=True)
    )


def gelu_parts(u):
    root = np.float32(np.sqrt(2.0 / np.pi))
    inner = root * (u + 0.044715 * u * u * u)
    tanh = jnp.tanh(inner)
    value = 0.5 * u * (1.0 + tanh)
    slope = 0.5 * (1.0 + tanh) + 0.5 * u * (1.0 - tanh * tanh) * root * (1.0 + 3 * 0.044715 * u * u)
    return value, slope


def exchange_rows(array, head):
    half = array.shape[0] // 2
    mine = lax.dynamic_slice_in_dim(array, head * half, half, 0)
    theirs = lax.dynamic_slice_in_dim(array, (1 - head) * half, half, 0)
    other = lax.ppermute(theirs, "head", [(0, 1), (1, 0)])
    first = jnp.where(head == 0, mine, other)
    second = jnp.where(head == 0, other, mine)
    return jnp.stack([first, second])[:, None]


def body(
    inputs, lengths,
    query_weight, key_weight, value_weight, position_weight, content_bias, position_bias,
    output_weight, output_bias, first_gain, first_shift, up_weight, up_bias, down_weight, down_bias,
    second_gain, second_shift, squeeze_weight, squeeze_bias, cotangent,
):
    seq = lax.axis_index("seq")
    head = lax.axis_index("head")
    rows, width = inputs.shape[2:]

    x = lax.dynamic_index_in_dim(inputs[:, 0], head, 0, keepdims=False)
    book_lengths = lax.dynamic_index_in_dim(lengths, head, 0, keepdims=False)
    padded_lengths = jnp.concatenate([jnp.zeros((4,), jnp.int32), book_lengths])
    window = lax.dynamic_slice_in_dim(padded_lengths, seq, 5, 0)
    own_length = window[4]

    memory = shifted(x, "seq", 1)
    w = gather_all(
        dict(
            q=query_weight, k=key_weight, v=value_weight, p=position_weight,
            o=output_weight, up=up_weight.T, down=down_weight, sq=squeeze_weight.T,
            cb=content_bias, pb=position_bias, ob=output_bias, g1=first_gain, s1=first_shift, ub=up_bias,
            db=down_bias, g2=second_gain, s2=second_shift, sb=squeeze_bias,
        )
    )
    cb, pb, ob, g1, s1, ub, db, g2, s2, sb = (
        w[n] for n in ("cb", "pb", "ob", "g1", "s1", "ub", "db", "g2", "s2", "sb")
    )

    pad, taps, collect, biased = squeeze_layout(rows)
    row_ids = jnp.arange(rows)
    kept = (row_ids < own_length)[:, None]
    masked = jnp.where(kept, x, jnp.zeros_like(x))
    made = biased * sb
    for tap in range(3):
        made = made + mm_nt(mm_tn(taps[tap], masked, BF), w["sq"][:, tap * width : (tap + 1) * width])
    made = made.astype(BF)
    arrived = jnp.concatenate(
        [shifted(made[role * pad : (role + 1) * pad], "seq", 4 - role) for role in range(3)], axis=0
    )
    squeezed = mm(collect, arrived, out=BF)
    keys_in = jnp.concatenate([squeezed, memory, x], axis=0)

    flat = np.arange(0, 3 * rows, 3)
    history_ok = jnp.asarray(flat % rows) < window[:3][flat // rows]
    valid = jnp.concatenate([history_ok, row_ids < window[3], row_ids < window[4]])
    key_bias = jnp.where(valid, 0.0, -1e30).astype(F32)[None]

    query = mm(x, w["q"])
    keys = mm(keys_in, w["k"], out=BF)
    values = mm(keys_in, w["v"], out=BF)
    table = jnp.asarray(table_rows(width, 3 * rows))
    places = mm(table, w["p"], out=BF)
    attended, probs = attend_forward(key_bias, cb, pb, query, keys, values, places)

    blended = x.astype(F32) + mm(attended, w["o"]) + ob
    unit1, scale1 = normalize(blended)
    normed = (unit1 * g1 + s1).astype(BF)
    u = mm_nt(normed, w["up"]) + ub
    hidden_f, slope = gelu_parts(u)
    hidden = hidden_f.astype(BF)
    unit2, scale2 = normalize(normed.astype(F32) + mm(hidden, w["down"]) + db)
    outputs = (unit2 * g2 + s2).astype(BF)

    grads = {}
    ct = lax.dynamic_index_in_dim(cotangent[:, 0], head, 0, keepdims=False).astype(F32)
    grads["g2"] = jnp.sum(ct * unit2, axis=0)
    grads["s2"] = jnp.sum(ct, axis=0)
    dy = normalize_back(ct, g2, unit2, scale2)
    grads["db"] = jnp.sum(dy, axis=0)
    dy_b = dy.astype(BF)
    grads["down"] = mm_tn(hidden, dy_b, BF)
    du = (mm_nt(dy_b, w["down"]) * slope).astype(BF)
    grads["ub"] = jnp.sum(du.astype(F32), axis=0)
    grads["up"] = mm_tn(du, normed, BF)
    dnormed = dy + mm(du, w["up"])
    grads["g1"] = jnp.sum(dnormed * unit1, axis=0)
    grads["s1"] = jnp.sum(dnormed, axis=0)
    dblended = normalize_back(dnormed, g1, unit1, scale1)
    grads["ob"] = jnp.sum(dblended, axis=0)
    dblended_b = dblended.astype(BF)
    grads["o"] = mm_tn(attended, dblended_b, BF)
    dattended = mm_nt(dblended_b, w["o"], BF)

    dq, dcb, dpb, dk, dv, dplaces = attend_backward(cb, pb, query, keys, values, places, probs, dattended)
    grads["cb"] = dcb[0]
    grads["pb"] = dpb[0]
    dkeys_in = mm_nt(dk, w["k"]) + mm_nt(dv, w["v"])
    dsqueezed = dkeys_in[:rows].astype(BF)
    grads["sb"] = jnp.sum(dsqueezed.astype(F32), axis=0)
    dmade = mm_tn(collect, dsqueezed, BF)
    returned = jnp.concatenate(
        [shifted(dmade[role * pad : (role + 1) * pad], "seq", role - 4) for role in range(3)], axis=0
    )
    from_next = shifted(dkeys_in[rows : 2 * rows].astype(BF), "seq", -1)
    grads["q"] = mm_tn(x, dq, BF)
    grads["k"] = mm_tn(keys_in, dk, BF)
    grads["v"] = mm_tn(keys_in, dv, BF)
    grads["p"] = mm_tn(table, dplaces, BF)
    dx = dblended + mm_nt(dq, w["q"]) + dkeys_in[2 * rows :] + from_next.astype(F32)
    dmasked = jnp.zeros((rows, width), F32)
    sq_grads = []
    for tap in range(3):
        spread = mm(taps[tap], returned, out=BF)
        dmasked = dmasked + mm(spread, w["sq"][:, tap * width : (tap + 1) * width])
        sq_grads.append(mm_tn(spread, masked, BF))
    grads["sq"] = jnp.concatenate(sq_grads, axis=1)
    dx = dx + jnp.where(kept, dmasked, 0.0)

    final = {**scatter_dense(grads), **scatter_attention(grads)}
    return (
        exchange_rows(outputs, head),
        exchange_rows(dx.astype(BF), head),
        final["q"], final["k"], final["v"], final["p"], final["cb"], final["pb"],
        final["o"], final["ob"], final["g1"], final["s1"], final["up"].T, final["ub"],
        final["down"], final["db"], final["g2"], final["s2"], final["sq"].T, final["sb"],
    )


def solution(mesh):
    both = ("head", "seq")
    matrix = P("seq", "head")
    in_specs = (
        P(None, "seq", None, None), P(), matrix, matrix, matrix, matrix, P(both), P(both),
        P(both, None), P("seq"), P("seq"), P("seq"), P(None, both), P(both), P(both, None), P("seq"),
        P("seq"), P("seq"), P(None, both), P(both), P(None, "seq", None, None),
    )
    rows = P(None, "seq", "head", None)
    out_specs = (
        rows, rows, matrix, matrix, matrix, matrix, P(both), P(both),
        P(both, None), P(both), P(both), P(both), P(None, both), P(both), P(both, None), P(both),
        P(both), P(both), P(None, both), P(both),
    )
    return jax.shard_map(body, mesh=mesh, in_specs=in_specs, out_specs=out_specs, check_vma=False)
```

```python
import functools

import jax
import jax.numpy as jnp
import numpy as np
from jax import lax
from jax.experimental import pallas as pl
from jax.experimental.pallas import tpu as pltpu
from jax.sharding import PartitionSpec as P

HD = 128
BF = jnp.bfloat16
F32 = jnp.float32
epsilon = 1e-05
MIB = 1024 * 1024


def mm(left, right, contract=((1,), (0,)), out=F32):
    return lax.dot_general(left, right, (contract, ((), ())), preferred_element_type=F32).astype(out)


def mm_nt(left, right, out=F32):
    return mm(left, right, ((1,), (1,)), out)


def mm_tn(left, right, out=F32):
    return mm(left, right, ((0,), (0,)), out)


def shifted(array, axis, by):
    count = lax.axis_size(axis)
    pairs = [(i, i + by) for i in range(count) if 0 <= i + by < count]
    return lax.ppermute(array, axis, pairs)


def table_rows(width, count):
    distance = np.arange(count - 1, -1, -1).astype(np.float32)[:, None]
    exponent = -np.arange(0, width, 2).astype(np.float32) / np.float32(width)
    frequency = np.power(np.float32(10000.0), exponent).astype(np.float32)
    angles = (distance * frequency[None, :]).astype(np.float32)
    return np.concatenate([np.sin(angles), np.cos(angles)], axis=1).astype(BF)


def squeeze_layout(rows):
    pad = -(-(rows // 3 + 2) // 16) * 16
    taps = np.zeros((3, rows, 3 * pad), np.float32)
    collect = np.zeros((rows, 3 * pad), np.float32)
    biased = np.zeros((3 * pad, 1), np.float32)
    for role in range(3):
        first = role * rows // 3
        for i in range(rows):
            flat = role * rows + i
            taps[flat % 3, i, role * pad + flat // 3 - first] = 1.0
            collect[flat // 3, role * pad + flat // 3 - first] = 1.0
        for c in range(first, ((role + 1) * rows - 1) // 3 + 1):
            if role == 0 or 3 * c >= role * rows:
                biased[role * pad + c - first] = 1.0
    return pad, taps.astype(BF), collect.astype(BF), biased


def attend_forward_kernel(bias_ref, cb_ref, pb_ref, q_ref, k_ref, v_ref, pl_ref, out_ref, p_ref, s_scr, x_scr):
    rows = q_ref.shape[0]
    keys = k_ref.shape[0]
    scale = HD ** (-0.5)
    q = q_ref[...]
    content_query = ((q + cb_ref[...]) * scale).astype(BF)
    place_query = ((q + pb_ref[...]) * scale).astype(BF)
    s_scr[...] = mm_nt(content_query, k_ref[...])
    x_scr[...] = mm_nt(place_query, pl_ref[...])
    step = 32
    bias = bias_ref[...]
    for start in range(0, rows, step):
        here = slice(start, start + step)
        located = pltpu.roll(
            x_scr[here], (start + keys - rows + 1) % keys, 1, stride=1, stride_axis=0
        )
        scores = s_scr[here] + located + bias
        row = start + lax.broadcasted_iota(jnp.int32, scores.shape, 0)
        col = lax.broadcasted_iota(jnp.int32, scores.shape, 1)
        scores = jnp.where(col <= 2 * rows + row, scores, -1e30)
        top = jnp.max(scores, axis=1, keepdims=True)
        weights = jnp.exp(scores - top)
        total = jnp.sum(weights, axis=1, keepdims=True)
        p_ref[0, here] = (weights * (1.0 / total)).astype(BF)
    out_ref[...] = mm(p_ref[0], v_ref[...]).astype(BF)


def attend_backward_kernel(
    cb_ref, pb_ref, q_ref, k_ref, v_ref, pl_ref, p_ref, do_ref,
    dq_ref, dcb_ref, dpb_ref, dk_ref, dv_ref, dpl_ref,
    dp_scr, ds_scr, dx_scr,
):
    rows = q_ref.shape[0]
    keys = k_ref.shape[0]
    scale = HD ** (-0.5)
    q = q_ref[...]
    content_query = ((q + cb_ref[...]) * scale).astype(BF)
    place_query = ((q + pb_ref[...]) * scale).astype(BF)
    block = 128
    flip = (
        lax.broadcasted_iota(jnp.int32, (block, block), 0)
        + lax.broadcasted_iota(jnp.int32, (block, block), 1)
        == block - 1
    ).astype(BF)
    dp_scr[...] = mm_nt(do_ref[...], v_ref[...])
    step = 32
    for start in range(0, rows, step):
        here = slice(start, start + step)
        prob = p_ref[0, here].astype(F32)
        dprob = dp_scr[here]
        delta = jnp.sum(prob * dprob, axis=1, keepdims=True)
        ds_scr[here] = (prob * (dprob - delta)).astype(BF)
    dv_ref[...] = mm_tn(do_ref[...], p_ref[0]).T.astype(BF)
    dk_ref[...] = mm_tn(content_query, ds_scr[...]).T.astype(BF)
    dcq = mm(ds_scr[...], k_ref[...]) * scale
    flipped = []
    for start in range(0, rows, block):
        here = slice(start, start + block)
        dp_scr[here] = mm(flip, ds_scr[here])
        flipped.append(mm(flip, place_query[here]).astype(BF))
        dx_scr[here] = pltpu.roll(
            dp_scr[here], rows - block - start, 1, stride=1, stride_axis=0
        ).astype(BF)
    dpl_ref[...] = mm_tn(jnp.concatenate(flipped, axis=0), dx_scr[...]).T.astype(BF)
    dpq_flipped = mm(dx_scr[...], pl_ref[...]) * scale
    dpq = []
    for start in range(0, rows, block):
        piece = dpq_flipped[start : start + block]
        high = piece.astype(BF)
        dpq.append(mm(flip, high) + mm(flip, (piece - high.astype(F32)).astype(BF)))
    dpq = jnp.concatenate(dpq, axis=0)
    dq_ref[...] = (dcq + dpq).astype(BF)
    dcb_ref[...] = jnp.sum(dcq, axis=0, keepdims=True)
    dpb_ref[...] = jnp.sum(dpq, axis=0, keepdims=True)


def attend_forward(key_bias, content_bias, position_bias, query, keys, values, places):
    rows, width = query.shape
    count = keys.shape[0]
    heads = width // HD
    row_spec = pl.BlockSpec((rows, HD), lambda h: (0, h))
    key_spec = pl.BlockSpec((count, HD), lambda h: (0, h))
    vec_spec = pl.BlockSpec((1, HD), lambda h: (0, h))
    return pl.pallas_call(
        attend_forward_kernel,
        grid=(heads,),
        in_specs=[pl.BlockSpec((1, count), lambda h: (0, 0)), vec_spec, vec_spec, row_spec, key_spec, key_spec, key_spec],
        out_specs=[row_spec, pl.BlockSpec((1, rows, count), lambda h: (h, 0, 0))],
        out_shape=[
            jax.ShapeDtypeStruct((rows, width), BF),
            jax.ShapeDtypeStruct((heads, rows, count), BF),
        ],
        scratch_shapes=[pltpu.VMEM((rows, count), F32), pltpu.VMEM((rows, count), F32)],
        compiler_params=pltpu.CompilerParams(vmem_limit_bytes=48 * MIB),
        cost_estimate=pl.CostEstimate(
            flops=6 * rows * count * width, bytes_accessed=2 * heads * rows * count, transcendentals=heads * rows * count
        ),
        name="attend_forward",
    )(key_bias, content_bias, position_bias, query, keys, values, places)


def attend_backward(content_bias, position_bias, query, keys, values, places, probs, d_out):
    rows, width = query.shape
    count = keys.shape[0]
    heads = width // HD
    row_spec = pl.BlockSpec((rows, HD), lambda h: (0, h))
    key_spec = pl.BlockSpec((count, HD), lambda h: (0, h))
    vec_spec = pl.BlockSpec((1, HD), lambda h: (0, h))
    p_spec = pl.BlockSpec((1, rows, count), lambda h: (h, 0, 0))
    return pl.pallas_call(
        attend_backward_kernel,
        grid=(heads,),
        in_specs=[vec_spec, vec_spec, row_spec, key_spec, key_spec, key_spec, p_spec, row_spec],
        out_specs=[row_spec, vec_spec, vec_spec, key_spec, key_spec, key_spec],
        out_shape=[
            jax.ShapeDtypeStruct((rows, width), BF),
            jax.ShapeDtypeStruct((1, width), F32),
            jax.ShapeDtypeStruct((1, width), F32),
            jax.ShapeDtypeStruct((count, width), BF),
            jax.ShapeDtypeStruct((count, width), BF),
            jax.ShapeDtypeStruct((count, width), BF),
        ],
        scratch_shapes=[
            pltpu.VMEM((rows, count), F32),
            pltpu.VMEM((rows, count), BF),
            pltpu.VMEM((rows, count), BF),
        ],
        compiler_params=pltpu.CompilerParams(vmem_limit_bytes=48 * MIB),
        cost_estimate=pl.CostEstimate(
            flops=12 * rows * count * width, bytes_accessed=2 * heads * rows * count, transcendentals=0
        ),
        name="attend_backward",
    )(content_bias, position_bias, query, keys, values, places, probs, d_out)


MESH = pl.DeviceIdType.MESH
CORE, XFLIP, YFLIP, UP, DOWN = range(5)


def repeat(count, run):
    def body(i, carry):
        run(i)
        return carry

    lax.fori_loop(0, count, body, 0)


class Place:
    def __init__(self, count):
        self.count = count
        self.n = count // 4
        self.h = lax.axis_index("head")
        self.s = lax.axis_index("seq")
        self.a = self.s // 4
        self.b = (self.s // 2) % 2
        self.c = self.s % 2

    def seq_of(self, a, b, c):
        return a * 4 + b * 2 + c

    def neighbour(self, kind):
        s, h = self.s, self.h
        if kind == CORE:
            return (h, s + 1 - 2 * self.c)
        if kind == XFLIP:
            return (h, s + 2 - 4 * self.b)
        if kind == YFLIP:
            return (1 - h, s)
        return (h, s + 4) if kind == UP else (h, s - 4)

    def when(self, kind):
        if kind == UP:
            return pl.when(self.a < self.n - 1)
        if kind == DOWN:
            return pl.when(self.a > 0)
        return lambda run: run()

    def barrier(self):
        barrier = pltpu.get_barrier_semaphore()
        for kind in range(5):
            @self.when(kind)
            def _(kind=kind):
                pl.semaphore_signal(barrier, inc=1, device_id=self.neighbour(kind), device_id_type=MESH)
        ends = jnp.where(self.a == 0, 1, 0) + jnp.where(self.a == self.n - 1, 1, 0)
        pl.semaphore_wait(barrier, 5 - ends)

    def along(self, i):
        return (self.a + self.n // 2 + i) % self.n


class Gather:
    def __init__(self, place, units, local_sem, send_sem, recv_sem):
        self.place, self.units = place, units
        self.local_sem, self.send_sem, self.recv_sem = local_sem, send_sem, recv_sem

    def view(self, u, h, s):
        shard, full, view, order = self.units[u]
        return view(full, h, s)

    def copy(self, u, kind, h, s, own=False):
        n = self.place.n
        a, b = s // 4, (s // 2) % 2
        order = self.units[u][3]
        other = b if order.index("x") < order.index("z") else h
        sent = {
            UP: other * n + a,
            DOWN: (2 + other) * n + a,
            XFLIP: (4 + h) * n + a,
            YFLIP: (6 + b) * n + a,
            CORE: (8 + h * 2 + b) * n + a,
        }[kind]
        there = self.view(u, h, s)
        return pltpu.make_async_remote_copy(
            src_ref=self.units[u][0] if own else there,
            dst_ref=there,
            send_sem=self.send_sem.at[u, sent],
            recv_sem=self.recv_sem.at[u, h * self.place.count + s],
            device_id=self.place.neighbour(kind),
            device_id_type=MESH,
        )

    def local(self, u):
        return pltpu.make_async_copy(self.units[u][0], self.view(u, self.place.h, self.place.s), self.local_sem.at[u])

    def sources(self):
        found = []
        for t in range(self.place.n):
            for sign in ((1, -1) if t else (0,)):
                for x in (0, 1):
                    for y in (0, 1):
                        if t or x or y:
                            found.append((t, sign, x, y))
        return sorted(found, key=lambda e: e[0] + e[2] + e[3])

    def onward(self, u, sign, x, y):
        order = self.units[u][3]
        moved = {"x": x, "y": y, "z": sign}
        last = max([i for i in range(3) if moved[order[i]]], default=-1)
        kinds = []
        if last >= 0 and order[last] == "z":
            kinds.append(UP if sign > 0 else DOWN)
        for dim in order[last + 1 :]:
            kinds += {"x": [XFLIP], "y": [YFLIP], "z": [UP, DOWN]}[dim]
        return kinds + [CORE]

    def send(self, u, kind, h, s, own, wait):
        @self.place.when(kind)
        def _():
            copy = self.copy(u, kind, h, s, own)
            if wait:
                copy.wait_send()
            else:
                copy.start()

    def begin(self, wait=False):
        p = self.place
        for u in range(len(self.units)):
            for kind in self.onward(u, 0, 0, 0):
                self.send(u, kind, p.h, p.s, True, wait)
        for u in range(len(self.units)):
            if wait:
                self.local(u).wait()
            else:
                self.local(u).start()

    def pass_on(self, entry, wait=False):
        p = self.place
        t, sign, x, y = entry
        a = p.a - sign * t
        h = 1 - p.h if y else p.h
        s = p.seq_of(a, 1 - p.b if x else p.b, p.c)

        def run():
            for u in range(len(self.units)):
                if not wait:
                    self.copy(u, CORE, h, s).wait_recv()
                for kind in self.onward(u, sign, x, y):
                    self.send(u, kind, h, s, False, wait)

        if t:
            pl.when(jnp.logical_and(a >= 0, a <= p.n - 1))(run)
        else:
            run()

    def finish(self):
        p = self.place

        def core(i):
            h, a, b = i // (2 * p.n), i // 2 % p.n, i % 2
            for u in range(len(self.units)):
                self.copy(u, CORE, h, p.seq_of(a, b, 1 - p.c)).wait_recv()

        repeat(4 * p.n, core)
        self.begin(True)
        for entry in self.sources():
            self.pass_on(entry, True)

    def steps(self):
        return [self.begin] + [functools.partial(self.pass_on, entry) for entry in self.sources()] + [self.finish]


GATHER_ORDERS = ("yzx", "xzy", "zxy", "zyx")


def halves(rows):
    return [(0, rows // 2), (rows // 2, rows // 2)] if rows % 32 == 0 else [(0, rows)]


def block_units(shard, full, count, first):
    rows = shard.shape[0]
    units = []
    for i, (at, size) in enumerate(halves(rows)):
        def view(ref, h, s, at=at, size=size):
            return ref.at[pl.ds(pl.multiple_of((h * count + s) * rows + at, size), size)]

        units.append((shard.at[pl.ds(at, size)], full, view, GATHER_ORDERS[(first + i) % 4]))
    return units


def square_unit(shard, full, order):
    r, w = shard.shape

    def view(ref, h, s):
        return ref.at[pl.ds(pl.multiple_of(s * r, r), r), pl.ds(pl.multiple_of(h * w, w), w)]

    return (shard, full, view, order)


def gather_attention_kernel(count, small_names, *refs):
    shards, (vec, vec_up) = refs[:6], refs[11:13]
    fulls = refs[6:11] + refs[13:14]
    place = Place(count)
    place.barrier()
    units = [square_unit(shards[i], fulls[i], GATHER_ORDERS[i]) for i in range(4)]
    units += block_units(shards[4], fulls[4], count, 0)
    small, small_f = shards[5], fulls[5]

    def small_view(ref, h, s):
        return ref.at[pl.ds(pl.multiple_of((h * count + s) * 8, 8), 8)]

    units.append((small, small_f, small_view, "zxy"))
    gather = Gather(place, units, *refs[14:])
    for step in gather.steps():
        step()
    for slot in range(2 * count):
        for name, row, at, size, target in small_names:
            if size * 2 * count > vec.shape[1] * (4 if name == "ub" else 1) and slot >= count:
                continue
            ref = vec_up if name == "ub" else vec
            ref[target : target + 1, slot * size : (slot + 1) * size] = small_f[slot * 8 + row : slot * 8 + row + 1, at : at + size]


def gather_dense_kernel(count, *refs):
    place = Place(count)
    place.barrier()
    units = []
    for i in range(3):
        units += block_units(refs[i], refs[3 + i], count, (0, 2, 1)[i])
    gather = Gather(place, units, *refs[6:])
    for step in gather.steps():
        step()


def gather_semaphores(count, units):
    return [
        pltpu.SemaphoreType.DMA((units,)),
        pltpu.SemaphoreType.DMA((units, 12 * (count // 4))),
        pltpu.SemaphoreType.DMA((units, 2 * count)),
    ]


def small_layout(both, seq):
    names = []
    for i, name in enumerate(("cb", "pb", "sb")):
        names.append((name, 0, i * both, both, i))
    names.append(("ub", 1, 0, 4 * both, 0))
    for i, name in enumerate(("ob", "g1", "s1", "db", "g2", "s2")):
        names.append((name, 2 + i // 2, (i % 2) * seq, seq, 3 + i))
    return names


def gather_attention(w):
    count = lax.axis_size("seq")
    both, seq = w["cb"].shape[0], w["ob"].shape[0]
    width = both * 2 * count
    layout = small_layout(both, seq)
    lines = [[] for _ in range(8)]
    for name, row, at, size, target in layout:
        lines[row].append(w[name].astype(F32))
    lines = [jnp.concatenate(parts) if parts else jnp.zeros((128,), F32) for parts in lines]
    small = jnp.stack([jnp.pad(line, (0, 128 - line.shape[0])) for line in lines])
    names = ("q", "k", "v", "p", "sq")
    any_spec = pl.BlockSpec(memory_space=pl.ANY)
    vmem_spec = pl.BlockSpec(memory_space=pltpu.VMEM)
    outs = pl.pallas_call(
        functools.partial(gather_attention_kernel, count, layout),
        in_specs=[any_spec] * 6,
        out_specs=[any_spec] * 5 + [vmem_spec] * 2,
        out_shape=[
            *[jax.ShapeDtypeStruct((width, width), BF) for _ in range(4)],
            jax.ShapeDtypeStruct((width, w["sq"].shape[1]), BF),
            jax.ShapeDtypeStruct((16, width), F32),
            jax.ShapeDtypeStruct((1, 4 * width), F32),
        ],
        scratch_shapes=[
            pltpu.VMEM((8 * 2 * count, 128), F32),
            *gather_semaphores(count, 5 + len(halves(w["sq"].shape[0]))),
        ],
        compiler_params=pltpu.CompilerParams(collective_id=0, has_side_effects=True, vmem_limit_bytes=16 * MIB),
        name="gather_attention",
    )(*[w[n] for n in names], small)
    full = dict(zip(names, outs))
    for name, row, at, size, target in layout:
        full[name] = outs[6] if name == "ub" else outs[5][target : target + 1]
    return full


def gather_dense(w):
    count = lax.axis_size("seq")
    names = ("up", "down", "o")
    any_spec = pl.BlockSpec(memory_space=pl.ANY)
    outs = pl.pallas_call(
        functools.partial(gather_dense_kernel, count),
        in_specs=[any_spec] * 3,
        out_specs=[any_spec] * 3,
        out_shape=[jax.ShapeDtypeStruct((w[n].shape[0] * 2 * count, w[n].shape[1]), BF) for n in names],
        scratch_shapes=gather_semaphores(count, sum(len(halves(w[n].shape[0])) for n in names)),
        compiler_params=pltpu.CompilerParams(collective_id=3, has_side_effects=True, vmem_limit_bytes=16 * MIB),
        name="gather_dense",
    )(*[w[n] for n in names])
    return dict(zip(names, outs))


class Scatter:
    def __init__(self, place, view, order, mine, core, first, second, line, local_sem, send_sem, recv_sem):
        self.place, self.view = place, view
        self.by_y = order[0] == "y"
        self.late = order[2] == "z"
        self.mine, self.core, self.first, self.second, self.line = mine, core, first, second, line
        self.local_sem, self.send_sem, self.recv_sem = local_sem, send_sem, recv_sem
        self.f, self.g = (place.h, place.b) if self.by_y else (place.b, place.h)
        self.flips = (YFLIP, XFLIP) if self.by_y else (XFLIP, YFLIP)

    def index(self, f, g, a):
        return (f * 2 + g) * self.place.n + a

    def slot(self, f, g, a, c):
        h, b = (f, g) if self.by_y else (g, f)
        return h, self.place.seq_of(a, b, c)

    def remote(self, source, target, kind, send_at, recv_at):
        return pltpu.make_async_remote_copy(
            src_ref=source,
            dst_ref=target,
            send_sem=self.send_sem.at[send_at],
            recv_sem=self.recv_sem.at[recv_at],
            device_id=self.place.neighbour(kind),
            device_id_type=MESH,
        )

    def core_copy(self, i):
        return self.remote(self.core.at[i], self.core.at[i], CORE, i, i)

    def first_copy(self, g, a):
        n = self.place.n
        to = g * n + a
        return self.remote(self.mine.at[self.index(1 - self.f, g, a)], self.first.at[to], self.flips[0], 4 * n + to, 4 * n + to)

    def second_copy(self, a):
        n = self.place.n
        to = a if self.late else 0
        return self.remote(self.mine.at[self.index(self.f, 1 - self.g, a)], self.second.at[to], self.flips[1], 6 * n + to, 6 * n + to)

    def line_at(self, g, at):
        return at if self.late else g * (self.place.n + 1) + at

    def line_copy(self, kind, g, a):
        n = self.place.n
        to = self.line_at(g, a if kind == UP else jnp.where(a == self.place.a - 1, n, a))
        sent = 7 * n + (a if self.late else g * n + a)
        return self.remote(self.mine.at[self.index(self.f, g, a)], self.line.at[to], kind, sent, 7 * n + to)

    def line_wait(self, at):
        n = self.place.n
        self.remote(self.line.at[at], self.line.at[at], CORE, 7 * n, 7 * n + at).wait_recv()

    def start(self, f, g, a):
        p = self.place
        i = self.index(f, g, a)
        for source, target in self.view(*self.slot(f, g, a, 1 - p.c), self.core.at[i]):
            self.remote(source, target, CORE, i, i).start()
        for source, target in self.view(*self.slot(f, g, a, p.c), self.mine.at[i]):
            pltpu.make_async_copy(source, target, self.local_sem.at[i]).start()

    def gather(self, f, g, a, more=()):
        i = self.index(f, g, a)
        pltpu.make_async_copy(self.mine.at[i], self.mine.at[i], self.local_sem.at[i]).wait()
        self.core_copy(i).wait_recv()
        return i, [(self.core, i), *more]

    def after_first(self, g, a):
        self.first_copy(g, a).wait_recv()
        return self.gather(self.f, g, a, [(self.first, g * self.place.n + a)])

    def add(self, i, refs):
        total = self.mine[i].astype(F32)
        for ref, at in refs:
            total = total + ref[at].astype(F32)
        self.mine[i] = total.astype(self.mine.dtype)

    def add_line(self, i, g):
        p = self.place
        for fed, at in ((p.a > 0, p.a), (p.a < p.n - 1, p.n)):
            @pl.when(fed)
            def _(at=self.line_at(g, at)):
                self.line_wait(at)
                self.add(i, [(self.line, at)])

    def flip_first(self, g, a):
        self.add(*self.gather(1 - self.f, g, a))
        self.first_copy(g, a).start()

    def flip_second(self, a):
        i, refs = self.after_first(1 - self.g, a)
        self.add(i, refs)
        if not self.late:
            self.add_line(i, 1 - self.g)
        self.second_copy(a).start()

    def move(self, g, d):
        p = self.place
        for kind, a, inside, fed in (
            (UP, p.a + d, p.a + d <= p.n - 1, p.a > 0),
            (DOWN, p.a - d, p.a - d >= 0, p.a < p.n - 1),
        ):
            @pl.when(inside)
            def _(kind=kind, a=a, fed=fed):
                i, refs = self.after_first(g, a)
                if self.late:
                    self.second_copy(a).wait_recv()
                    refs.append((self.second, a))
                self.add(i, refs)

                @pl.when(fed)
                def _():
                    at = self.line_at(g, a)
                    self.line_wait(at)
                    self.add(i, [(self.line, at)])

                self.line_copy(kind, g, a).start()

    def finish(self, store):
        p = self.place
        n = p.n
        i, refs = self.after_first(self.g, p.a)
        to = p.a if self.late else 0
        self.second_copy(p.a).wait_recv()
        self.add(i, refs + [(self.second, to)])
        self.add_line(i, self.g)
        store(self.mine[i].astype(F32))
        repeat(4 * n, lambda i: self.core_copy(i).wait_send())
        repeat(2 * n, lambda i: self.first_copy(i // n, i % n).wait_send())
        if self.late:
            repeat(n, lambda a: self.second_copy(a).wait_send())
        else:
            self.second_copy(p.a).wait_send()

        def line_done(a):
            for kind, inside in ((UP, a > p.a), (DOWN, a < p.a)):
                @pl.when(inside)
                def _(kind=kind):
                    for g in (self.g,) if self.late else (0, 1):
                        self.line_copy(kind, g, a).wait_send()

        repeat(n, line_done)


def scatter_scratch(count, shape, order):
    n = count // 4
    late = order[2] == "z"
    lines = n + 1 if late else 2 * n + 2
    return [
        *[pltpu.VMEM((k, *shape), BF) for k in (4 * n, 4 * n, 2 * n, n if late else 1, lines)],
        pltpu.SemaphoreType.DMA((4 * n,)),
        pltpu.SemaphoreType.DMA((9 * n,)),
        pltpu.SemaphoreType.DMA((7 * n + lines,)),
    ]


SCATTER_ORDERS = ("yzx", "xzy", "yxz", "xyz")


def block_scatters(rows, first):
    return [(at, size, SCATTER_ORDERS[(first + i) % 4]) for i, (at, size) in enumerate(halves(rows))]


def block_pairs(ref, rows, at, size, count):
    def view(h, s, target):
        return [(ref.at[pl.ds(pl.multiple_of((h * count + s) * rows + at, size), size)], target)]

    return view


def square_pairs(ref, r, w):
    def view(h, s, target):
        return [(ref.at[pl.ds(pl.multiple_of(s * r, r), r), pl.ds(pl.multiple_of(h * w, w), w)], target)]

    return view


def scatter_steps(place, units, stores, between=lambda at: None):
    n = place.n
    middle = [u for u in units if not u.late]
    late = [u for u in units if u.late]

    def each(run, some=units):
        def one(i):
            for unit in some:
                run(unit, i)

        return one

    def begin():
        repeat(n, each(lambda u, i: u.start(1 - u.f, 1 - u.g, place.along(i))))
        repeat(n, each(lambda u, i: u.start(1 - u.f, u.g, place.along(i))))
        repeat(n, each(lambda u, i: u.start(u.f, 1 - u.g, place.along(i))))
        repeat(n, each(lambda u, i: u.start(u.f, u.g, place.along(i))))
        between(0)

    def flips():
        repeat(n, each(lambda u, i: u.flip_first(1 - u.g, place.along(i)), middle))
        repeat(n, each(lambda u, i: u.flip_first(1 - u.g, place.along(i)), late))
        repeat(n, each(lambda u, i: u.flip_first(u.g, place.along(i)), middle))
        repeat(n, each(lambda u, i: u.flip_first(u.g, place.along(i)), late))
        between(1)

    def second(d):
        for u in middle:
            u.move(1 - u.g, d)
        for u in late:
            u.flip_second(place.along(n - 1 - d))

    def third(d):
        for u in middle:
            u.move(u.g, d)

    def fourth():
        for u in late:
            u.flip_second(place.along(n - 1))
        for u in middle:
            u.flip_second(place.a)
        between(2)

    def fifth(d):
        for u in late:
            u.move(u.g, d)

    def finish():
        between(3)
        for unit, store in zip(units, stores):
            unit.finish(store)
        between(4)

    far = range(n - 1, 0, -1)
    return (
        [begin, flips]
        + [functools.partial(second, d) for d in far]
        + [functools.partial(third, d) for d in far]
        + [fourth]
        + [functools.partial(fifth, d) for d in far]
        + [finish]
    )


def store_into(out):
    def store(value):
        out[...] = value

    return store


def scatter_dense_units(place, count, grads, outs, scratch):
    units, stores = [], []
    for ref, out, first in zip(grads, outs, (0, 2, 1)):
        rows = out.shape[0]
        for at, size, order in block_scatters(rows, first):
            units.append(Scatter(place, block_pairs(ref, rows, at, size, count), order, *scratch[:8]))
            stores.append(store_into(out.at[pl.ds(at, size)]))
            scratch = scratch[8:]
    return units, stores


def scatter_dense_scratch(count, shapes):
    scratch = []
    for (rows, width), first in zip(shapes, (0, 2, 1)):
        for at, size, order in block_scatters(rows, first):
            scratch += scatter_scratch(count, (size, width), order)
    return scratch


def scatter_dense_kernel(count, up, down, o, up_out, down_out, o_out, *scratch):
    place = Place(count)
    place.barrier()
    units, stores = scatter_dense_units(place, count, (up, down, o), (up_out, down_out, o_out), scratch)
    for step in scatter_steps(place, units, stores):
        step()


def scatter_attention_kernel(
    count, q, k, v, p, sq, vec, q_out, k_out, v_out, p_out, sq_out, vec_out, ub_out, sums, parts, vec_send, vec_recv, *scratch
):
    place = Place(count)
    place.barrier()
    r, w = q_out.shape
    units, stores = [], []
    for ref, out, order in zip((q, k, v, p), (q_out, k_out, v_out, p_out), SCATTER_ORDERS):
        units.append(Scatter(place, square_pairs(ref, r, w), order, *scratch[:8]))
        stores.append(store_into(out))
        scratch = scratch[8:]
    rows = sq_out.shape[0]
    for at, size, order in block_scatters(rows, 0):
        units.append(Scatter(place, block_pairs(sq, rows, at, size, count), order, *scratch[:8]))
        stores.append(store_into(sq_out.at[pl.ds(at, size)]))
        scratch = scratch[8:]

    def vec_copy(kind):
        return pltpu.make_async_remote_copy(
            src_ref=sums.at[kind],
            dst_ref=parts.at[kind],
            send_sem=vec_send.at[kind],
            recv_sem=vec_recv.at[kind],
            device_id=place.neighbour(kind),
            device_id_type=MESH,
        )

    def between(at):
        kinds = (CORE, XFLIP, YFLIP)
        if at == 0:
            sums[CORE] = vec[...]
            vec_copy(CORE).start()
        elif at < 3:
            vec_copy(kinds[at - 1]).wait_recv()
            sums[kinds[at]] = sums[kinds[at - 1]] + parts[kinds[at - 1]]
            vec_copy(kinds[at]).start()
        elif at == 3:
            vec_copy(YFLIP).wait_recv()
            total = sums[YFLIP] + parts[YFLIP]
            ends = (place.a > 0, place.a < place.n - 1)
            sums[UP] = total
            sums[DOWN] = total
            for kind, fed in ((UP, ends[0]), (DOWN, ends[1])):
                @pl.when(fed)
                def _(kind=kind):
                    vec_copy(kind).wait_recv()
                    sums[kind] = sums[kind] + parts[kind]

                @place.when(kind)
                def _(kind=kind):
                    vec_copy(kind).start()
        else:
            total = sums[UP] + sums[DOWN] - (sums[YFLIP] + parts[YFLIP])
            width = total.shape[1]
            both = vec_out.shape[1]
            k = place.h * count + place.s
            mine = pltpu.roll(total, lax.rem(width - k * both, width), 1)
            vec_out[...] = mine[:, :both]
            wide = ub_out.shape[1]
            flat = k * wide
            lanes = lax.rem(flat, width)
            mine = pltpu.roll(total, lax.rem(width - lanes, width), 1)[:, :wide]
            row = lax.broadcasted_iota(jnp.int32, mine.shape, 0)
            ub_out[...] = jnp.sum(jnp.where(row == 12 + flat // width, mine, 0.0), axis=0, keepdims=True)
            for kind in range(5):
                @place.when(kind)
                def _(kind=kind):
                    vec_copy(kind).wait_send()

    for step in scatter_steps(place, units, stores, between):
        step()


def scatter_dense(g):
    count = lax.axis_size("seq")
    names = ("up", "down", "o")
    shapes = [(g[n].shape[0] // (2 * count), g[n].shape[1]) for n in names]
    outs = pl.pallas_call(
        functools.partial(scatter_dense_kernel, count),
        in_specs=[pl.BlockSpec(memory_space=pl.ANY)] * 3,
        out_specs=[pl.BlockSpec(memory_space=pltpu.VMEM)] * 3,
        out_shape=[jax.ShapeDtypeStruct(shape, F32) for shape in shapes],
        scratch_shapes=scatter_dense_scratch(count, shapes),
        compiler_params=pltpu.CompilerParams(collective_id=1, has_side_effects=True, vmem_limit_bytes=48 * MIB),
        name="scatter_dense",
    )(*[g[n] for n in names])
    return dict(zip(names, outs))


VECTORS = ("cb", "pb", "sb", "ob", "g1", "s1", "db", "g2", "s2")


def scatter_attention(g):
    count = lax.axis_size("seq")
    width = g["q"].shape[0]
    both = width // (2 * count)
    lines = [g[n].reshape(1, width) for n in VECTORS]
    vec = jnp.concatenate(lines + [jnp.zeros((12 - len(lines), width), F32), g["ub"].reshape(-1, width)], axis=0)
    square = (width // count, width // 2)
    narrow = (both, g["sq"].shape[1])
    scratch = []
    for order in SCATTER_ORDERS:
        scratch += scatter_scratch(count, square, order)
    for at, size, order in block_scatters(both, 0):
        scratch += scatter_scratch(count, (size, narrow[1]), order)
    vmem = pl.BlockSpec(memory_space=pltpu.VMEM)
    outs = pl.pallas_call(
        functools.partial(scatter_attention_kernel, count),
        in_specs=[pl.BlockSpec(memory_space=pl.ANY)] * 5 + [vmem],
        out_specs=[vmem] * 7,
        out_shape=[jax.ShapeDtypeStruct(square, F32)] * 4
        + [jax.ShapeDtypeStruct(s, F32) for s in (narrow, (16, both), (1, 4 * both))],
        scratch_shapes=[
            pltpu.VMEM((5, 16, width), F32),
            pltpu.VMEM((5, 16, width), F32),
            pltpu.SemaphoreType.DMA((5,)),
            pltpu.SemaphoreType.DMA((5,)),
            *scratch,
        ],
        compiler_params=pltpu.CompilerParams(collective_id=2, has_side_effects=True, vmem_limit_bytes=48 * MIB),
        name="scatter_attention",
    )(g["q"], g["k"], g["v"], g["p"], g["sq"], vec)
    final = dict(zip(("q", "k", "v", "p", "sq"), outs[:5]))
    final.update({n: outs[5][i] for i, n in enumerate(VECTORS)})
    final["ub"] = outs[6].reshape(4 * both)
    return final


def normalize(values):
    centre = values - jnp.mean(values, axis=-1, keepdims=True)
    spread = jnp.mean(centre * centre, axis=-1, keepdims=True)
    scale = lax.rsqrt(spread + epsilon)
    return centre * scale, scale


def normalize_back(grad, gain, unit, scale):
    pulled = grad * gain
    return scale * (
        pulled
        - jnp.mean(pulled, axis=-1, keepdims=True)
        - unit * jnp.mean(pulled * unit, axis=-1, keepdims=True)
    )


def gelu_parts(u):
    root = np.float32(np.sqrt(2.0 / np.pi))
    inner = root * (u + 0.044715 * u * u * u)
    tanh = jnp.tanh(inner)
    value = 0.5 * u * (1.0 + tanh)
    slope = 0.5 * (1.0 + tanh) + 0.5 * u * (1.0 - tanh * tanh) * root * (1.0 + 3 * 0.044715 * u * u)
    return value, slope


def exchange_rows(array, head):
    half = array.shape[0] // 2
    mine = lax.dynamic_slice_in_dim(array, head * half, half, 0)
    theirs = lax.dynamic_slice_in_dim(array, (1 - head) * half, half, 0)
    other = lax.ppermute(theirs, "head", [(0, 1), (1, 0)])
    first = jnp.where(head == 0, mine, other)
    second = jnp.where(head == 0, other, mine)
    return jnp.stack([first, second])[:, None]


def body(
    inputs, lengths,
    query_weight, key_weight, value_weight, position_weight, content_bias, position_bias,
    output_weight, output_bias, first_gain, first_shift, up_weight, up_bias, down_weight, down_bias,
    second_gain, second_shift, squeeze_weight, squeeze_bias, cotangent,
):
    seq = lax.axis_index("seq")
    head = lax.axis_index("head")
    rows, width = inputs.shape[2:]

    x = lax.dynamic_index_in_dim(inputs[:, 0], head, 0, keepdims=False)
    book_lengths = lax.dynamic_index_in_dim(lengths, head, 0, keepdims=False)
    padded_lengths = jnp.concatenate([jnp.zeros((4,), jnp.int32), book_lengths])
    window = lax.dynamic_slice_in_dim(padded_lengths, seq, 5, 0)
    own_length = window[4]

    memory = shifted(x, "seq", 1)
    shards = dict(
            q=query_weight, k=key_weight, v=value_weight, p=position_weight,
            o=output_weight, up=up_weight.T, down=down_weight, sq=squeeze_weight.T,
            cb=content_bias, pb=position_bias, ob=output_bias, g1=first_gain, s1=first_shift, ub=up_bias,
            db=down_bias, g2=second_gain, s2=second_shift, sb=squeeze_bias,
    )
    w = gather_attention(shards)
    w.update(gather_dense(shards))
    cb, pb, ob, g1, s1, ub, db, g2, s2, sb = (
        w[n] for n in ("cb", "pb", "ob", "g1", "s1", "ub", "db", "g2", "s2", "sb")
    )

    pad, taps, collect, biased = squeeze_layout(rows)
    row_ids = jnp.arange(rows)
    kept = (row_ids < own_length)[:, None]
    masked = jnp.where(kept, x, jnp.zeros_like(x))
    made = biased * sb
    for tap in range(3):
        made = made + mm_nt(mm_tn(taps[tap], masked, BF), w["sq"][:, tap * width : (tap + 1) * width])
    made = made.astype(BF)
    arrived = jnp.concatenate(
        [shifted(made[role * pad : (role + 1) * pad], "seq", 4 - role) for role in range(3)], axis=0
    )
    squeezed = mm(collect, arrived, out=BF)
    keys_in = jnp.concatenate([squeezed, memory, x], axis=0)

    flat = np.arange(0, 3 * rows, 3)
    history_ok = jnp.asarray(flat % rows) < window[:3][flat // rows]
    valid = jnp.concatenate([history_ok, row_ids < window[3], row_ids < window[4]])
    key_bias = jnp.where(valid, 0.0, -1e30).astype(F32)[None]

    query = mm(x, w["q"])
    keys = mm(keys_in, w["k"], out=BF)
    values = mm(keys_in, w["v"], out=BF)
    table = jnp.asarray(table_rows(width, 3 * rows))
    places = mm(table, w["p"], out=BF)
    attended, probs = attend_forward(key_bias, cb, pb, query, keys, values, places)

    blended = x.astype(F32) + mm(attended, w["o"]) + ob
    unit1, scale1 = normalize(blended)
    normed = (unit1 * g1 + s1).astype(BF)
    u = mm_nt(normed, w["up"]) + ub
    hidden_f, slope = gelu_parts(u)
    hidden = hidden_f.astype(BF)
    unit2, scale2 = normalize(normed.astype(F32) + mm(hidden, w["down"]) + db)
    outputs = (unit2 * g2 + s2).astype(BF)

    grads = {}
    ct = lax.dynamic_index_in_dim(cotangent[:, 0], head, 0, keepdims=False).astype(F32)
    grads["g2"] = jnp.sum(ct * unit2, axis=0)
    grads["s2"] = jnp.sum(ct, axis=0)
    dy = normalize_back(ct, g2, unit2, scale2)
    grads["db"] = jnp.sum(dy, axis=0)
    dy_b = dy.astype(BF)
    grads["down"] = mm_tn(hidden, dy_b, BF)
    du = (mm_nt(dy_b, w["down"]) * slope).astype(BF)
    grads["ub"] = jnp.sum(du.astype(F32), axis=0)
    grads["up"] = mm_tn(du, normed, BF)
    dnormed = dy + mm(du, w["up"])
    grads["g1"] = jnp.sum(dnormed * unit1, axis=0)
    grads["s1"] = jnp.sum(dnormed, axis=0)
    dblended = normalize_back(dnormed, g1, unit1, scale1)
    grads["ob"] = jnp.sum(dblended, axis=0)
    dblended_b = dblended.astype(BF)
    grads["o"] = mm_tn(attended, dblended_b, BF)
    dattended = mm_nt(dblended_b, w["o"], BF)

    dq, dcb, dpb, dk, dv, dplaces = attend_backward(cb, pb, query, keys, values, places, probs, dattended)
    grads["cb"] = dcb[0]
    grads["pb"] = dpb[0]
    dkeys_in = mm_nt(dk, w["k"]) + mm_nt(dv, w["v"])
    dsqueezed = dkeys_in[:rows].astype(BF)
    grads["sb"] = jnp.sum(dsqueezed.astype(F32), axis=0)
    dmade = mm_tn(collect, dsqueezed, BF)
    returned = jnp.concatenate(
        [shifted(dmade[role * pad : (role + 1) * pad], "seq", role - 4) for role in range(3)], axis=0
    )
    from_next = shifted(dkeys_in[rows : 2 * rows].astype(BF), "seq", -1)
    grads["q"] = mm_tn(x, dq, BF)
    grads["k"] = mm_tn(keys_in, dk, BF)
    grads["v"] = mm_tn(keys_in, dv, BF)
    grads["p"] = mm_tn(table, dplaces, BF)
    dx = dblended + mm_nt(dq, w["q"]) + dkeys_in[2 * rows :] + from_next.astype(F32)
    dmasked = jnp.zeros((rows, width), F32)
    sq_grads = []
    for tap in range(3):
        spread = mm(taps[tap], returned, out=BF)
        dmasked = dmasked + mm(spread, w["sq"][:, tap * width : (tap + 1) * width])
        sq_grads.append(mm_tn(spread, masked, BF))
    grads["sq"] = jnp.concatenate(sq_grads, axis=1)
    dx = dx + jnp.where(kept, dmasked, 0.0)

    final = {**scatter_dense(grads), **scatter_attention(grads)}
    return (
        exchange_rows(outputs, head),
        exchange_rows(dx.astype(BF), head),
        final["q"], final["k"], final["v"], final["p"], final["cb"], final["pb"],
        final["o"], final["ob"], final["g1"], final["s1"], final["up"].T, final["ub"],
        final["down"], final["db"], final["g2"], final["s2"], final["sq"].T, final["sb"],
    )


def solution(mesh):
    both = ("head", "seq")
    matrix = P("seq", "head")
    in_specs = (
        P(None, "seq", None, None), P(), matrix, matrix, matrix, matrix, P(both), P(both),
        P(both, None), P("seq"), P("seq"), P("seq"), P(None, both), P(both), P(both, None), P("seq"),
        P("seq"), P("seq"), P(None, both), P(both), P(None, "seq", None, None),
    )
    rows = P(None, "seq", "head", None)
    out_specs = (
        rows, rows, matrix, matrix, matrix, matrix, P(both), P(both),
        P(both, None), P(both), P(both), P(both), P(None, both), P(both), P(both, None), P(both),
        P(both), P(both), P(None, both), P(both),
    )
    return jax.shard_map(body, mesh=mesh, in_specs=in_specs, out_specs=out_specs, check_vma=False)
```

```python
import functools

import jax
import jax.numpy as jnp
import numpy as np
from jax import lax
from jax.experimental import pallas as pl
from jax.experimental.pallas import tpu as pltpu
from jax.sharding import PartitionSpec as P

HD = 128
BF = jnp.bfloat16
F32 = jnp.float32
epsilon = 1e-05
MIB = 1024 * 1024


def mm(left, right, contract=((1,), (0,)), out=F32):
    return lax.dot_general(left, right, (contract, ((), ())), preferred_element_type=F32).astype(out)


def mm_nt(left, right, out=F32):
    return mm(left, right, ((1,), (1,)), out)


def mm_tn(left, right, out=F32):
    return mm(left, right, ((0,), (0,)), out)


def shifted(array, axis, by):
    count = lax.axis_size(axis)
    pairs = [(i, i + by) for i in range(count) if 0 <= i + by < count]
    return lax.ppermute(array, axis, pairs)


def table_rows(width, count):
    distance = np.arange(count - 1, -1, -1).astype(np.float32)[:, None]
    exponent = -np.arange(0, width, 2).astype(np.float32) / np.float32(width)
    frequency = np.power(np.float32(10000.0), exponent).astype(np.float32)
    angles = (distance * frequency[None, :]).astype(np.float32)
    return np.concatenate([np.sin(angles), np.cos(angles)], axis=1).astype(BF)


def squeeze_layout(rows):
    pad = -(-(rows // 3 + 2) // 16) * 16
    taps = np.zeros((3, rows, 3 * pad), np.float32)
    collect = np.zeros((rows, 3 * pad), np.float32)
    biased = np.zeros((3 * pad, 1), np.float32)
    for role in range(3):
        first = role * rows // 3
        for i in range(rows):
            flat = role * rows + i
            taps[flat % 3, i, role * pad + flat // 3 - first] = 1.0
            collect[flat // 3, role * pad + flat // 3 - first] = 1.0
        for c in range(first, ((role + 1) * rows - 1) // 3 + 1):
            if role == 0 or 3 * c >= role * rows:
                biased[role * pad + c - first] = 1.0
    return pad, taps.astype(BF), collect.astype(BF), biased


MESH = pl.DeviceIdType.MESH
CORE, XFLIP, YFLIP, UP, DOWN = range(5)


def repeat(count, run):
    def body(i, carry):
        run(i)
        return carry

    lax.fori_loop(0, count, body, 0)


class Place:
    def __init__(self, count):
        self.count = count
        self.n = count // 4
        self.h = lax.axis_index("head")
        self.s = lax.axis_index("seq")
        self.a = self.s // 4
        self.b = (self.s // 2) % 2
        self.c = self.s % 2

    def seq_of(self, a, b, c):
        return a * 4 + b * 2 + c

    def neighbour(self, kind):
        s, h = self.s, self.h
        if kind == CORE:
            return (h, s + 1 - 2 * self.c)
        if kind == XFLIP:
            return (h, s + 2 - 4 * self.b)
        if kind == YFLIP:
            return (1 - h, s)
        return (h, s + 4) if kind == UP else (h, s - 4)

    def when(self, kind):
        if kind == UP:
            return pl.when(self.a < self.n - 1)
        if kind == DOWN:
            return pl.when(self.a > 0)
        return lambda run: run()

    def barrier(self):
        barrier = pltpu.get_barrier_semaphore()
        for kind in range(5):
            @self.when(kind)
            def _(kind=kind):
                pl.semaphore_signal(barrier, inc=1, device_id=self.neighbour(kind), device_id_type=MESH)
        ends = jnp.where(self.a == 0, 1, 0) + jnp.where(self.a == self.n - 1, 1, 0)
        pl.semaphore_wait(barrier, 5 - ends)

    def along(self, i):
        return (self.a + self.n // 2 + i) % self.n


class Gather:
    def __init__(self, place, units, local_sem, send_sem, recv_sem):
        self.place, self.units = place, units
        self.local_sem, self.send_sem, self.recv_sem = local_sem, send_sem, recv_sem

    def view(self, u, h, s):
        shard, full, view, order = self.units[u]
        return view(full, h, s)

    def copy(self, u, kind, h, s, own=False):
        n = self.place.n
        a, b = s // 4, (s // 2) % 2
        order = self.units[u][3]
        other = b if order.index("x") < order.index("z") else h
        sent = {
            UP: other * n + a,
            DOWN: (2 + other) * n + a,
            XFLIP: (4 + h) * n + a,
            YFLIP: (6 + b) * n + a,
            CORE: (8 + h * 2 + b) * n + a,
        }[kind]
        there = self.view(u, h, s)
        return pltpu.make_async_remote_copy(
            src_ref=self.units[u][0] if own else there,
            dst_ref=there,
            send_sem=self.send_sem.at[u, sent],
            recv_sem=self.recv_sem.at[u, h * self.place.count + s],
            device_id=self.place.neighbour(kind),
            device_id_type=MESH,
        )

    def local(self, u):
        return pltpu.make_async_copy(self.units[u][0], self.view(u, self.place.h, self.place.s), self.local_sem.at[u])

    def sources(self):
        found = []
        for t in range(self.place.n):
            for sign in ((1, -1) if t else (0,)):
                for x in (0, 1):
                    for y in (0, 1):
                        if t or x or y:
                            found.append((t, sign, x, y))
        return sorted(found, key=lambda e: e[0] + e[2] + e[3])

    def onward(self, u, sign, x, y):
        order = self.units[u][3]
        moved = {"x": x, "y": y, "z": sign}
        last = max([i for i in range(3) if moved[order[i]]], default=-1)
        kinds = []
        if last >= 0 and order[last] == "z":
            kinds.append(UP if sign > 0 else DOWN)
        for dim in order[last + 1 :]:
            kinds += {"x": [XFLIP], "y": [YFLIP], "z": [UP, DOWN]}[dim]
        return kinds + [CORE]

    def send(self, u, kind, h, s, own, wait):
        @self.place.when(kind)
        def _():
            copy = self.copy(u, kind, h, s, own)
            if wait:
                copy.wait_send()
            else:
                copy.start()

    def begin(self, wait=False):
        p = self.place
        for u in range(len(self.units)):
            for kind in self.onward(u, 0, 0, 0):
                self.send(u, kind, p.h, p.s, True, wait)
        for u in range(len(self.units)):
            if wait:
                self.local(u).wait()
            else:
                self.local(u).start()

    def pass_on(self, entry, wait=False):
        p = self.place
        t, sign, x, y = entry
        a = p.a - sign * t
        h = 1 - p.h if y else p.h
        s = p.seq_of(a, 1 - p.b if x else p.b, p.c)

        def run():
            for u in range(len(self.units)):
                if not wait:
                    self.copy(u, CORE, h, s).wait_recv()
                for kind in self.onward(u, sign, x, y):
                    self.send(u, kind, h, s, False, wait)

        if t:
            pl.when(jnp.logical_and(a >= 0, a <= p.n - 1))(run)
        else:
            run()

    def finish(self):
        p = self.place

        def core(i):
            h, a, b = i // (2 * p.n), i // 2 % p.n, i % 2
            for u in range(len(self.units)):
                self.copy(u, CORE, h, p.seq_of(a, b, 1 - p.c)).wait_recv()

        repeat(4 * p.n, core)
        self.begin(True)
        for entry in self.sources():
            self.pass_on(entry, True)

    def steps(self):
        return [self.begin] + [functools.partial(self.pass_on, entry) for entry in self.sources()] + [self.finish]


GATHER_ORDERS = ("yzx", "xzy", "zxy", "zyx")


def halves(rows):
    return [(0, rows // 2), (rows // 2, rows // 2)] if rows % 32 == 0 else [(0, rows)]


def block_units(shard, full, count, first):
    rows = shard.shape[0]
    units = []
    for i, (at, size) in enumerate(halves(rows)):
        def view(ref, h, s, at=at, size=size):
            return ref.at[pl.ds(pl.multiple_of((h * count + s) * rows + at, size), size)]

        units.append((shard.at[pl.ds(at, size)], full, view, GATHER_ORDERS[(first + i) % 4]))
    return units


def square_unit(shard, full, order):
    r, w = shard.shape

    def view(ref, h, s):
        return ref.at[pl.ds(pl.multiple_of(s * r, r), r), pl.ds(pl.multiple_of(h * w, w), w)]

    return (shard, full, view, order)


def gather_attention_kernel(count, small_names, *refs):
    shards, (vec, vec_up) = refs[:6], refs[11:13]
    fulls = refs[6:11] + refs[13:14]
    place = Place(count)
    place.barrier()
    units = [square_unit(shards[i], fulls[i], GATHER_ORDERS[i]) for i in range(4)]
    units += block_units(shards[4], fulls[4], count, 0)
    small, small_f = shards[5], fulls[5]

    def small_view(ref, h, s):
        return ref.at[pl.ds(pl.multiple_of((h * count + s) * 8, 8), 8)]

    units.append((small, small_f, small_view, "zxy"))
    gather = Gather(place, units, *refs[14:])
    for step in gather.steps():
        step()
    for slot in range(2 * count):
        for name, row, at, size, target in small_names:
            if size * 2 * count > vec.shape[1] * (4 if name == "ub" else 1) and slot >= count:
                continue
            ref = vec_up if name == "ub" else vec
            ref[target : target + 1, slot * size : (slot + 1) * size] = small_f[slot * 8 + row : slot * 8 + row + 1, at : at + size]


def gather_semaphores(count, units):
    return [
        pltpu.SemaphoreType.DMA((units,)),
        pltpu.SemaphoreType.DMA((units, 12 * (count // 4))),
        pltpu.SemaphoreType.DMA((units, 2 * count)),
    ]


def small_layout(both, seq):
    names = []
    for i, name in enumerate(("cb", "pb", "sb")):
        names.append((name, 0, i * both, both, i))
    names.append(("ub", 1, 0, 4 * both, 0))
    for i, name in enumerate(("ob", "g1", "s1", "db", "g2", "s2")):
        names.append((name, 2 + i // 2, (i % 2) * seq, seq, 3 + i))
    return names


def gather_attention(w):
    count = lax.axis_size("seq")
    both, seq = w["cb"].shape[0], w["ob"].shape[0]
    width = both * 2 * count
    layout = small_layout(both, seq)
    lines = [[] for _ in range(8)]
    for name, row, at, size, target in layout:
        lines[row].append(w[name].astype(F32))
    lines = [jnp.concatenate(parts) if parts else jnp.zeros((128,), F32) for parts in lines]
    small = jnp.stack([jnp.pad(line, (0, 128 - line.shape[0])) for line in lines])
    names = ("q", "k", "v", "p", "sq")
    any_spec = pl.BlockSpec(memory_space=pl.ANY)
    vmem_spec = pl.BlockSpec(memory_space=pltpu.VMEM)
    outs = pl.pallas_call(
        functools.partial(gather_attention_kernel, count, layout),
        in_specs=[any_spec] * 6,
        out_specs=[any_spec] * 5 + [vmem_spec] * 2,
        out_shape=[
            *[jax.ShapeDtypeStruct((width, width), BF) for _ in range(4)],
            jax.ShapeDtypeStruct((width, w["sq"].shape[1]), BF),
            jax.ShapeDtypeStruct((16, width), F32),
            jax.ShapeDtypeStruct((1, 4 * width), F32),
        ],
        scratch_shapes=[
            pltpu.VMEM((8 * 2 * count, 128), F32),
            *gather_semaphores(count, 5 + len(halves(w["sq"].shape[0]))),
        ],
        compiler_params=pltpu.CompilerParams(collective_id=0, has_side_effects=True, vmem_limit_bytes=16 * MIB),
        name="gather_attention",
    )(*[w[n] for n in names], small)
    full = dict(zip(names, outs))
    for name, row, at, size, target in layout:
        full[name] = outs[6] if name == "ub" else outs[5][target : target + 1]
    return full


class Scatter:
    def __init__(self, place, view, order, sums, own, first, second, line, local_sem, send_sem, recv_sem):
        self.place, self.view = place, view
        self.by_y = order[0] == "y"
        self.late = order[2] == "z"
        self.sums, self.own, self.first, self.second, self.line = sums, own, first, second, line
        self.local_sem, self.send_sem, self.recv_sem = local_sem, send_sem, recv_sem
        self.f, self.g = (place.h, place.b) if self.by_y else (place.b, place.h)
        self.flips = (YFLIP, XFLIP) if self.by_y else (XFLIP, YFLIP)

    def index(self, f, g, a):
        return (f * 2 + g) * self.place.n + a

    def slot(self, f, g, a, c):
        h, b = (f, g) if self.by_y else (g, f)
        return h, self.place.seq_of(a, b, c)

    def remote(self, source, target, kind, send_at, recv_at):
        return pltpu.make_async_remote_copy(
            src_ref=source,
            dst_ref=target,
            send_sem=self.send_sem.at[send_at],
            recv_sem=self.recv_sem.at[recv_at],
            device_id=self.place.neighbour(kind),
            device_id_type=MESH,
        )

    def core_copy(self, i):
        return self.remote(self.sums.at[i], self.sums.at[i], CORE, i, i)

    def first_copy(self, g, a):
        n = self.place.n
        to = g * n + a
        return self.remote(self.sums.at[self.index(1 - self.f, g, a)], self.first.at[to], self.flips[0], 4 * n + to, 4 * n + to)

    def second_copy(self, a):
        n = self.place.n
        to = a if self.late else 0
        return self.remote(self.sums.at[self.index(self.f, 1 - self.g, a)], self.second.at[to], self.flips[1], 6 * n + to, 6 * n + to)

    def line_at(self, g, at):
        return at if self.late else g * (self.place.n + 1) + at

    def line_copy(self, kind, g, a):
        n = self.place.n
        to = self.line_at(g, a if kind == UP else jnp.where(a == self.place.a - 1, n, a))
        sent = 7 * n + (a if self.late else g * n + a)
        return self.remote(self.sums.at[self.index(self.f, g, a)], self.line.at[to], kind, sent, 7 * n + to)

    def line_wait(self, at):
        n = self.place.n
        self.remote(self.line.at[at], self.line.at[at], CORE, 7 * n, 7 * n + at).wait_recv()

    def piece(self, part, i):
        return (self.f if part >= 2 else 1 - self.f, self.g if part % 2 else 1 - self.g, self.place.along(i))

    def trade(self, part, i):
        f, g, a = self.piece(part, i)
        at = self.index(f, g, a)
        source = self.view(*self.slot(f, g, a, 1 - self.place.c))
        self.remote(source, self.sums.at[at], CORE, at, at).start()

    def load(self, part, i):
        source = self.view(*self.slot(*self.piece(part, i), self.place.c))
        return pltpu.make_async_copy(source, self.own.at[i % 4], self.local_sem.at[i % 4])

    def absorb(self, part, i):
        n = self.place.n
        f, g, a = self.piece(part, i)
        at = self.index(f, g, a)
        self.load(part, i).wait()
        self.core_copy(at).wait_recv()
        self.add(at, [(self.own, i % 4)])

        @pl.when(i + 4 < n)
        def _():
            self.load(part, i + 4).start()

        if part < 3:
            @pl.when(i + 4 >= n)
            def _():
                self.load(part + 1, i + 4 - n).start()

        if part < 2:
            self.first_copy(g, a).start()

    def after_first(self, g, a):
        self.first_copy(g, a).wait_recv()
        return self.index(self.f, g, a), [(self.first, g * self.place.n + a)]

    def add(self, i, refs):
        total = self.sums[i].astype(F32)
        for ref, at in refs:
            total = total + ref[at].astype(F32)
        self.sums[i] = total.astype(BF)

    def add_line(self, i, g):
        p = self.place
        for fed, at in ((p.a > 0, p.a), (p.a < p.n - 1, p.n)):
            @pl.when(fed)
            def _(at=self.line_at(g, at)):
                self.line_wait(at)
                self.add(i, [(self.line, at)])

    def flip_second(self, a):
        i, refs = self.after_first(1 - self.g, a)
        self.add(i, refs)
        if not self.late:
            self.add_line(i, 1 - self.g)
        self.second_copy(a).start()

    def move(self, g, d):
        p = self.place
        for kind, a, inside, fed in (
            (UP, p.a + d, p.a + d <= p.n - 1, p.a > 0),
            (DOWN, p.a - d, p.a - d >= 0, p.a < p.n - 1),
        ):
            @pl.when(inside)
            def _(kind=kind, a=a, fed=fed):
                i, refs = self.after_first(g, a)
                if self.late:
                    self.second_copy(a).wait_recv()
                    refs.append((self.second, a))
                self.add(i, refs)

                @pl.when(fed)
                def _():
                    at = self.line_at(g, a)
                    self.line_wait(at)
                    self.add(i, [(self.line, at)])

                self.line_copy(kind, g, a).start()

    def finish(self, store):
        p = self.place
        n = p.n
        i, refs = self.after_first(self.g, p.a)
        to = p.a if self.late else 0
        self.second_copy(p.a).wait_recv()
        self.add(i, refs + [(self.second, to)])
        self.add_line(i, self.g)
        store(self.sums[i].astype(F32))
        repeat(4 * n, lambda i: self.core_copy(i).wait_send())
        repeat(2 * n, lambda i: self.first_copy(i // n, i % n).wait_send())
        if self.late:
            repeat(n, lambda a: self.second_copy(a).wait_send())
        else:
            self.second_copy(p.a).wait_send()

        def line_done(a):
            for kind, inside in ((UP, a > p.a), (DOWN, a < p.a)):
                @pl.when(inside)
                def _(kind=kind):
                    for g in (self.g,) if self.late else (0, 1):
                        self.line_copy(kind, g, a).wait_send()

        repeat(n, line_done)


def scatter_scratch(count, shape, order):
    n = count // 4
    late = order[2] == "z"
    lines = n + 1 if late else 2 * n + 2
    return [
        *[pltpu.VMEM((k, *shape), BF) for k in (4 * n, 4, 2 * n, n if late else 1, lines)],
        pltpu.SemaphoreType.DMA((4,)),
        pltpu.SemaphoreType.DMA((9 * n,)),
        pltpu.SemaphoreType.DMA((7 * n + lines,)),
    ]


SCATTER_ORDERS = ("yzx", "xzy", "yxz", "xyz")


def block_scatters(rows, first):
    return [(at, size, SCATTER_ORDERS[(first + i) % 4]) for i, (at, size) in enumerate(halves(rows))]


def block_pairs(ref, rows, at, size, count):
    def view(h, s):
        return ref.at[pl.ds(pl.multiple_of((h * count + s) * rows + at, size), size)]

    return view


def square_pairs(ref, r, w):
    def view(h, s):
        return ref.at[pl.ds(pl.multiple_of(s * r, r), r), pl.ds(pl.multiple_of(h * w, w), w)]

    return view


def scatter_steps(place, units, stores, between=lambda at: None):
    n = place.n
    middle = [u for u in units if not u.late]
    late = [u for u in units if u.late]

    def each(run, some=units):
        def one(i):
            for unit in some:
                run(unit, i)

        return one

    def begin():
        for part in range(4):
            repeat(n, each(lambda u, i, part=part: u.trade(part, i)))
            if part == 0:
                repeat(4, each(lambda u, i: u.load(0, i).start()))
        between(0)

    def absorb(part):
        repeat(n, each(lambda u, i: u.absorb(part, i), middle + late))

    def second(d):
        for u in middle:
            u.move(1 - u.g, d)
        for u in late:
            u.flip_second(place.along(n - 1 - d))

    def third(d):
        for u in middle:
            u.move(u.g, d)

    def fourth():
        between(1)
        for u in late:
            u.flip_second(place.along(n - 1))
        for u in middle:
            u.flip_second(place.a)
        between(2)

    def fifth(d):
        for u in late:
            u.move(u.g, d)

    def finish():
        between(3)
        for unit, store in zip(units, stores):
            unit.finish(store)
        between(4)

    far = range(n - 1, 0, -1)
    return (
        [begin]
        + [functools.partial(absorb, part) for part in range(4)]
        + [functools.partial(second, d) for d in far]
        + [functools.partial(third, d) for d in far]
        + [fourth]
        + [functools.partial(fifth, d) for d in far]
        + [finish]
    )


def store_into(out):
    def store(value):
        out[...] = value

    return store


def scatter_dense_units(place, count, grads, outs, scratch):
    units, stores = [], []
    for ref, out, first in zip(grads, outs, (0, 2, 1)):
        rows = out.shape[0]
        for at, size, order in block_scatters(rows, first):
            units.append(Scatter(place, block_pairs(ref, rows, at, size, count), order, *scratch[:8]))
            stores.append(store_into(out.at[pl.ds(at, size)]))
            scratch = scratch[8:]
    return units, stores


def scatter_dense_scratch(count, shapes):
    scratch = []
    for (rows, width), first in zip(shapes, (0, 2, 1)):
        for at, size, order in block_scatters(rows, first):
            scratch += scatter_scratch(count, (size, width), order)
    return scratch


def scatter_attention_kernel(
    count, q, k, v, p, sq, vec, q_out, k_out, v_out, p_out, sq_out, vec_out, ub_out, sums, parts, vec_send, vec_recv, *scratch
):
    place = Place(count)
    place.barrier()
    r, w = q_out.shape
    units, stores = [], []
    for ref, out, order in zip((q, k, v, p), (q_out, k_out, v_out, p_out), SCATTER_ORDERS):
        units.append(Scatter(place, square_pairs(ref, r, w), order, *scratch[:8]))
        stores.append(store_into(out))
        scratch = scratch[8:]
    rows = sq_out.shape[0]
    for at, size, order in block_scatters(rows, 0):
        units.append(Scatter(place, block_pairs(sq, rows, at, size, count), order, *scratch[:8]))
        stores.append(store_into(sq_out.at[pl.ds(at, size)]))
        scratch = scratch[8:]

    def vec_copy(kind):
        return pltpu.make_async_remote_copy(
            src_ref=sums.at[kind],
            dst_ref=parts.at[kind],
            send_sem=vec_send.at[kind],
            recv_sem=vec_recv.at[kind],
            device_id=place.neighbour(kind),
            device_id_type=MESH,
        )

    def between(at):
        kinds = (CORE, XFLIP, YFLIP)
        if at == 0:
            sums[CORE] = vec[...]
            vec_copy(CORE).start()
        elif at < 3:
            vec_copy(kinds[at - 1]).wait_recv()
            sums[kinds[at]] = sums[kinds[at - 1]] + parts[kinds[at - 1]]
            vec_copy(kinds[at]).start()
        elif at == 3:
            vec_copy(YFLIP).wait_recv()
            total = sums[YFLIP] + parts[YFLIP]
            ends = (place.a > 0, place.a < place.n - 1)
            sums[UP] = total
            sums[DOWN] = total
            for kind, fed in ((UP, ends[0]), (DOWN, ends[1])):
                @pl.when(fed)
                def _(kind=kind):
                    vec_copy(kind).wait_recv()
                    sums[kind] = sums[kind] + parts[kind]

                @place.when(kind)
                def _(kind=kind):
                    vec_copy(kind).start()
        else:
            total = sums[UP] + sums[DOWN] - (sums[YFLIP] + parts[YFLIP])
            width = total.shape[1]
            both = vec_out.shape[1]
            k = place.h * count + place.s
            mine = pltpu.roll(total, lax.rem(width - k * both, width), 1)
            vec_out[...] = mine[:, :both]
            wide = ub_out.shape[1]
            flat = k * wide
            lanes = lax.rem(flat, width)
            mine = pltpu.roll(total, lax.rem(width - lanes, width), 1)[:, :wide]
            row = lax.broadcasted_iota(jnp.int32, mine.shape, 0)
            ub_out[...] = jnp.sum(jnp.where(row == 12 + flat // width, mine, 0.0), axis=0, keepdims=True)
            for kind in range(5):
                @place.when(kind)
                def _(kind=kind):
                    vec_copy(kind).wait_send()

    for step in scatter_steps(place, units, stores, between):
        step()


VECTORS = ("cb", "pb", "sb", "ob", "g1", "s1", "db", "g2", "s2")


def scatter_attention(g):
    count = lax.axis_size("seq")
    width = g["q"].shape[0]
    both = width // (2 * count)
    lines = [g[n].reshape(1, width) for n in VECTORS]
    vec = jnp.concatenate(lines + [jnp.zeros((12 - len(lines), width), F32), g["ub"].reshape(-1, width)], axis=0)
    square = (width // count, width // 2)
    narrow = (both, g["sq"].shape[1])
    scratch = []
    for order in SCATTER_ORDERS:
        scratch += scatter_scratch(count, square, order)
    for at, size, order in block_scatters(both, 0):
        scratch += scatter_scratch(count, (size, narrow[1]), order)
    vmem = pl.BlockSpec(memory_space=pltpu.VMEM)
    outs = pl.pallas_call(
        functools.partial(scatter_attention_kernel, count),
        in_specs=[pl.BlockSpec(memory_space=pl.ANY)] * 5 + [vmem],
        out_specs=[vmem] * 7,
        out_shape=[jax.ShapeDtypeStruct(square, F32)] * 4
        + [jax.ShapeDtypeStruct(s, F32) for s in (narrow, (16, both), (1, 4 * both))],
        scratch_shapes=[
            pltpu.VMEM((5, 16, width), F32),
            pltpu.VMEM((5, 16, width), F32),
            pltpu.SemaphoreType.DMA((5,)),
            pltpu.SemaphoreType.DMA((5,)),
            *scratch,
        ],
        compiler_params=pltpu.CompilerParams(collective_id=2, has_side_effects=True, vmem_limit_bytes=48 * MIB),
        name="scatter_attention",
    )(g["q"], g["k"], g["v"], g["p"], g["sq"], vec)
    final = dict(zip(("q", "k", "v", "p", "sq"), outs[:5]))
    final.update({n: outs[5][i] for i, n in enumerate(VECTORS)})
    final["ub"] = outs[6].reshape(4 * both)
    return final


def spread_steps(steps, points):
    out = [[] for _ in range(points)]
    for i, step in enumerate(steps):
        out[i * points // len(steps)].append(step)
    return out


def attend_forward_kernel(
    count, bias_ref, cb_ref, pb_ref, in_ref, table_ref, wq_ref, wk_ref, wv_ref, wp_ref, up, down, o,
    out_ref, p_ref, cq_ref, pq_ref, k_ref, v_ref, pl_ref, up_f, down_f, o_f,
    s_scr, x_scr, *sems,
):
    turn, turns = pl.program_id(0), pl.num_programs(0)
    place = Place(count)
    units = []
    for shard, full, first in ((up, up_f, 0), (down, down_f, 2), (o, o_f, 1)):
        units += block_units(shard, full, count, first)
    gather = Gather(place, units, *sems)
    first, *steps, last = gather.steps()
    heads = cq_ref.shape[1] // HD
    points = 2 + heads
    plan = spread_steps(steps, turns * points - 1)

    def point(k):
        for t in range(turns):
            chosen = plan[t * points + k - 1] if t or k else [place.barrier, first]
            if chosen:
                @pl.when(turn == t)
                def _(chosen=chosen):
                    for step in chosen:
                        step()

    rows, keys = cq_ref.shape[0], k_ref.shape[0]
    scale = HD ** (-0.5)
    point(0)
    query = mm(in_ref[2 * rows :], wq_ref[...])
    cq_ref[...] = ((query + cb_ref[...]) * scale).astype(BF)
    pq_ref[...] = ((query + pb_ref[...]) * scale).astype(BF)

    def project(source, weight, target):
        def one(i):
            here = pl.ds(pl.multiple_of(i * rows, rows), rows)
            target[here] = mm(source[here], weight[...]).astype(BF)

        repeat(keys // rows, one)

    project(in_ref, wk_ref, k_ref)
    point(1)
    project(in_ref, wv_ref, v_ref)
    project(table_ref, wp_ref, pl_ref)
    step = 32
    for head in range(heads):
        point(2 + head)
        cols = slice(head * HD, (head + 1) * HD)
        s_scr[...] = mm_nt(cq_ref[:, cols], k_ref[:, cols])
        x_scr[...] = mm_nt(pq_ref[:, cols], pl_ref[:, cols])
        for start in range(0, rows, step):
            here = slice(start, start + step)
            located = pltpu.roll(x_scr[here], (start + keys - rows + 1) % keys, 1, stride=1, stride_axis=0)
            scores = s_scr[here] + located + bias_ref[...]
            early, own = scores[:, : 2 * rows], scores[:, 2 * rows :]
            row = start + lax.broadcasted_iota(jnp.int32, own.shape, 0)
            col = lax.broadcasted_iota(jnp.int32, own.shape, 1)
            own = jnp.where(col <= row, own, -1e30)
            top = jnp.maximum(jnp.max(early, axis=1, keepdims=True), jnp.max(own, axis=1, keepdims=True))
            early, own = jnp.exp(early - top), jnp.exp(own - top)
            total = jnp.sum(early, axis=1, keepdims=True) + jnp.sum(own, axis=1, keepdims=True)
            share = 1.0 / total
            p_ref[head, here, : 2 * rows] = (early * share).astype(BF)
            p_ref[head, here, 2 * rows :] = (own * share).astype(BF)
        out_ref[:, cols] = mm(p_ref[head], v_ref[:, cols]).astype(BF)

    @pl.when(turn == turns - 1)
    def _():
        last()


def attend_forward(key_bias, content_bias, position_bias, keys_in, table, w, shards):
    count = lax.axis_size("seq")
    keys, width = keys_in.shape
    rows = keys // 3
    pair = 2 * HD
    names = ("up", "down", "o")

    def whole(shape):
        return pl.BlockSpec(shape, lambda t: (0,) * len(shape), pipeline_mode=pl.Buffered(1))

    def columns(height):
        return pl.BlockSpec((height, pair), lambda t: (0, t))

    any_spec = pl.BlockSpec(memory_space=pl.ANY)
    outs = pl.pallas_call(
        functools.partial(attend_forward_kernel, count),
        grid=(width // pair,),
        in_specs=[whole((1, keys)), columns(1), columns(1), whole((keys, width)), whole((keys, width))]
        + [columns(width)] * 4
        + [any_spec] * 3,
        out_specs=[columns(rows), pl.BlockSpec((2, rows, keys), lambda t: (t, 0, 0))]
        + [columns(rows)] * 2
        + [columns(keys)] * 3
        + [any_spec] * 3,
        out_shape=[
            jax.ShapeDtypeStruct((rows, width), BF),
            jax.ShapeDtypeStruct((width // HD, rows, keys), BF),
            *[jax.ShapeDtypeStruct((rows, width), BF)] * 2,
            *[jax.ShapeDtypeStruct((keys, width), BF)] * 3,
            *[jax.ShapeDtypeStruct((shards[n].shape[0] * 2 * count, width), BF) for n in names],
        ],
        scratch_shapes=[
            pltpu.VMEM((rows, keys), F32),
            pltpu.VMEM((rows, keys), F32),
            *gather_semaphores(count, sum(len(halves(shards[n].shape[0])) for n in names)),
        ],
        compiler_params=pltpu.CompilerParams(collective_id=3, has_side_effects=True, vmem_limit_bytes=56 * MIB),
        name="attend_forward",
    )(key_bias, content_bias, position_bias, keys_in, table, w["q"], w["k"], w["v"], w["p"], *[shards[n] for n in names])
    return outs[:7], dict(zip(names, outs[7:]))


BACKWARD_PLAN = (
    (0, 0), (0, 1), (0, 2), (1, 1), (1, 2),
    (3, 3), (4, 1), (4, 2),
    (5, 0), (5, 1), (5, 2),
    (5, 3),
    (6, 1), (7, 0), (7, 2),
)


def attend_backward_kernel(
    count, cq_ref, pq_ref, k_ref, v_ref, pl_ref, p_ref, do_ref, in_t_ref, table_t_ref, wq_ref, wk_ref, wv_ref, up, down, o,
    dcb_ref, dpb_ref, gq_ref, gk_ref, gv_ref, gp_ref, up_out, down_out, o_out, dsq_out, dmem_out, dcur_out,
    dp_scr, ds_scr, dq_scr, dk_scr, dv_scr, dpl_scr, total, out_sem, *scratch,
):
    head, heads = pl.program_id(0), pl.num_programs(0)
    place = Place(count)
    units, stores = scatter_dense_units(place, count, (up, down, o), (up_out, down_out, o_out), scratch)
    first, *steps, last = scatter_steps(place, units, stores)
    plan = {at: [] for at in BACKWARD_PLAN}
    plan[BACKWARD_PLAN[0]] = [place.barrier, first]
    for i, step in enumerate(steps):
        plan[BACKWARD_PLAN[min(1 + i * (len(BACKWARD_PLAN) - 1) // len(steps), len(BACKWARD_PLAN) - 1)]].append(step)

    def point(k):
        for (t, at), chosen in plan.items():
            if at == k:
                @pl.when(head == t)
                def _(chosen=chosen):
                    for step in chosen:
                        step()

    rows, keys = cq_ref.shape[0], k_ref.shape[0]
    scale = HD ** (-0.5)
    block = 128
    flip = (
        lax.broadcasted_iota(jnp.int32, (block, block), 0)
        + lax.broadcasted_iota(jnp.int32, (block, block), 1)
        == block - 1
    ).astype(BF)
    point(0)
    dp_scr[...] = mm_nt(do_ref[...], v_ref[...])
    step = 32
    for start in range(0, rows, step):
        here = slice(start, start + step)
        prob = p_ref[0, here].astype(F32)
        dprob = dp_scr[here]
        delta = jnp.sum(prob * dprob, axis=1, keepdims=True)
        ds_scr[here] = (prob * (dprob - delta)).astype(BF)
    point(1)
    side = head % 2
    dv_scr[side] = mm_tn(do_ref[...], p_ref[0]).T.astype(BF)
    dk_scr[side] = mm_tn(cq_ref[...], ds_scr[...]).T.astype(BF)
    dcq = mm(ds_scr[...], k_ref[...]) * scale
    flipped = []
    for start in range(0, rows, block):
        here = slice(start, start + block)
        dp_scr[here] = mm(flip, ds_scr[here])
        flipped.append(mm(flip, pq_ref[here]).astype(BF))
        ds_scr[here] = pltpu.roll(dp_scr[here], rows - block - start, 1, stride=1, stride_axis=0).astype(BF)
    dpl_scr[side] = mm_tn(jnp.concatenate(flipped, axis=0), ds_scr[...]).T.astype(BF)
    dpq_flipped = mm(ds_scr[...], pl_ref[...]) * scale
    dpq = []
    for start in range(0, rows, block):
        piece = dpq_flipped[start : start + block]
        high = piece.astype(BF)
        dpq.append(mm(flip, high) + mm(flip, (piece - high.astype(F32)).astype(BF)))
    dpq = jnp.concatenate(dpq, axis=0)
    dq_scr[side] = (dcq + dpq).astype(BF)
    dcb_ref[...] = jnp.sum(dcq, axis=0, keepdims=True)
    dpb_ref[...] = jnp.sum(dpq, axis=0, keepdims=True)
    point(2)

    @pl.when(side == 1)
    def _():
        dq, dk, dv, dpl = (jnp.concatenate([ref[0], ref[1]], axis=1) for ref in (dq_scr, dk_scr, dv_scr, dpl_scr))
        gk_ref[...] = mm(in_t_ref[...], dk).astype(BF)
        gv_ref[...] = mm(in_t_ref[...], dv).astype(BF)
        gp_ref[...] = mm(table_t_ref[...], dpl).astype(BF)
        gq_ref[...] = mm(in_t_ref[:, 2 * rows :], dq).astype(BF)
        point(3)

        @pl.when(head == 1)
        def _():
            total[...] = jnp.zeros_like(total)

        for start in range(0, keys, rows):
            here = slice(start, start + rows)
            more = mm_nt(dk[here], wk_ref[...]) + mm_nt(dv[here], wv_ref[...])
            if start == 2 * rows:
                more = more + mm_nt(dq, wq_ref[...])
            total[here] += more

    @pl.when(head == heads - 1)
    def _():
        width = total.shape[1]
        own = pltpu.make_async_copy(total.at[pl.ds(2 * rows, rows)], dcur_out, out_sem.at[0])
        own.start()
        for i, out in enumerate((dsq_out, dmem_out)):
            ds_scr[:, :width] = total[i * rows : (i + 1) * rows].astype(BF)
            copy = pltpu.make_async_copy(ds_scr.at[:, pl.ds(0, width)], out, out_sem.at[1 + i])
            copy.start()
            copy.wait()
        own.wait()
        last()


def attend_backward(saved, probs, d_out, inputs_t, table_t, w, dense):
    count = lax.axis_size("seq")
    rows, width = d_out.shape
    keys = inputs_t.shape[1]
    heads = width // HD
    names = ("up", "down", "o")
    shapes = [(dense[n].shape[0] // (2 * count), width) for n in names]

    def whole(shape):
        return pl.BlockSpec(shape, lambda h: (0,) * len(shape), pipeline_mode=pl.Buffered(1))

    def columns(height):
        return pl.BlockSpec((height, HD), lambda h: (0, h))

    pair = pl.BlockSpec((width, 2 * HD), lambda h: (0, h // 2))
    any_spec = pl.BlockSpec(memory_space=pl.ANY)
    vmem = pl.BlockSpec(memory_space=pltpu.VMEM)
    outs = pl.pallas_call(
        functools.partial(attend_backward_kernel, count),
        grid=(heads,),
        in_specs=[columns(rows)] * 2
        + [columns(keys)] * 3
        + [pl.BlockSpec((1, rows, keys), lambda h: (h, 0, 0)), columns(rows), whole((width, keys)), whole((width, keys))]
        + [pair] * 3
        + [any_spec] * 3,
        out_specs=[columns(1)] * 2 + [pair] * 4 + [vmem] * 3 + [any_spec] * 3,
        out_shape=[
            *[jax.ShapeDtypeStruct((1, width), F32)] * 2,
            *[jax.ShapeDtypeStruct((width, width), BF)] * 4,
            *[jax.ShapeDtypeStruct(shape, F32) for shape in shapes],
            *[jax.ShapeDtypeStruct((rows, width), BF)] * 2,
            jax.ShapeDtypeStruct((rows, width), F32),
        ],
        scratch_shapes=[
            pltpu.VMEM((rows, keys), F32),
            pltpu.VMEM((rows, keys), BF),
            pltpu.VMEM((2, rows, HD), BF),
            *[pltpu.VMEM((2, keys, HD), BF)] * 3,
            pltpu.VMEM((keys, width), F32),
            pltpu.SemaphoreType.DMA((3,)),
            *scatter_dense_scratch(count, shapes),
        ],
        compiler_params=pltpu.CompilerParams(collective_id=1, has_side_effects=True, vmem_limit_bytes=62 * MIB),
        name="attend_backward",
    )(*saved, probs, d_out, inputs_t, table_t, w["q"], w["k"], w["v"], *[dense[n] for n in names])
    return outs[:2], outs[2:6], dict(zip(names, outs[6:9])), outs[9:]


def normalize(values):
    centre = values - jnp.mean(values, axis=-1, keepdims=True)
    spread = jnp.mean(centre * centre, axis=-1, keepdims=True)
    scale = lax.rsqrt(spread + epsilon)
    return centre * scale, scale


def normalize_back(grad, gain, unit, scale):
    pulled = grad * gain
    return scale * (
        pulled
        - jnp.mean(pulled, axis=-1, keepdims=True)
        - unit * jnp.mean(pulled * unit, axis=-1, keepdims=True)
    )


def gelu_parts(u):
    root = np.float32(np.sqrt(2.0 / np.pi))
    inner = root * (u + 0.044715 * u * u * u)
    tanh = jnp.tanh(inner)
    value = 0.5 * u * (1.0 + tanh)
    slope = 0.5 * (1.0 + tanh) + 0.5 * u * (1.0 - tanh * tanh) * root * (1.0 + 3 * 0.044715 * u * u)
    return value, slope


def exchange_rows(array, head):
    half = array.shape[0] // 2
    mine = lax.dynamic_slice_in_dim(array, head * half, half, 0)
    theirs = lax.dynamic_slice_in_dim(array, (1 - head) * half, half, 0)
    other = lax.ppermute(theirs, "head", [(0, 1), (1, 0)])
    first = jnp.where(head == 0, mine, other)
    second = jnp.where(head == 0, other, mine)
    return jnp.stack([first, second])[:, None]


def body(
    inputs, lengths,
    query_weight, key_weight, value_weight, position_weight, content_bias, position_bias,
    output_weight, output_bias, first_gain, first_shift, up_weight, up_bias, down_weight, down_bias,
    second_gain, second_shift, squeeze_weight, squeeze_bias, cotangent,
):
    seq = lax.axis_index("seq")
    head = lax.axis_index("head")
    rows, width = inputs.shape[2:]

    x = lax.dynamic_index_in_dim(inputs[:, 0], head, 0, keepdims=False)
    book_lengths = lax.dynamic_index_in_dim(lengths, head, 0, keepdims=False)
    padded_lengths = jnp.concatenate([jnp.zeros((4,), jnp.int32), book_lengths])
    window = lax.dynamic_slice_in_dim(padded_lengths, seq, 5, 0)
    own_length = window[4]

    memory = shifted(x, "seq", 1)
    shards = dict(
            q=query_weight, k=key_weight, v=value_weight, p=position_weight,
            o=output_weight, up=up_weight.T, down=down_weight, sq=squeeze_weight.T,
            cb=content_bias, pb=position_bias, ob=output_bias, g1=first_gain, s1=first_shift, ub=up_bias,
            db=down_bias, g2=second_gain, s2=second_shift, sb=squeeze_bias,
    )
    w = gather_attention(shards)
    cb, pb, ob, g1, s1, ub, db, g2, s2, sb = (
        w[n] for n in ("cb", "pb", "ob", "g1", "s1", "ub", "db", "g2", "s2", "sb")
    )

    pad, taps, collect, biased = squeeze_layout(rows)
    row_ids = jnp.arange(rows)
    kept = (row_ids < own_length)[:, None]
    masked = jnp.where(kept, x, jnp.zeros_like(x))
    made = biased * sb
    for tap in range(3):
        made = made + mm_nt(mm_tn(taps[tap], masked, BF), w["sq"][:, tap * width : (tap + 1) * width])
    made = made.astype(BF)
    arrived = jnp.concatenate(
        [shifted(made[role * pad : (role + 1) * pad], "seq", 4 - role) for role in range(3)], axis=0
    )
    squeezed = mm(collect, arrived, out=BF)
    keys_in = jnp.concatenate([squeezed, memory, x], axis=0)

    flat = np.arange(0, 3 * rows, 3)
    history_ok = jnp.asarray(flat % rows) < window[:3][flat // rows]
    valid = jnp.concatenate([history_ok, row_ids < window[3], row_ids < window[4]])
    key_bias = jnp.where(valid, 0.0, -1e30).astype(F32)[None]

    table = table_rows(width, 3 * rows)
    (attended, probs, *saved), dense = attend_forward(key_bias, cb, pb, keys_in, jnp.asarray(table), w, shards)
    w.update(dense)

    blended = x.astype(F32) + mm(attended, w["o"]) + ob
    unit1, scale1 = normalize(blended)
    normed = (unit1 * g1 + s1).astype(BF)
    u = mm_nt(normed, w["up"]) + ub
    hidden_f, slope = gelu_parts(u)
    hidden = hidden_f.astype(BF)
    unit2, scale2 = normalize(normed.astype(F32) + mm(hidden, w["down"]) + db)
    outputs = (unit2 * g2 + s2).astype(BF)

    grads = {}
    ct = lax.dynamic_index_in_dim(cotangent[:, 0], head, 0, keepdims=False).astype(F32)
    grads["g2"] = jnp.sum(ct * unit2, axis=0)
    grads["s2"] = jnp.sum(ct, axis=0)
    dy = normalize_back(ct, g2, unit2, scale2)
    grads["db"] = jnp.sum(dy, axis=0)
    dy_b = dy.astype(BF)
    grads["down"] = mm_tn(hidden, dy_b, BF)
    du = (mm_nt(dy_b, w["down"]) * slope).astype(BF)
    grads["ub"] = jnp.sum(du.astype(F32), axis=0)
    grads["up"] = mm_tn(du, normed, BF)
    dnormed = dy + mm(du, w["up"])
    grads["g1"] = jnp.sum(dnormed * unit1, axis=0)
    grads["s1"] = jnp.sum(dnormed, axis=0)
    dblended = normalize_back(dnormed, g1, unit1, scale1)
    grads["ob"] = jnp.sum(dblended, axis=0)
    dblended_b = dblended.astype(BF)
    grads["o"] = mm_tn(attended, dblended_b, BF)
    dattended = mm_nt(dblended_b, w["o"], BF)

    (dcb, dpb), squares, final, (dsqueezed, dmemory, dcurrent) = attend_backward(
        saved, probs, dattended, keys_in.T, jnp.asarray(np.ascontiguousarray(table.T)), w, grads
    )
    grads.update(zip(("q", "k", "v", "p"), squares))
    grads["cb"] = dcb[0]
    grads["pb"] = dpb[0]
    grads["sb"] = jnp.sum(dsqueezed.astype(F32), axis=0)
    dmade = mm_tn(collect, dsqueezed, BF)
    returned = jnp.concatenate(
        [shifted(dmade[role * pad : (role + 1) * pad], "seq", role - 4) for role in range(3)], axis=0
    )
    from_next = shifted(dmemory, "seq", -1)
    dx = dblended + dcurrent + from_next.astype(F32)
    dmasked = jnp.zeros((rows, width), F32)
    sq_grads = []
    for tap in range(3):
        spread = mm(taps[tap], returned, out=BF)
        dmasked = dmasked + mm(spread, w["sq"][:, tap * width : (tap + 1) * width])
        sq_grads.append(mm_tn(spread, masked, BF))
    grads["sq"] = jnp.concatenate(sq_grads, axis=1)
    dx = dx + jnp.where(kept, dmasked, 0.0)

    final.update(scatter_attention(grads))
    return (
        exchange_rows(outputs, head),
        exchange_rows(dx.astype(BF), head),
        final["q"], final["k"], final["v"], final["p"], final["cb"], final["pb"],
        final["o"], final["ob"], final["g1"], final["s1"], final["up"].T, final["ub"],
        final["down"], final["db"], final["g2"], final["s2"], final["sq"].T, final["sb"],
    )


def solution(mesh):
    both = ("head", "seq")
    matrix = P("seq", "head")
    in_specs = (
        P(None, "seq", None, None), P(), matrix, matrix, matrix, matrix, P(both), P(both),
        P(both, None), P("seq"), P("seq"), P("seq"), P(None, both), P(both), P(both, None), P("seq"),
        P("seq"), P("seq"), P(None, both), P(both), P(None, "seq", None, None),
    )
    rows = P(None, "seq", "head", None)
    out_specs = (
        rows, rows, matrix, matrix, matrix, matrix, P(both), P(both),
        P(both, None), P(both), P(both), P(both), P(None, both), P(both), P(both, None), P(both),
        P(both), P(both), P(None, both), P(both),
    )
    return jax.shard_map(body, mesh=mesh, in_specs=in_specs, out_specs=out_specs, check_vma=False)
```

```python
import functools

import jax
import jax.numpy as jnp
import numpy as np
from jax import lax
from jax.experimental import pallas as pl
from jax.experimental.pallas import tpu as pltpu
from jax.sharding import PartitionSpec as P

HD = 128
BF = jnp.bfloat16
F32 = jnp.float32
epsilon = 1e-05
MIB = 1024 * 1024


def mm(left, right, contract=((1,), (0,)), out=F32):
    return lax.dot_general(left, right, (contract, ((), ())), preferred_element_type=F32).astype(out)


def mm_nt(left, right, out=F32):
    return mm(left, right, ((1,), (1,)), out)


def mm_tn(left, right, out=F32):
    return mm(left, right, ((0,), (0,)), out)


def table_rows(width, count):
    distance = np.arange(count - 1, -1, -1).astype(np.float32)[:, None]
    exponent = -np.arange(0, width, 2).astype(np.float32) / np.float32(width)
    frequency = np.power(np.float32(10000.0), exponent).astype(np.float32)
    angles = (distance * frequency[None, :]).astype(np.float32)
    return np.concatenate([np.sin(angles), np.cos(angles)], axis=1).astype(BF)


def squeeze_layout(rows):
    pad = -(-(rows // 3 + 2) // 16) * 16
    taps = np.zeros((3, rows, 3 * pad), np.float32)
    collect = np.zeros((rows, 3 * pad), np.float32)
    biased = np.zeros((3 * pad, 1), np.float32)
    for role in range(3):
        first = role * rows // 3
        for i in range(rows):
            flat = role * rows + i
            taps[flat % 3, i, role * pad + flat // 3 - first] = 1.0
            collect[flat // 3, role * pad + flat // 3 - first] = 1.0
        for c in range(first, ((role + 1) * rows - 1) // 3 + 1):
            if role == 0 or 3 * c >= role * rows:
                biased[role * pad + c - first] = 1.0
    return pad, taps.astype(BF), collect.astype(BF), biased


MESH = pl.DeviceIdType.MESH
CORE, XFLIP, YFLIP, UP, DOWN = range(5)


def repeat(count, run):
    def body(i, carry):
        run(i)
        return carry

    lax.fori_loop(0, count, body, 0)


class Place:
    def __init__(self, count):
        self.count = count
        self.n = count // 4
        self.h = lax.axis_index("head")
        self.s = lax.axis_index("seq")
        self.a = self.s // 4
        self.b = (self.s // 2) % 2
        self.c = self.s % 2

    def seq_of(self, a, b, c):
        return a * 4 + b * 2 + c

    def neighbour(self, kind):
        s, h = self.s, self.h
        if kind == CORE:
            return (h, s + 1 - 2 * self.c)
        if kind == XFLIP:
            return (h, s + 2 - 4 * self.b)
        if kind == YFLIP:
            return (1 - h, s)
        return (h, s + 4) if kind == UP else (h, s - 4)

    def when(self, kind):
        if kind == UP:
            return pl.when(self.a < self.n - 1)
        if kind == DOWN:
            return pl.when(self.a > 0)
        return lambda run: run()

    def far(self):
        s, count = self.s, self.count
        for by, other in ((1, self.c == 1), (-1, self.c == 0), (2, self.b == 1), (-2, self.b == 0), (3, None), (-3, None)):
            inside = self.inside(by)
            yield by, inside if other is None else jnp.logical_and(inside, other)

    def inside(self, by):
        return self.s + by < self.count if by > 0 else self.s + by >= 0

    def barrier(self, shifts=False):
        barrier = pltpu.get_barrier_semaphore()
        for kind in range(5):
            @self.when(kind)
            def _(kind=kind):
                pl.semaphore_signal(barrier, inc=1, device_id=self.neighbour(kind), device_id_type=MESH)
        peers = 5 - jnp.where(self.a == 0, 1, 0) - jnp.where(self.a == self.n - 1, 1, 0)
        if shifts:
            for by, there in self.far():
                @pl.when(there)
                def _(by=by):
                    pl.semaphore_signal(barrier, inc=1, device_id=(self.h, self.s + by), device_id_type=MESH)
                peers = peers + jnp.where(there, 1, 0)
        pl.semaphore_wait(barrier, peers)

    def along(self, i):
        return (self.a + self.n // 2 + i) % self.n


class Gather:
    def __init__(self, place, units, local_sem, send_sem, recv_sem):
        self.place, self.units = place, units
        self.local_sem, self.send_sem, self.recv_sem = local_sem, send_sem, recv_sem

    def view(self, u, h, s):
        shard, full, view, order = self.units[u]
        return view(full, h, s)

    def copy(self, u, kind, h, s, own=False):
        n = self.place.n
        a, b = s // 4, (s // 2) % 2
        order = self.units[u][3]
        other = b if order.index("x") < order.index("z") else h
        sent = {
            UP: other * n + a,
            DOWN: (2 + other) * n + a,
            XFLIP: (4 + h) * n + a,
            YFLIP: (6 + b) * n + a,
            CORE: (8 + h * 2 + b) * n + a,
        }[kind]
        there = self.view(u, h, s)
        return pltpu.make_async_remote_copy(
            src_ref=self.units[u][0] if own else there,
            dst_ref=there,
            send_sem=self.send_sem.at[u, sent],
            recv_sem=self.recv_sem.at[u, h * self.place.count + s],
            device_id=self.place.neighbour(kind),
            device_id_type=MESH,
        )

    def local(self, u):
        return pltpu.make_async_copy(self.units[u][0], self.view(u, self.place.h, self.place.s), self.local_sem.at[u])

    def sources(self):
        found = []
        for t in range(self.place.n):
            for sign in ((1, -1) if t else (0,)):
                for x in (0, 1):
                    for y in (0, 1):
                        if t or x or y:
                            found.append((t, sign, x, y))
        return sorted(found, key=lambda e: e[0] + e[2] + e[3])

    def onward(self, u, sign, x, y):
        order = self.units[u][3]
        moved = {"x": x, "y": y, "z": sign}
        last = max([i for i in range(3) if moved[order[i]]], default=-1)
        kinds = []
        if last >= 0 and order[last] == "z":
            kinds.append(UP if sign > 0 else DOWN)
        for dim in order[last + 1 :]:
            kinds += {"x": [XFLIP], "y": [YFLIP], "z": [UP, DOWN]}[dim]
        return kinds + [CORE]

    def send(self, u, kind, h, s, own, wait):
        @self.place.when(kind)
        def _():
            copy = self.copy(u, kind, h, s, own)
            if wait:
                copy.wait_send()
            else:
                copy.start()

    def begin(self, wait=False):
        p = self.place
        for u in range(len(self.units)):
            for kind in self.onward(u, 0, 0, 0):
                self.send(u, kind, p.h, p.s, True, wait)
        if not wait:
            for u in range(len(self.units)):
                self.local(u).start()

    def pass_on(self, entry, wait=False):
        p = self.place
        t, sign, x, y = entry
        a = p.a - sign * t
        h = 1 - p.h if y else p.h
        s = p.seq_of(a, 1 - p.b if x else p.b, p.c)

        def run():
            for u in range(len(self.units)):
                if not wait:
                    self.copy(u, CORE, h, s).wait_recv()
                for kind in self.onward(u, sign, x, y):
                    self.send(u, kind, h, s, False, wait)

        if t:
            pl.when(jnp.logical_and(a >= 0, a <= p.n - 1))(run)
        else:
            run()

    def arrived(self):
        p = self.place

        def core(i):
            h, a, b = i // (2 * p.n), i // 2 % p.n, i % 2
            for u in range(len(self.units)):
                self.copy(u, CORE, h, p.seq_of(a, b, 1 - p.c)).wait_recv()

        repeat(4 * p.n, core)
        for u in range(len(self.units)):
            self.local(u).wait()

    def sent(self):
        self.begin(True)
        for entry in self.sources():
            self.pass_on(entry, True)

    def finish(self):
        self.arrived()
        self.sent()

    def steps(self):
        return [self.begin] + [functools.partial(self.pass_on, entry) for entry in self.sources()] + [self.finish]


GATHER_ORDERS = ("yzx", "xzy", "zxy", "zyx")


def halves(rows):
    return [(0, rows // 2), (rows // 2, rows // 2)] if rows % 32 == 0 else [(0, rows)]


def block_units(shard, full, count, first):
    rows = shard.shape[0]
    units = []
    for i, (at, size) in enumerate(halves(rows)):
        def view(ref, h, s, at=at, size=size):
            return ref.at[pl.ds(pl.multiple_of((h * count + s) * rows + at, size), size)]

        units.append((shard.at[pl.ds(at, size)], full, view, GATHER_ORDERS[(first + i) % 4]))
    return units


def square_unit(shard, full, order):
    r, w = shard.shape

    def view(ref, h, s):
        return ref.at[pl.ds(pl.multiple_of(s * r, r), r), pl.ds(pl.multiple_of(h * w, w), w)]

    return (shard, full, view, order)


def open_kernel(
    count, small_names, q, k, v, p, sq, small, x, masked, taps_t, collect, biased,
    q_f, k_f, v_f, p_f, sq_f, vec, vec_up, squeezed, memory,
    small_f, taps_scr, masked_scr, sq_scr, grouped, made, made_low, arriving, load_sem, row_send, row_recv, *sems,
):
    place = Place(count)
    place.barrier(True)
    rows, width = masked_scr.shape
    pad = made.shape[0] // 3

    def small_view(ref, h, s):
        return ref.at[pl.ds(pl.multiple_of((h * count + s) * 8, 8), 8)]

    early = Gather(place, block_units(sq, sq_f, count, 0) + [(small, small_f, small_view, "zxy")], *sems[:3])
    late = Gather(
        place, [square_unit(*pair, GATHER_ORDERS[i]) for i, pair in enumerate(((q, q_f), (k, k_f), (v, v_f), (p, p_f)))], *sems[3:]
    )

    def rows_copy(i):
        by = 4 - i if i < 3 else 1
        here = pl.ds(i * pad, pad)
        return pltpu.make_async_remote_copy(
            src_ref=made_low.at[here] if i < 3 else x,
            dst_ref=arriving.at[here] if i < 3 else memory,
            send_sem=row_send.at[i],
            recv_sem=row_recv.at[i],
            device_id=(place.h, place.s + by),
            device_id_type=MESH,
        )

    def send_rows(i, wait=False):
        @pl.when(place.inside(4 - i if i < 3 else 1))
        def _():
            if wait:
                rows_copy(i).wait_send()
            else:
                rows_copy(i).start()

    def take_rows(i):
        @pl.when(place.inside(i - 4 if i < 3 else -1))
        def _():
            rows_copy(i).wait_recv()

    loads = [
        pltpu.make_async_copy(source, target, load_sem.at[i])
        for i, (source, target) in enumerate(((taps_t, taps_scr), (masked, masked_scr), (sq_f, sq_scr)))
    ]
    early.begin()
    loads[0].start()
    loads[1].start()
    send_rows(3)
    late.begin()

    @pl.when(place.s == 0)
    def _():
        made_low[...] = jnp.zeros_like(made_low)
        blank = pltpu.make_async_copy(made_low.at[pl.ds(0, rows)], memory, load_sem.at[3])
        blank.start()
        blank.wait()

    for i in range(3):
        @pl.when(jnp.logical_not(place.inside(i - 4)))
        def _(i=i):
            arriving[i * pad : (i + 1) * pad] = jnp.zeros((pad, width), BF)

    entries = early.sources()

    def passed(gather, depth):
        for entry in entries:
            if entry[0] + entry[2] + entry[3] == depth:
                gather.pass_on(entry)

    deepest = place.n + 1
    loads[0].wait()
    loads[1].wait()
    passed(early, 1)
    for tap in range(3):
        grouped[tap] = mm(taps_scr[tap], masked_scr[...]).astype(BF)
    for depth in range(2, deepest + 1):
        passed(early, depth)
        if depth > 2:
            passed(late, depth - 2)
    early.arrived()
    loads[2].start()
    for slot in range(2 * count):
        for name, row, at, size, target in small_names:
            if size * 2 * count > vec.shape[1] * (4 if name == "ub" else 1) and slot >= count:
                continue
            ref = vec_up if name == "ub" else vec
            ref[target : target + 1, slot * size : (slot + 1) * size] = small_f[slot * 8 + row : slot * 8 + row + 1, at : at + size]
    loads[2].wait()
    made[...] = mm_nt(grouped[0], sq_scr[:, :width]) + biased[...] * vec[2:3]
    passed(late, deepest - 1)
    made[...] += mm_nt(grouped[1], sq_scr[:, width : 2 * width])
    passed(late, deepest)
    made_low[...] = (made[...] + mm_nt(grouped[2], sq_scr[:, 2 * width :])).astype(BF)
    for i in range(3):
        send_rows(i)
    late.arrived()
    for i in range(4):
        take_rows(i)
    squeezed[...] = mm(collect[...], arriving[...]).astype(BF)
    for i in range(4):
        send_rows(i, True)
    early.sent()
    late.sent()


def gather_semaphores(count, units):
    return [
        pltpu.SemaphoreType.DMA((units,)),
        pltpu.SemaphoreType.DMA((units, 12 * (count // 4))),
        pltpu.SemaphoreType.DMA((units, 2 * count)),
    ]


def small_layout(both, seq):
    names = []
    for i, name in enumerate(("cb", "pb", "sb")):
        names.append((name, 0, i * both, both, i))
    names.append(("ub", 1, 0, 4 * both, 0))
    for i, name in enumerate(("ob", "g1", "s1", "db", "g2", "s2")):
        names.append((name, 2 + i // 2, (i % 2) * seq, seq, 3 + i))
    return names


def open_layer(w, x, masked, layout):
    pad, taps, collect, biased = layout
    count = lax.axis_size("seq")
    both, seq = w["cb"].shape[0], w["ob"].shape[0]
    rows, width = x.shape
    layout = small_layout(both, seq)
    lines = [[] for _ in range(8)]
    for name, row, at, size, target in layout:
        lines[row].append(w[name].astype(F32))
    lines = [jnp.concatenate(parts) if parts else jnp.zeros((128,), F32) for parts in lines]
    small = jnp.stack([jnp.pad(line, (0, 128 - line.shape[0])) for line in lines])
    names = ("q", "k", "v", "p", "sq")
    tall = w["sq"].shape[1]
    any_spec = pl.BlockSpec(memory_space=pl.ANY)
    vmem_spec = pl.BlockSpec(memory_space=pltpu.VMEM)
    outs = pl.pallas_call(
        functools.partial(open_kernel, count, layout),
        in_specs=[any_spec] * 9 + [vmem_spec] * 2,
        out_specs=[any_spec] * 5 + [vmem_spec] * 3 + [any_spec],
        out_shape=[
            *[jax.ShapeDtypeStruct((width, width), BF) for _ in range(4)],
            jax.ShapeDtypeStruct((width, tall), BF),
            jax.ShapeDtypeStruct((16, width), F32),
            jax.ShapeDtypeStruct((1, 4 * width), F32),
            jax.ShapeDtypeStruct((rows, width), BF),
            jax.ShapeDtypeStruct((rows, width), BF),
        ],
        scratch_shapes=[
            pltpu.VMEM((8 * 2 * count, 128), F32),
            pltpu.VMEM((3, 3 * pad, rows), BF),
            pltpu.VMEM((rows, width), BF),
            pltpu.VMEM((width, tall), BF),
            pltpu.VMEM((3, 3 * pad, width), BF),
            pltpu.VMEM((3 * pad, width), F32),
            pltpu.VMEM((3 * pad, width), BF),
            pltpu.VMEM((3 * pad, width), BF),
            pltpu.SemaphoreType.DMA((4,)),
            pltpu.SemaphoreType.DMA((4,)),
            pltpu.SemaphoreType.DMA((4,)),
            *gather_semaphores(count, 1 + len(halves(w["sq"].shape[0]))),
            *gather_semaphores(count, 4),
        ],
        compiler_params=pltpu.CompilerParams(collective_id=0, has_side_effects=True, vmem_limit_bytes=48 * MIB),
        name="open_layer",
    )(*[w[n] for n in names], small, x, masked, jnp.asarray(np.ascontiguousarray(taps.transpose(0, 2, 1))), jnp.asarray(collect), jnp.asarray(biased))
    full = dict(zip(names, outs), vec=outs[5], ub=outs[6])
    return full, outs[7], outs[8]


class Scatter:
    def __init__(self, place, view, order, sums, own, first, second, line, local_sem, send_sem, recv_sem):
        self.place, self.view = place, view
        self.by_y = order[0] == "y"
        self.late = order[2] == "z"
        self.sums, self.own, self.first, self.second, self.line = sums, own, first, second, line
        self.local_sem, self.send_sem, self.recv_sem = local_sem, send_sem, recv_sem
        self.f, self.g = (place.h, place.b) if self.by_y else (place.b, place.h)
        self.flips = (YFLIP, XFLIP) if self.by_y else (XFLIP, YFLIP)

    def index(self, f, g, a):
        return (f * 2 + g) * self.place.n + a

    def slot(self, f, g, a, c):
        h, b = (f, g) if self.by_y else (g, f)
        return h, self.place.seq_of(a, b, c)

    def remote(self, source, target, kind, send_at, recv_at):
        return pltpu.make_async_remote_copy(
            src_ref=source,
            dst_ref=target,
            send_sem=self.send_sem.at[send_at],
            recv_sem=self.recv_sem.at[recv_at],
            device_id=self.place.neighbour(kind),
            device_id_type=MESH,
        )

    def core_copy(self, i):
        return self.remote(self.sums.at[i], self.sums.at[i], CORE, i, i)

    def first_copy(self, g, a):
        n = self.place.n
        to = g * n + a
        return self.remote(self.sums.at[self.index(1 - self.f, g, a)], self.first.at[to], self.flips[0], 4 * n + to, 4 * n + to)

    def second_copy(self, a):
        n = self.place.n
        to = a if self.late else 0
        return self.remote(self.sums.at[self.index(self.f, 1 - self.g, a)], self.second.at[to], self.flips[1], 6 * n + to, 6 * n + to)

    def line_at(self, g, at):
        return at if self.late else g * (self.place.n + 1) + at

    def line_copy(self, kind, g, a):
        n = self.place.n
        to = self.line_at(g, a if kind == UP else jnp.where(a == self.place.a - 1, n, a))
        sent = 7 * n + (a if self.late else g * n + a)
        return self.remote(self.sums.at[self.index(self.f, g, a)], self.line.at[to], kind, sent, 7 * n + to)

    def line_wait(self, at):
        n = self.place.n
        self.remote(self.line.at[at], self.line.at[at], CORE, 7 * n, 7 * n + at).wait_recv()

    def piece(self, part, i):
        return (self.f if part >= 2 else 1 - self.f, self.g if part % 2 else 1 - self.g, self.place.along(i))

    def trade(self, part, i):
        f, g, a = self.piece(part, i)
        at = self.index(f, g, a)
        source = self.view(*self.slot(f, g, a, 1 - self.place.c))
        self.remote(source, self.sums.at[at], CORE, at, at).start()

    def load(self, part, i):
        source = self.view(*self.slot(*self.piece(part, i), self.place.c))
        return pltpu.make_async_copy(source, self.own.at[i % 4], self.local_sem.at[i % 4])

    def absorb(self, part, i):
        n = self.place.n
        f, g, a = self.piece(part, i)
        at = self.index(f, g, a)
        self.load(part, i).wait()
        self.core_copy(at).wait_recv()
        self.add(at, [(self.own, i % 4)])

        @pl.when(i + 4 < n)
        def _():
            self.load(part, i + 4).start()

        if part < 3:
            @pl.when(i + 4 >= n)
            def _():
                self.load(part + 1, i + 4 - n).start()

        if part < 2:
            self.first_copy(g, a).start()

    def after_first(self, g, a):
        self.first_copy(g, a).wait_recv()
        return self.index(self.f, g, a), [(self.first, g * self.place.n + a)]

    def add(self, i, refs):
        total = self.sums[i].astype(F32)
        for ref, at in refs:
            total = total + ref[at].astype(F32)
        self.sums[i] = total.astype(BF)

    def add_line(self, i, g):
        p = self.place
        for fed, at in ((p.a > 0, p.a), (p.a < p.n - 1, p.n)):
            @pl.when(fed)
            def _(at=self.line_at(g, at)):
                self.line_wait(at)
                self.add(i, [(self.line, at)])

    def flip_second(self, a):
        i, refs = self.after_first(1 - self.g, a)
        self.add(i, refs)
        if not self.late:
            self.add_line(i, 1 - self.g)
        self.second_copy(a).start()

    def move(self, g, d):
        p = self.place
        for kind, a, inside, fed in (
            (UP, p.a + d, p.a + d <= p.n - 1, p.a > 0),
            (DOWN, p.a - d, p.a - d >= 0, p.a < p.n - 1),
        ):
            @pl.when(inside)
            def _(kind=kind, a=a, fed=fed):
                i, refs = self.after_first(g, a)
                if self.late:
                    self.second_copy(a).wait_recv()
                    refs.append((self.second, a))
                self.add(i, refs)

                @pl.when(fed)
                def _():
                    at = self.line_at(g, a)
                    self.line_wait(at)
                    self.add(i, [(self.line, at)])

                self.line_copy(kind, g, a).start()

    def finish(self, store):
        p = self.place
        n = p.n
        i, refs = self.after_first(self.g, p.a)
        to = p.a if self.late else 0
        self.second_copy(p.a).wait_recv()
        self.add(i, refs + [(self.second, to)])
        self.add_line(i, self.g)
        store(self.sums[i].astype(F32))
        repeat(4 * n, lambda i: self.core_copy(i).wait_send())
        repeat(2 * n, lambda i: self.first_copy(i // n, i % n).wait_send())
        if self.late:
            repeat(n, lambda a: self.second_copy(a).wait_send())
        else:
            self.second_copy(p.a).wait_send()

        def line_done(a):
            for kind, inside in ((UP, a > p.a), (DOWN, a < p.a)):
                @pl.when(inside)
                def _(kind=kind):
                    for g in (self.g,) if self.late else (0, 1):
                        self.line_copy(kind, g, a).wait_send()

        repeat(n, line_done)


def scatter_scratch(count, shape, order):
    n = count // 4
    late = order[2] == "z"
    lines = n + 1 if late else 2 * n + 2
    return [
        *[pltpu.VMEM((k, *shape), BF) for k in (4 * n, 4, 2 * n, n if late else 1, lines)],
        pltpu.SemaphoreType.DMA((4,)),
        pltpu.SemaphoreType.DMA((9 * n,)),
        pltpu.SemaphoreType.DMA((7 * n + lines,)),
    ]


SCATTER_ORDERS = ("yzx", "xzy", "yxz", "xyz")


def block_scatters(rows, first):
    return [(at, size, SCATTER_ORDERS[(first + i) % 4]) for i, (at, size) in enumerate(halves(rows))]


def block_pairs(ref, rows, at, size, count):
    def view(h, s):
        return ref.at[pl.ds(pl.multiple_of((h * count + s) * rows + at, size), size)]

    return view


def square_pairs(ref, r, w):
    def view(h, s):
        return ref.at[pl.ds(pl.multiple_of(s * r, r), r), pl.ds(pl.multiple_of(h * w, w), w)]

    return view


def scatter_steps(place, units, stores, between=lambda at: None):
    n = place.n
    middle = [u for u in units if not u.late]
    late = [u for u in units if u.late]

    def each(run, some=units):
        def one(i):
            for unit in some:
                run(unit, i)

        return one

    def begin():
        for part in range(4):
            repeat(n, each(lambda u, i, part=part: u.trade(part, i)))
            if part == 0:
                repeat(4, each(lambda u, i: u.load(0, i).start()))
        between(0)

    def absorb(part):
        repeat(n, each(lambda u, i: u.absorb(part, i), middle + late))

    def second(d):
        for u in middle:
            u.move(1 - u.g, d)
        for u in late:
            u.flip_second(place.along(n - 1 - d))

    def third(d):
        for u in middle:
            u.move(u.g, d)

    def fourth():
        between(1)
        for u in late:
            u.flip_second(place.along(n - 1))
        for u in middle:
            u.flip_second(place.a)
        between(2)

    def fifth(d):
        for u in late:
            u.move(u.g, d)

    def finish():
        between(3)
        for unit, store in zip(units, stores):
            unit.finish(store)
        between(4)

    far = range(n - 1, 0, -1)
    return (
        [begin]
        + [functools.partial(absorb, part) for part in range(4)]
        + [functools.partial(second, d) for d in far]
        + [functools.partial(third, d) for d in far]
        + [fourth]
        + [functools.partial(fifth, d) for d in far]
        + [finish]
    )


def store_into(out):
    def store(value):
        out[...] = value

    return store


def scatter_dense_units(place, count, grads, outs, scratch):
    units, stores = [], []
    for ref, out, first in zip(grads, outs, (0, 2, 1)):
        rows = out.shape[0]
        for at, size, order in block_scatters(rows, first):
            units.append(Scatter(place, block_pairs(ref, rows, at, size, count), order, *scratch[:8]))
            stores.append(store_into(out.at[pl.ds(at, size)]))
            scratch = scratch[8:]
    return units, stores


def scatter_dense_scratch(count, shapes):
    scratch = []
    for (rows, width), first in zip(shapes, (0, 2, 1)):
        for at, size, order in block_scatters(rows, first):
            scratch += scatter_scratch(count, (size, width), order)
    return scratch


def close_kernel(
    count, gq, gk, gv, gp, sqw, dcb, dpb, vec, dub, dsq, dmem, dcur, dbl, masked, kept, taps, collect_t, outputs,
    q_out, k_out, v_out, p_out, sq_out, vec_out, ub_out, dx_out, rows_out,
    sums, parts, vec_send, vec_recv, dmade, returned, from_next, gsq, sq_scr, dcur_scr, dbl_scr, masked_scr, taps_scr,
    spread, dmasked, load_sem, row_send, row_recv, out_sem, out_send, out_recv, *scratch,
):
    place = Place(count)
    place.barrier(True)
    r, w = q_out.shape
    rows, width = dsq.shape
    half = rows // 2
    pad = dmade.shape[0] // 3
    units, stores = [], []
    for ref, out, order in zip((gq, gk, gv, gp), (q_out, k_out, v_out, p_out), SCATTER_ORDERS):
        units.append(Scatter(place, square_pairs(ref, r, w), order, *scratch[:8]))
        stores.append(store_into(out))
        scratch = scratch[8:]
    low_units, low_stores = [], []
    wide = sq_out.shape[0]
    for at, size, order in block_scatters(wide, 0):
        low_units.append(Scatter(place, block_pairs(gsq, wide, at, size, count), order, *scratch[:8]))
        low_stores.append(store_into(sq_out.at[pl.ds(at, size)]))
        scratch = scratch[8:]

    loads = [
        pltpu.make_async_copy(source, target, load_sem.at[i])
        for i, (source, target) in enumerate(
            ((taps, taps_scr), (masked, masked_scr), (sqw, sq_scr), (dcur, dcur_scr), (dbl, dbl_scr))
        )
    ]

    def rows_copy(i):
        by = i - 4 if i < 3 else -1
        here = pl.ds(i * pad, pad)
        return pltpu.make_async_remote_copy(
            src_ref=dmade.at[here] if i < 3 else dmem,
            dst_ref=returned.at[here] if i < 3 else from_next,
            send_sem=row_send.at[i],
            recv_sem=row_recv.at[i],
            device_id=(place.h, place.s + by),
            device_id_type=MESH,
        )

    def exchange(i, source, target, wait=False):
        own = pltpu.make_async_copy(source.at[pl.ds(pl.multiple_of(place.h * half, half), half)], target.at[place.h], out_sem.at[i])
        other = pltpu.make_async_remote_copy(
            src_ref=source.at[pl.ds(pl.multiple_of((1 - place.h) * half, half), half)],
            dst_ref=target.at[place.h],
            send_sem=out_send.at[i],
            recv_sem=out_recv.at[i],
            device_id=place.neighbour(YFLIP),
            device_id_type=MESH,
        )
        if wait:
            own.wait()
            other.wait()
        else:
            other.start()
            own.start()

    def vec_copy(kind):
        return pltpu.make_async_remote_copy(
            src_ref=sums.at[kind],
            dst_ref=parts.at[kind],
            send_sem=vec_send.at[kind],
            recv_sem=vec_recv.at[kind],
            device_id=place.neighbour(kind),
            device_id_type=MESH,
        )

    def between(at):
        kinds = (CORE, XFLIP, YFLIP)
        if at == 0:
            sums[CORE, 0:16] = vec[...]
            sums[CORE, 0:1] = dcb[...]
            sums[CORE, 1:2] = dpb[...]
            sums[CORE, 2:3] = jnp.sum(dsq[...].astype(F32), axis=0, keepdims=True)
            for i in range(4):
                sums[CORE, 12 + i : 13 + i] = dub[:, i * width : (i + 1) * width]
            vec_copy(CORE).start()
        elif at < 3:
            vec_copy(kinds[at - 1]).wait_recv()
            sums[kinds[at]] = sums[kinds[at - 1]] + parts[kinds[at - 1]]
            vec_copy(kinds[at]).start()
        elif at == 3:
            vec_copy(YFLIP).wait_recv()
            total = sums[YFLIP] + parts[YFLIP]
            ends = (place.a > 0, place.a < place.n - 1)
            sums[UP] = total
            sums[DOWN] = total
            for kind, fed in ((UP, ends[0]), (DOWN, ends[1])):
                @pl.when(fed)
                def _(kind=kind):
                    vec_copy(kind).wait_recv()
                    sums[kind] = sums[kind] + parts[kind]

                @place.when(kind)
                def _(kind=kind):
                    vec_copy(kind).start()
        else:
            total = sums[UP] + sums[DOWN] - (sums[YFLIP] + parts[YFLIP])
            both = vec_out.shape[1]
            k = place.h * count + place.s
            mine = pltpu.roll(total, lax.rem(width - k * both, width), 1)
            vec_out[...] = mine[:, :both]
            wide = ub_out.shape[1]
            flat = k * wide
            lanes = lax.rem(flat, width)
            mine = pltpu.roll(total, lax.rem(width - lanes, width), 1)[:, :wide]
            row = lax.broadcasted_iota(jnp.int32, mine.shape, 0)
            ub_out[...] = jnp.sum(jnp.where(row == 12 + flat // width, mine, 0.0), axis=0, keepdims=True)
            for kind in range(5):
                @place.when(kind)
                def _(kind=kind):
                    vec_copy(kind).wait_send()

    main = scatter_steps(place, units, stores, between)
    low = scatter_steps(place, low_units, low_stores)
    far = place.n - 1

    for load in loads:
        load.start()
    dmade[...] = mm(collect_t[...], dsq[...]).astype(BF)
    for i in range(4):
        by = i - 4 if i < 3 else -1

        @pl.when(place.inside(by))
        def _(i=i):
            rows_copy(i).start()

        @pl.when(jnp.logical_not(place.inside(-by)))
        def _(i=i):
            if i < 3:
                returned[i * pad : (i + 1) * pad] = jnp.zeros((pad, width), BF)
            else:
                from_next[...] = jnp.zeros_like(from_next)

    exchange(0, outputs, rows_out)
    for step in main[:5]:
        step()
    for i in range(4):
        @pl.when(place.inside(4 - i if i < 3 else 1))
        def _(i=i):
            rows_copy(i).wait_recv()
    for load in loads:
        load.wait()

    def compressed(tap):
        cols = slice(tap * width, (tap + 1) * width)
        spread[...] = mm(taps_scr[tap], returned[...]).astype(BF)
        more = mm(spread[...], sq_scr[:, cols])
        if tap:
            more = more + dmasked[...]
        dmasked[...] = more
        gsq[:, cols] = mm_tn(spread[...], masked_scr[...]).astype(BF)

    compressed(0)
    compressed(1)
    for step in main[5 : 5 + far]:
        step()
    compressed(2)
    low[0]()
    spread[...] = (dbl_scr[...] + dcur_scr[...] + from_next[...].astype(F32) + kept[...] * dmasked[...]).astype(BF)
    exchange(1, spread, dx_out)
    for step in low[1:5]:
        step()
    for step in main[5 + far : 5 + 2 * far + 1]:
        step()
    for step in low[5 : 5 + far]:
        step()
    for step in main[6 + 2 * far : 6 + 3 * far]:
        step()
    for step in low[5 + far : 6 + 3 * far]:
        step()
    main[-1]()
    low[-1]()
    for i in range(4):
        @pl.when(place.inside(i - 4 if i < 3 else -1))
        def _(i=i):
            rows_copy(i).wait_send()
    exchange(0, outputs, rows_out, True)
    exchange(1, spread, dx_out, True)


def close_layer(g, w, layout, dsq, dmem, dcur, dbl, masked, kept, outputs):
    pad, taps, collect, biased = layout
    count = lax.axis_size("seq")
    rows, width = dsq.shape
    both = width // (2 * count)
    square = (width // count, width // 2)
    tall = w["sq"].shape[1]
    scratch = []
    for order in SCATTER_ORDERS:
        scratch += scatter_scratch(count, square, order)
    for at, size, order in block_scatters(both, 0):
        scratch += scatter_scratch(count, (size, tall), order)
    vmem = pl.BlockSpec(memory_space=pltpu.VMEM)
    any_spec = pl.BlockSpec(memory_space=pl.ANY)
    outs = pl.pallas_call(
        functools.partial(close_kernel, count),
        in_specs=[any_spec] * 5 + [vmem] * 5 + [any_spec] * 4 + [vmem] + [any_spec] + [vmem] + [any_spec],
        out_specs=[vmem] * 7 + [any_spec] * 2,
        out_shape=[jax.ShapeDtypeStruct(square, F32)] * 4
        + [jax.ShapeDtypeStruct(s, F32) for s in ((both, tall), (16, both), (1, 4 * both))]
        + [jax.ShapeDtypeStruct((2, rows // 2, width), BF)] * 2,
        scratch_shapes=[
            pltpu.VMEM((5, 16, width), F32),
            pltpu.VMEM((5, 16, width), F32),
            pltpu.SemaphoreType.DMA((5,)),
            pltpu.SemaphoreType.DMA((5,)),
            pltpu.VMEM((3 * pad, width), BF),
            pltpu.VMEM((3 * pad, width), BF),
            pltpu.VMEM((rows, width), BF),
            pltpu.VMEM((width, tall), BF),
            pltpu.VMEM((width, tall), BF),
            pltpu.VMEM((rows, width), F32),
            pltpu.VMEM((rows, width), F32),
            pltpu.VMEM((rows, width), BF),
            pltpu.VMEM((3, rows, 3 * pad), BF),
            pltpu.VMEM((rows, width), BF),
            pltpu.VMEM((rows, width), F32),
            pltpu.SemaphoreType.DMA((5,)),
            *[pltpu.SemaphoreType.DMA((4,))] * 2,
            *[pltpu.SemaphoreType.DMA((2,))] * 3,
            *scratch,
        ],
        compiler_params=pltpu.CompilerParams(collective_id=2, has_side_effects=True, vmem_limit_bytes=60 * MIB),
        name="close_layer",
    )(
        g["q"], g["k"], g["v"], g["p"], w["sq"], g["cb"], g["pb"], g["sums"], g["ub"],
        dsq, dmem, dcur, dbl, masked, kept, jnp.asarray(taps), jnp.asarray(np.ascontiguousarray(collect.T)), outputs,
    )
    final = dict(zip(("q", "k", "v", "p", "sq"), outs[:5]))
    final.update({n: outs[5][i] for i, n in enumerate(VECTORS)})
    final["ub"] = outs[6].reshape(4 * both)
    return final, outs[7], outs[8]


def spread_steps(steps, points):
    out = [[] for _ in range(points)]
    for i, step in enumerate(steps):
        out[i * points // len(steps)].append(step)
    return out


def attend_forward_kernel(
    count, bias_ref, vec_ref, in0_ref, in1_ref, in2_ref, table_ref, wq_ref, wk_ref, wv_ref, wp_ref, up, down, o,
    out_ref, p_ref, cq_ref, pq_ref, k_ref, v_ref, pl_ref, in_t_ref, up_f, down_f, o_f,
    s_scr, x_scr, *sems,
):
    turn, turns = pl.program_id(0), pl.num_programs(0)
    place = Place(count)
    units = []
    for shard, full, first in ((up, up_f, 0), (down, down_f, 2), (o, o_f, 1)):
        units += block_units(shard, full, count, first)
    gather = Gather(place, units, *sems)
    first, *steps, last = gather.steps()
    heads = cq_ref.shape[1] // HD
    points = 2 + heads
    plan = spread_steps(steps, turns * points - 1)

    def point(k):
        for t in range(turns):
            chosen = plan[t * points + k - 1] if t or k else [place.barrier, first]
            if chosen:
                @pl.when(turn == t)
                def _(chosen=chosen):
                    for step in chosen:
                        step()

    rows, keys = cq_ref.shape[0], k_ref.shape[0]
    scale = HD ** (-0.5)
    point(0)
    sources = (in0_ref, in1_ref, in2_ref)
    query = mm(in2_ref[...], wq_ref[...])
    cq_ref[...] = ((query + vec_ref[0:1]) * scale).astype(BF)
    pq_ref[...] = ((query + vec_ref[1:2]) * scale).astype(BF)
    for i, source in enumerate(sources):
        k_ref[i * rows : (i + 1) * rows] = mm(source[...], wk_ref[...]).astype(BF)
    point(1)
    for i, source in enumerate(sources):
        v_ref[i * rows : (i + 1) * rows] = mm(source[...], wv_ref[...]).astype(BF)
        here = slice(i * rows, (i + 1) * rows)
        pl_ref[here] = mm(table_ref[here], wp_ref[...]).astype(BF)

        @pl.when(turn == i)
        def _(source=source, here=here):
            in_t_ref[:, here] = source[...].T
    step = 32
    for head in range(heads):
        point(2 + head)
        cols = slice(head * HD, (head + 1) * HD)
        s_scr[...] = mm_nt(cq_ref[:, cols], k_ref[:, cols])
        x_scr[...] = mm_nt(pq_ref[:, cols], pl_ref[:, cols])
        for start in range(0, rows, step):
            here = slice(start, start + step)
            located = pltpu.roll(x_scr[here], (start + keys - rows + 1) % keys, 1, stride=1, stride_axis=0)
            scores = s_scr[here] + located + bias_ref[...]
            early, own = scores[:, : 2 * rows], scores[:, 2 * rows :]
            row = start + lax.broadcasted_iota(jnp.int32, own.shape, 0)
            col = lax.broadcasted_iota(jnp.int32, own.shape, 1)
            own = jnp.where(col <= row, own, -1e30)
            top = jnp.maximum(jnp.max(early, axis=1, keepdims=True), jnp.max(own, axis=1, keepdims=True))
            early, own = jnp.exp(early - top), jnp.exp(own - top)
            total = jnp.sum(early, axis=1, keepdims=True) + jnp.sum(own, axis=1, keepdims=True)
            share = 1.0 / total
            p_ref[head, here, : 2 * rows] = (early * share).astype(BF)
            p_ref[head, here, 2 * rows :] = (own * share).astype(BF)
        out_ref[:, cols] = mm(p_ref[head], v_ref[:, cols]).astype(BF)

    @pl.when(turn == turns - 1)
    def _():
        last()


def attend_forward(key_bias, squeezed, memory, x, table, w, shards):
    count = lax.axis_size("seq")
    rows, width = x.shape
    keys = 3 * rows
    pair = 2 * HD
    names = ("up", "down", "o")

    def whole(shape):
        return pl.BlockSpec(shape, lambda t: (0,) * len(shape), pipeline_mode=pl.Buffered(1))

    def columns(height):
        return pl.BlockSpec((height, pair), lambda t: (0, t))

    any_spec = pl.BlockSpec(memory_space=pl.ANY)
    outs = pl.pallas_call(
        functools.partial(attend_forward_kernel, count),
        grid=(width // pair,),
        in_specs=[whole((1, keys)), columns(16), *[whole((rows, width))] * 3, whole((keys, width))]
        + [columns(width)] * 4
        + [any_spec] * 3,
        out_specs=[columns(rows), pl.BlockSpec((2, rows, keys), lambda t: (t, 0, 0))]
        + [columns(rows)] * 2
        + [columns(keys)] * 3
        + [pl.BlockSpec((width, keys), lambda t: (0, 0))]
        + [any_spec] * 3,
        out_shape=[
            jax.ShapeDtypeStruct((rows, width), BF),
            jax.ShapeDtypeStruct((width // HD, rows, keys), BF),
            *[jax.ShapeDtypeStruct((rows, width), BF)] * 2,
            *[jax.ShapeDtypeStruct((keys, width), BF)] * 3,
            jax.ShapeDtypeStruct((width, keys), BF),
            *[jax.ShapeDtypeStruct((shards[n].shape[0] * 2 * count, width), BF) for n in names],
        ],
        scratch_shapes=[
            pltpu.VMEM((rows, keys), F32),
            pltpu.VMEM((rows, keys), F32),
            *gather_semaphores(count, sum(len(halves(shards[n].shape[0])) for n in names)),
        ],
        compiler_params=pltpu.CompilerParams(collective_id=3, has_side_effects=True, vmem_limit_bytes=56 * MIB),
        name="attend_forward",
    )(key_bias, w["vec"], squeezed, memory, x, table, w["q"], w["k"], w["v"], w["p"], *[shards[n] for n in names])
    return outs[:8], dict(zip(names, outs[8:]))


BACKWARD_PLAN = (
    (0, 0), (0, 1), (0, 2), (1, 1), (1, 2),
    (3, 3), (4, 1), (4, 2),
    (5, 0), (5, 1), (5, 2),
    (5, 3),
    (6, 1), (7, 0), (7, 2),
)


def attend_backward_kernel(
    count, cq_ref, pq_ref, k_ref, v_ref, pl_ref, p_ref, do_ref, in_t_ref, table_t_ref, wq_ref, wk_ref, wv_ref, up, down, o,
    dcb_ref, dpb_ref, gq_ref, gk_ref, gv_ref, gp_ref, up_out, down_out, o_out, dsq_out, dmem_out, dcur_out,
    dp_scr, ds_scr, dq_scr, dk_scr, dv_scr, dpl_scr, total, out_sem, *scratch,
):
    head, heads = pl.program_id(0), pl.num_programs(0)
    place = Place(count)
    units, stores = scatter_dense_units(place, count, (up, down, o), (up_out, down_out, o_out), scratch)
    first, *steps, last = scatter_steps(place, units, stores)
    plan = {at: [] for at in BACKWARD_PLAN}
    plan[BACKWARD_PLAN[0]] = [place.barrier, first]
    for i, step in enumerate(steps):
        plan[BACKWARD_PLAN[min(1 + i * (len(BACKWARD_PLAN) - 1) // len(steps), len(BACKWARD_PLAN) - 1)]].append(step)

    def point(k):
        for (t, at), chosen in plan.items():
            if at == k:
                @pl.when(head == t)
                def _(chosen=chosen):
                    for step in chosen:
                        step()

    rows, keys = cq_ref.shape[0], k_ref.shape[0]
    scale = HD ** (-0.5)
    block = 128
    flip = (
        lax.broadcasted_iota(jnp.int32, (block, block), 0)
        + lax.broadcasted_iota(jnp.int32, (block, block), 1)
        == block - 1
    ).astype(BF)
    point(0)
    dp_scr[...] = mm_nt(do_ref[...], v_ref[...])
    step = 32
    for start in range(0, rows, step):
        here = slice(start, start + step)
        prob = p_ref[0, here].astype(F32)
        dprob = dp_scr[here]
        delta = jnp.sum(prob * dprob, axis=1, keepdims=True)
        ds_scr[here] = (prob * (dprob - delta)).astype(BF)
    point(1)
    side = head % 2
    dv_scr[side] = mm_tn(do_ref[...], p_ref[0]).T.astype(BF)
    dk_scr[side] = mm_tn(cq_ref[...], ds_scr[...]).T.astype(BF)
    dcq = mm(ds_scr[...], k_ref[...]) * scale
    flipped = []
    for start in range(0, rows, block):
        here = slice(start, start + block)
        dp_scr[here] = mm(flip, ds_scr[here])
        flipped.append(mm(flip, pq_ref[here]).astype(BF))
        ds_scr[here] = pltpu.roll(dp_scr[here], rows - block - start, 1, stride=1, stride_axis=0).astype(BF)
    dpl_scr[side] = mm_tn(jnp.concatenate(flipped, axis=0), ds_scr[...]).T.astype(BF)
    dpq_flipped = mm(ds_scr[...], pl_ref[...]) * scale
    dpq = []
    for start in range(0, rows, block):
        piece = dpq_flipped[start : start + block]
        high = piece.astype(BF)
        dpq.append(mm(flip, high) + mm(flip, (piece - high.astype(F32)).astype(BF)))
    dpq = jnp.concatenate(dpq, axis=0)
    dq_scr[side] = (dcq + dpq).astype(BF)
    dcb_ref[...] = jnp.sum(dcq, axis=0, keepdims=True)
    dpb_ref[...] = jnp.sum(dpq, axis=0, keepdims=True)
    point(2)

    @pl.when(side == 1)
    def _():
        dq, dk, dv, dpl = (jnp.concatenate([ref[0], ref[1]], axis=1) for ref in (dq_scr, dk_scr, dv_scr, dpl_scr))
        gk_ref[...] = mm(in_t_ref[...], dk).astype(BF)
        gv_ref[...] = mm(in_t_ref[...], dv).astype(BF)
        gp_ref[...] = mm(table_t_ref[...], dpl).astype(BF)
        gq_ref[...] = mm(in_t_ref[:, 2 * rows :], dq).astype(BF)
        point(3)

        @pl.when(head == 1)
        def _():
            total[...] = jnp.zeros_like(total)

        for start in range(0, keys, rows):
            here = slice(start, start + rows)
            more = mm_nt(dk[here], wk_ref[...]) + mm_nt(dv[here], wv_ref[...])
            if start == 2 * rows:
                more = more + mm_nt(dq, wq_ref[...])
            total[here] += more

    @pl.when(head == heads - 1)
    def _():
        width = total.shape[1]
        own = pltpu.make_async_copy(total.at[pl.ds(2 * rows, rows)], dcur_out, out_sem.at[0])
        own.start()
        for i, out in enumerate((dsq_out, dmem_out)):
            ds_scr[:, :width] = total[i * rows : (i + 1) * rows].astype(BF)
            copy = pltpu.make_async_copy(ds_scr.at[:, pl.ds(0, width)], out, out_sem.at[1 + i])
            copy.start()
            copy.wait()
        own.wait()
        last()


def attend_backward(saved, probs, d_out, inputs_t, table_t, w, dense):
    count = lax.axis_size("seq")
    rows, width = d_out.shape
    keys = inputs_t.shape[1]
    heads = width // HD
    names = ("up", "down", "o")
    shapes = [(dense[n].shape[0] // (2 * count), width) for n in names]

    def whole(shape):
        return pl.BlockSpec(shape, lambda h: (0,) * len(shape), pipeline_mode=pl.Buffered(1))

    def columns(height):
        return pl.BlockSpec((height, HD), lambda h: (0, h))

    pair = pl.BlockSpec((width, 2 * HD), lambda h: (0, h // 2))
    any_spec = pl.BlockSpec(memory_space=pl.ANY)
    vmem = pl.BlockSpec(memory_space=pltpu.VMEM)
    outs = pl.pallas_call(
        functools.partial(attend_backward_kernel, count),
        grid=(heads,),
        in_specs=[columns(rows)] * 2
        + [columns(keys)] * 3
        + [pl.BlockSpec((1, rows, keys), lambda h: (h, 0, 0)), columns(rows), whole((width, keys)), whole((width, keys))]
        + [pair] * 3
        + [any_spec] * 3,
        out_specs=[columns(1)] * 2 + [pair] * 4 + [vmem] * 3 + [any_spec] * 3,
        out_shape=[
            *[jax.ShapeDtypeStruct((1, width), F32)] * 2,
            *[jax.ShapeDtypeStruct((width, width), BF)] * 4,
            *[jax.ShapeDtypeStruct(shape, F32) for shape in shapes],
            *[jax.ShapeDtypeStruct((rows, width), BF)] * 2,
            jax.ShapeDtypeStruct((rows, width), F32),
        ],
        scratch_shapes=[
            pltpu.VMEM((rows, keys), F32),
            pltpu.VMEM((rows, keys), BF),
            pltpu.VMEM((2, rows, HD), BF),
            *[pltpu.VMEM((2, keys, HD), BF)] * 3,
            pltpu.VMEM((keys, width), F32),
            pltpu.SemaphoreType.DMA((3,)),
            *scatter_dense_scratch(count, shapes),
        ],
        compiler_params=pltpu.CompilerParams(collective_id=1, has_side_effects=True, vmem_limit_bytes=62 * MIB),
        name="attend_backward",
    )(*saved, probs, d_out, inputs_t, table_t, w["q"], w["k"], w["v"], *[dense[n] for n in names])
    return outs[:2], outs[2:6], dict(zip(names, outs[6:9])), outs[9:]


def normalize(values):
    centre = values - jnp.mean(values, axis=-1, keepdims=True)
    spread = jnp.mean(centre * centre, axis=-1, keepdims=True)
    scale = lax.rsqrt(spread + epsilon)
    return centre * scale, scale


def normalize_back(grad, gain, unit, scale):
    pulled = grad * gain
    return scale * (
        pulled
        - jnp.mean(pulled, axis=-1, keepdims=True)
        - unit * jnp.mean(pulled * unit, axis=-1, keepdims=True)
    )


def gelu_parts(u):
    root = np.float32(np.sqrt(2.0 / np.pi))
    square = u * u
    tanh = jnp.tanh(u * (root + (root * 0.044715) * square))
    half = 0.5 * u
    value = half + half * tanh
    slope = 0.5 + 0.5 * tanh + half * (1.0 - tanh * tanh) * (root + (3 * 0.044715 * root) * square)
    return value, slope


VECTORS = ("cb", "pb", "sb", "ob", "g1", "s1", "db", "g2", "s2")


def feed_kernel(
    att_ref, x_ref, ct_ref, wo_ref, up_ref, down_ref, ub_ref, vec_ref,
    out_ref, gup_ref, gdown_ref, go_ref, dub_ref, sums_ref, dbl_ref, datt_ref,
    unit, scale, normed, acc, hidden, slope, dy, dy_low,
):
    turn = pl.program_id(0)
    chunks = pl.num_programs(0) // 2
    rows = x_ref.shape[0]
    at = {name: slice(i, i + 1) for i, name in enumerate(VECTORS)}

    def by_rows(run):
        repeat(rows // 128, lambda k: run(pl.ds(pl.multiple_of(k * 128, 128), 128)))

    def tally(name, values):
        sums_ref[at[name]] += jnp.sum(values, axis=0, keepdims=True)

    @pl.when(turn == 0)
    def _():
        sums_ref[...] = jnp.zeros_like(sums_ref)
        acc[...] = mm(att_ref[...], wo_ref[...])

        def first(here):
            unit[here], scale[here] = normalize(x_ref[here].astype(F32) + acc[here] + vec_ref[at["ob"]])
            normed[here] = (unit[here] * vec_ref[at["g1"]] + vec_ref[at["s1"]]).astype(BF)
            acc[here] = jnp.zeros_like(acc[here])

        by_rows(first)

    @pl.when(turn < chunks)
    def _():
        value, slope_here = gelu_parts(mm_nt(normed[...], up_ref[...]) + ub_ref[...])
        hidden[turn] = value.astype(BF)
        slope[turn] = slope_here.astype(BF)
        acc[...] += mm(hidden[turn], down_ref[...])

    @pl.when(turn == chunks - 1)
    def _():
        def second(here):
            unit2, scale2 = normalize(normed[here].astype(F32) + acc[here] + vec_ref[at["db"]])
            out_ref[here] = (unit2 * vec_ref[at["g2"]] + vec_ref[at["s2"]]).astype(BF)
            ct = ct_ref[here].astype(F32)
            tally("g2", ct * unit2)
            tally("s2", ct)
            dy[here] = normalize_back(ct, vec_ref[at["g2"]], unit2, scale2)
            tally("db", dy[here])
            dy_low[here] = dy[here].astype(BF)
            acc[here] = jnp.zeros_like(acc[here])

        by_rows(second)

    @pl.when(turn >= chunks)
    def _():
        j = 2 * chunks - 1 - turn
        gdown_ref[...] = mm_tn(hidden[j], dy_low[...]).astype(BF)
        du = (mm_nt(dy_low[...], down_ref[...]) * slope[j].astype(F32)).astype(BF)
        dub_ref[...] = jnp.sum(du.astype(F32), axis=0, keepdims=True)
        gup_ref[...] = mm_tn(du, normed[...]).astype(BF)
        acc[...] += mm(du, up_ref[...])

    @pl.when(turn == 2 * chunks - 1)
    def _():
        def third(here):
            dnormed = dy[here] + acc[here]
            tally("g1", dnormed * unit[here])
            tally("s1", dnormed)
            dbl = normalize_back(dnormed, vec_ref[at["g1"]], unit[here], scale[here])
            tally("ob", dbl)
            dbl_ref[here] = dbl
            dy_low[here] = dbl.astype(BF)

        by_rows(third)
        go_ref[...] = mm_tn(att_ref[...], dy_low[...]).astype(BF)
        datt_ref[...] = mm_nt(dy_low[...], wo_ref[...]).astype(BF)


def feed(attended, x, ct, w):
    rows, width = x.shape
    hidden = w["up"].shape[0]
    size = 512
    chunks = hidden // size

    def whole(shape):
        return pl.BlockSpec(shape, lambda t: (0,) * len(shape), pipeline_mode=pl.Buffered(1))

    def kept(shape):
        return pl.BlockSpec(shape, lambda t: (0,) * len(shape))

    def weight(t):
        return jnp.where(t < chunks, t, 2 * chunks - 1 - t)

    def grad(t):
        return jnp.where(t < chunks, chunks - 1, 2 * chunks - 1 - t)

    outs = pl.pallas_call(
        feed_kernel,
        grid=(2 * chunks,),
        in_specs=[whole((rows, width))] * 3
        + [whole((width, width))]
        + [pl.BlockSpec((size, width), lambda t: (weight(t), 0))] * 2
        + [pl.BlockSpec((1, size), lambda t: (0, weight(t))), whole((16, width))],
        out_specs=[kept((rows, width))]
        + [pl.BlockSpec((size, width), lambda t: (grad(t), 0))] * 2
        + [kept((width, width)), pl.BlockSpec((1, size), lambda t: (0, grad(t))), kept((16, width))]
        + [kept((rows, width))] * 2,
        out_shape=[
            jax.ShapeDtypeStruct((rows, width), BF),
            *[jax.ShapeDtypeStruct((hidden, width), BF)] * 2,
            jax.ShapeDtypeStruct((width, width), BF),
            jax.ShapeDtypeStruct((1, hidden), F32),
            jax.ShapeDtypeStruct((16, width), F32),
            jax.ShapeDtypeStruct((rows, width), F32),
            jax.ShapeDtypeStruct((rows, width), BF),
        ],
        scratch_shapes=[
            pltpu.VMEM((rows, width), F32),
            pltpu.VMEM((rows, 1), F32),
            pltpu.VMEM((rows, width), BF),
            pltpu.VMEM((rows, width), F32),
            pltpu.VMEM((chunks, rows, size), BF),
            pltpu.VMEM((chunks, rows, size), BF),
            pltpu.VMEM((rows, width), F32),
            pltpu.VMEM((rows, width), BF),
        ],
        compiler_params=pltpu.CompilerParams(vmem_limit_bytes=56 * MIB),
        name="feed",
    )(attended, x, ct, w["o"], w["up"], w["down"], w["ub"], w["vec"])
    outputs, gup, gdown, go, dub, sums, dbl, datt = outs
    return outputs, dict(up=gup, down=gdown, o=go, ub=dub, sums=sums), dbl, datt


def body(
    inputs, lengths,
    query_weight, key_weight, value_weight, position_weight, content_bias, position_bias,
    output_weight, output_bias, first_gain, first_shift, up_weight, up_bias, down_weight, down_bias,
    second_gain, second_shift, squeeze_weight, squeeze_bias, cotangent,
):
    seq = lax.axis_index("seq")
    head = lax.axis_index("head")
    rows, width = inputs.shape[2:]

    x = lax.dynamic_index_in_dim(inputs[:, 0], head, 0, keepdims=False)
    book_lengths = lax.dynamic_index_in_dim(lengths, head, 0, keepdims=False)
    padded_lengths = jnp.concatenate([jnp.zeros((4,), jnp.int32), book_lengths])
    window = lax.dynamic_slice_in_dim(padded_lengths, seq, 5, 0)
    own_length = window[4]

    layout = squeeze_layout(rows)
    row_ids = jnp.arange(rows)
    kept = (row_ids < own_length)[:, None]
    masked = jnp.where(kept, x, jnp.zeros_like(x))
    shards = dict(
        q=query_weight, k=key_weight, v=value_weight, p=position_weight,
        o=output_weight, up=up_weight.T, down=down_weight, sq=squeeze_weight.T,
        cb=content_bias, pb=position_bias, ob=output_bias, g1=first_gain, s1=first_shift, ub=up_bias,
        db=down_bias, g2=second_gain, s2=second_shift, sb=squeeze_bias,
    )
    w, squeezed, memory = open_layer(shards, x, masked, layout)

    flat = np.arange(0, 3 * rows, 3)
    history_ok = jnp.asarray(flat % rows) < window[:3][flat // rows]
    valid = jnp.concatenate([history_ok, row_ids < window[3], row_ids < window[4]])
    key_bias = jnp.where(valid, 0.0, -1e30).astype(F32)[None]

    table = table_rows(width, 3 * rows)
    (attended, probs, *saved, keys_in_t), dense = attend_forward(key_bias, squeezed, memory, x, jnp.asarray(table), w, shards)
    w.update(dense)

    ct = lax.dynamic_index_in_dim(cotangent[:, 0], head, 0, keepdims=False)
    outputs, grads, dblended, dattended = feed(attended, x, ct, w)

    (dcb, dpb), squares, final, (dsqueezed, dmemory, dcurrent) = attend_backward(
        saved, probs, dattended, keys_in_t, jnp.asarray(np.ascontiguousarray(table.T)), w, grads
    )
    grads.update(zip(("q", "k", "v", "p"), squares))
    grads["cb"] = dcb
    grads["pb"] = dpb
    more, input_rows, output_rows = close_layer(
        grads, w, layout, dsqueezed, dmemory, dcurrent, dblended, masked, kept.astype(F32), outputs
    )
    final.update(more)
    return (
        output_rows[:, None], input_rows[:, None],
        final["q"], final["k"], final["v"], final["p"], final["cb"], final["pb"],
        final["o"], final["ob"], final["g1"], final["s1"], final["up"].T, final["ub"],
        final["down"], final["db"], final["g2"], final["s2"], final["sq"].T, final["sb"],
    )


def solution(mesh):
    both = ("head", "seq")
    matrix = P("seq", "head")
    in_specs = (
        P(None, "seq", None, None), P(), matrix, matrix, matrix, matrix, P(both), P(both),
        P(both, None), P("seq"), P("seq"), P("seq"), P(None, both), P(both), P(both, None), P("seq"),
        P("seq"), P("seq"), P(None, both), P(both), P(None, "seq", None, None),
    )
    rows = P(None, "seq", "head", None)
    out_specs = (
        rows, rows, matrix, matrix, matrix, matrix, P(both), P(both),
        P(both, None), P(both), P(both), P(both), P(None, both), P(both), P(both, None), P(both),
        P(both), P(both), P(None, both), P(both),
    )
    return jax.shard_map(body, mesh=mesh, in_specs=in_specs, out_specs=out_specs, check_vma=False)
```

```python
import functools

import jax
import jax.numpy as jnp
import numpy as np
from jax import lax
from jax.experimental import pallas as pl
from jax.experimental.pallas import tpu as pltpu
from jax.sharding import PartitionSpec as P

HD = 128
BF = jnp.bfloat16
F32 = jnp.float32
epsilon = 1e-05
MIB = 1024 * 1024


def mm(left, right, contract=((1,), (0,)), out=F32):
    return lax.dot_general(left, right, (contract, ((), ())), preferred_element_type=F32).astype(out)


def mm_nt(left, right, out=F32):
    return mm(left, right, ((1,), (1,)), out)


def mm_tn(left, right, out=F32):
    return mm(left, right, ((0,), (0,)), out)


def table_rows(width, count):
    distance = np.arange(count - 1, -1, -1).astype(np.float32)[:, None]
    exponent = -np.arange(0, width, 2).astype(np.float32) / np.float32(width)
    frequency = np.power(np.float32(10000.0), exponent).astype(np.float32)
    angles = (distance * frequency[None, :]).astype(np.float32)
    return np.concatenate([np.sin(angles), np.cos(angles)], axis=1).astype(BF)


def squeeze_layout(rows):
    pad = -(-(rows // 3 + 2) // 16) * 16
    taps = np.zeros((3, rows, 3 * pad), np.float32)
    collect = np.zeros((rows, 3 * pad), np.float32)
    biased = np.zeros((3 * pad, 1), np.float32)
    for role in range(3):
        first = role * rows // 3
        for i in range(rows):
            flat = role * rows + i
            taps[flat % 3, i, role * pad + flat // 3 - first] = 1.0
            collect[flat // 3, role * pad + flat // 3 - first] = 1.0
        for c in range(first, ((role + 1) * rows - 1) // 3 + 1):
            if role == 0 or 3 * c >= role * rows:
                biased[role * pad + c - first] = 1.0
    return pad, taps.astype(BF), collect.astype(BF), biased


MESH = pl.DeviceIdType.MESH
CORE, XFLIP, YFLIP, UP, DOWN = range(5)


def repeat(count, run):
    def body(i, carry):
        run(i)
        return carry

    lax.fori_loop(0, count, body, 0)


class Place:
    def __init__(self, count):
        self.count = count
        self.n = count // 4
        self.h = lax.axis_index("head")
        self.s = lax.axis_index("seq")
        self.a = self.s // 4
        self.b = (self.s // 2) % 2
        self.c = self.s % 2

    def seq_of(self, a, b, c):
        return a * 4 + b * 2 + c

    def neighbour(self, kind):
        s, h = self.s, self.h
        if kind == CORE:
            return (h, s + 1 - 2 * self.c)
        if kind == XFLIP:
            return (h, s + 2 - 4 * self.b)
        if kind == YFLIP:
            return (1 - h, s)
        return (h, s + 4) if kind == UP else (h, s - 4)

    def when(self, kind):
        if kind == UP:
            return pl.when(self.a < self.n - 1)
        if kind == DOWN:
            return pl.when(self.a > 0)
        return lambda run: run()

    def far(self):
        s, count = self.s, self.count
        for by, other in ((1, self.c == 1), (-1, self.c == 0), (2, self.b == 1), (-2, self.b == 0), (3, None), (-3, None)):
            inside = self.inside(by)
            yield by, inside if other is None else jnp.logical_and(inside, other)

    def inside(self, by):
        return self.s + by < self.count if by > 0 else self.s + by >= 0

    def barrier(self, shifts=False):
        barrier = pltpu.get_barrier_semaphore()
        for kind in range(5):
            @self.when(kind)
            def _(kind=kind):
                pl.semaphore_signal(barrier, inc=1, device_id=self.neighbour(kind), device_id_type=MESH)
        peers = 5 - jnp.where(self.a == 0, 1, 0) - jnp.where(self.a == self.n - 1, 1, 0)
        if shifts:
            for by, there in self.far():
                @pl.when(there)
                def _(by=by):
                    pl.semaphore_signal(barrier, inc=1, device_id=(self.h, self.s + by), device_id_type=MESH)
                peers = peers + jnp.where(there, 1, 0)
        pl.semaphore_wait(barrier, peers)

    def along(self, i):
        return (self.a + self.n // 2 + i) % self.n


class Gather:
    def __init__(self, place, units, local_sem, send_sem, recv_sem):
        self.place, self.units = place, units
        self.local_sem, self.send_sem, self.recv_sem = local_sem, send_sem, recv_sem

    def view(self, u, h, s):
        shard, full, view, order = self.units[u]
        return view(full, h, s)

    def copy(self, u, kind, h, s, own=False):
        n = self.place.n
        a, b = s // 4, (s // 2) % 2
        order = self.units[u][3]
        other = b if order.index("x") < order.index("z") else h
        sent = {
            UP: other * n + a,
            DOWN: (2 + other) * n + a,
            XFLIP: (4 + h) * n + a,
            YFLIP: (6 + b) * n + a,
            CORE: (8 + h * 2 + b) * n + a,
        }[kind]
        there = self.view(u, h, s)
        return pltpu.make_async_remote_copy(
            src_ref=self.units[u][0] if own else there,
            dst_ref=there,
            send_sem=self.send_sem.at[u, sent],
            recv_sem=self.recv_sem.at[u, h * self.place.count + s],
            device_id=self.place.neighbour(kind),
            device_id_type=MESH,
        )

    def local(self, u):
        return pltpu.make_async_copy(self.units[u][0], self.view(u, self.place.h, self.place.s), self.local_sem.at[u])

    def sources(self):
        found = []
        for t in range(self.place.n):
            for sign in ((1, -1) if t else (0,)):
                for x in (0, 1):
                    for y in (0, 1):
                        if t or x or y:
                            found.append((t, sign, x, y))
        return sorted(found, key=lambda e: e[0] + 2 * (e[2] + e[3]))

    def onward(self, u, sign, x, y):
        order = self.units[u][3]
        moved = {"x": x, "y": y, "z": sign}
        last = max([i for i in range(3) if moved[order[i]]], default=-1)
        kinds = []
        if last >= 0 and order[last] == "z":
            kinds.append(UP if sign > 0 else DOWN)
        for dim in order[last + 1 :]:
            kinds += {"x": [XFLIP], "y": [YFLIP], "z": [UP, DOWN]}[dim]
        return kinds + [CORE]

    def send(self, u, kind, h, s, own, wait):
        @self.place.when(kind)
        def _():
            copy = self.copy(u, kind, h, s, own)
            if wait:
                copy.wait_send()
            else:
                copy.start()

    def begin(self, wait=False):
        p = self.place
        for u in range(len(self.units)):
            for kind in self.onward(u, 0, 0, 0):
                self.send(u, kind, p.h, p.s, True, wait)
        if not wait:
            for u in range(len(self.units)):
                self.local(u).start()

    def pass_on(self, entry, wait=False):
        p = self.place
        t, sign, x, y = entry
        a = p.a - sign * t
        h = 1 - p.h if y else p.h
        s = p.seq_of(a, 1 - p.b if x else p.b, p.c)

        def run():
            for u in range(len(self.units)):
                if not wait:
                    self.copy(u, CORE, h, s).wait_recv()
                for kind in self.onward(u, sign, x, y):
                    self.send(u, kind, h, s, False, wait)

        if t:
            pl.when(jnp.logical_and(a >= 0, a <= p.n - 1))(run)
        else:
            run()

    def arrived(self):
        p = self.place

        def core(i):
            h, a, b = i // (2 * p.n), i // 2 % p.n, i % 2
            for u in range(len(self.units)):
                self.copy(u, CORE, h, p.seq_of(a, b, 1 - p.c)).wait_recv()

        repeat(4 * p.n, core)
        for u in range(len(self.units)):
            self.local(u).wait()

    def sent(self):
        self.begin(True)
        for entry in self.sources():
            self.pass_on(entry, True)

    def finish(self):
        self.arrived()
        self.sent()

    def steps(self):
        return [self.begin] + [functools.partial(self.pass_on, entry) for entry in self.sources()] + [self.finish]


GATHER_ORDERS = ("yzx", "xzy", "zxy", "zyx")


def halves(rows):
    return [(0, rows // 2), (rows // 2, rows // 2)] if rows % 32 == 0 else [(0, rows)]


def block_units(shard, full, count, first):
    rows = shard.shape[0]
    units = []
    for i, (at, size) in enumerate(halves(rows)):
        def view(ref, h, s, at=at, size=size):
            return ref.at[pl.ds(pl.multiple_of((h * count + s) * rows + at, size), size)]

        units.append((shard.at[pl.ds(at, size)], full, view, GATHER_ORDERS[(first + i) % 4]))
    return units


def square_unit(shard, full, order):
    r, w = shard.shape

    def view(ref, h, s):
        return ref.at[pl.ds(pl.multiple_of(s * r, r), r), pl.ds(pl.multiple_of(h * w, w), w)]

    return (shard, full, view, order)


def kept_rows(rows, window):
    at = lax.broadcasted_iota(jnp.int32, rows.shape, 0)
    return jnp.where(at < window[4], rows.astype(F32), 0.0).astype(rows.dtype)


def key_bias(rows, window):
    key = lax.broadcasted_iota(jnp.int32, (1, 3 * rows), 1)
    flat = 3 * key
    source = jnp.where(flat >= 2 * rows, 2, jnp.where(flat >= rows, 1, 0))
    source = jnp.where(key >= 2 * rows, 4, jnp.where(key >= rows, 3, source))
    first = jnp.where(key >= 2 * rows, 2 * rows, jnp.where(key >= rows, rows, source * rows))
    limit = sum(jnp.where(source == i, window[i], 0) for i in range(5))
    return jnp.where(jnp.where(key < rows, flat, key) - first < limit, 0.0, -1e30)


def open_kernel(
    count, small_names, q, k, v, p, sq, small, both, taps_t, window, biased,
    q_f, k_f, v_f, p_f, sq_f, vec, vec_up, made_out, memory,
    small_f, taps_scr, x_scr, sq_scr, grouped, made, load_sem, row_send, row_recv, *sems,
):
    place = Place(count)
    place.barrier(True)
    rows, width = x_scr.shape
    x = both.at[place.h]

    def small_view(ref, h, s):
        return ref.at[pl.ds(pl.multiple_of((h * count + s) * 8, 8), 8)]

    early = Gather(place, block_units(sq, sq_f, count, 0) + [(small, small_f, small_view, "zxy")], *sems[:3])
    late = Gather(
        place, [square_unit(*pair, GATHER_ORDERS[i]) for i, pair in enumerate(((q, q_f), (k, k_f), (v, v_f), (p, p_f)))], *sems[3:]
    )
    rows_copy = pltpu.make_async_remote_copy(
        src_ref=x,
        dst_ref=memory,
        send_sem=row_send,
        recv_sem=row_recv,
        device_id=(place.h, place.s + 1),
        device_id_type=MESH,
    )
    loads = [
        pltpu.make_async_copy(source, target, load_sem.at[i])
        for i, (source, target) in enumerate(((taps_t, taps_scr), (x, x_scr), (sq_f, sq_scr)))
    ]
    early.begin()
    late.begin()

    @pl.when(place.inside(1))
    def _():
        rows_copy.start()

    loads[0].start()
    loads[1].start()
    blank = pltpu.make_async_copy(made_out.at[pl.ds(0, rows)], memory, load_sem.at[3])

    @pl.when(place.s == 0)
    def _():
        made_out[...] = jnp.zeros_like(made_out)
        blank.start()
        blank.wait()

    loads[0].wait()
    loads[1].wait()
    x_scr[...] = kept_rows(x_scr[...], window)
    entries = early.sources()

    def group(tap):
        grouped[tap] = mm(taps_scr[tap], x_scr[...]).astype(BF)

    def square(tap):
        more = mm_nt(grouped[tap], sq_scr[:, tap * width : (tap + 1) * width])
        if tap:
            made[...] += more
        else:
            made[...] = more + biased[...] * vec[2:3]

    def unpack():
        for slot in range(2 * count):
            for name, row, at, size, target in small_names:
                if size * 2 * count > vec.shape[1] * (4 if name == "ub" else 1) and slot >= count:
                    continue
                ref = vec_up if name == "ub" else vec
                ref[target : target + 1, slot * size : (slot + 1) * size] = small_f[slot * 8 + row : slot * 8 + row + 1, at : at + size]

    lag = len(entries) // OPEN_LAG
    for i, entry in enumerate(entries):
        early.pass_on(entry)
        if i >= lag:
            late.pass_on(entries[i - lag])
        if i < 3:
            group(i)
    early.arrived()
    loads[2].start()
    unpack()
    loads[2].wait()
    rest = spread_steps([functools.partial(late.pass_on, entry) for entry in entries[len(entries) - lag :]], 3)
    for tap in range(3):
        for step in rest[tap]:
            step()
        square(tap)
    made_out[...] = made[...].astype(BF)
    late.arrived()

    @pl.when(place.inside(-1))
    def _():
        rows_copy.wait_recv()

    @pl.when(place.inside(1))
    def _():
        rows_copy.wait_send()

    early.sent()
    late.sent()


def spread_steps(steps, points):
    out = [[] for _ in range(points)]
    for i, step in enumerate(steps):
        out[i * points // len(steps)].append(step)
    return out


OPEN_LAG = 2


def gather_semaphores(count, units):
    return [
        pltpu.SemaphoreType.DMA((units,)),
        pltpu.SemaphoreType.DMA((units, 12 * (count // 4))),
        pltpu.SemaphoreType.DMA((units, 2 * count)),
    ]


def small_layout(both, seq):
    names = []
    for i, name in enumerate(("cb", "pb", "sb")):
        names.append((name, 0, i * both, both, i))
    names.append(("ub", 1, 0, 4 * both, 0))
    for i, name in enumerate(("ob", "g1", "s1", "db", "g2", "s2")):
        names.append((name, 2 + i // 2, (i % 2) * seq, seq, 3 + i))
    return names


def open_layer(w, inputs, window, layout):
    pad, taps, collect, biased = layout
    count = lax.axis_size("seq")
    both, seq = w["cb"].shape[0], w["ob"].shape[0]
    rows, width = inputs.shape[1:]
    layout = small_layout(both, seq)
    lines = [[] for _ in range(8)]
    for name, row, at, size, target in layout:
        lines[row].append(w[name].astype(F32))
    lines = [jnp.concatenate(parts) if parts else jnp.zeros((128,), F32) for parts in lines]
    small = jnp.stack([jnp.pad(line, (0, 128 - line.shape[0])) for line in lines])
    names = ("q", "k", "v", "p", "sq")
    any_spec = pl.BlockSpec(memory_space=pl.ANY)
    vmem_spec = pl.BlockSpec(memory_space=pltpu.VMEM)
    outs = pl.pallas_call(
        functools.partial(open_kernel, count, layout),
        in_specs=[any_spec] * 8 + [pl.BlockSpec(memory_space=pltpu.SMEM), vmem_spec],
        out_specs=[any_spec] * 5 + [vmem_spec] * 3 + [any_spec],
        out_shape=[
            *[jax.ShapeDtypeStruct((width, width), BF) for _ in range(4)],
            jax.ShapeDtypeStruct((width, w["sq"].shape[1]), BF),
            jax.ShapeDtypeStruct((16, width), F32),
            jax.ShapeDtypeStruct((1, 4 * width), F32),
            jax.ShapeDtypeStruct((3 * pad, width), BF),
            jax.ShapeDtypeStruct((rows, width), BF),
        ],
        scratch_shapes=[
            pltpu.VMEM((8 * 2 * count, 128), F32),
            pltpu.VMEM((3, 3 * pad, rows), BF),
            pltpu.VMEM((rows, width), BF),
            pltpu.VMEM((width, w["sq"].shape[1]), BF),
            pltpu.VMEM((3, 3 * pad, width), BF),
            pltpu.VMEM((3 * pad, width), F32),
            pltpu.SemaphoreType.DMA((4,)),
            *[pltpu.SemaphoreType.DMA] * 2,
            *gather_semaphores(count, 1 + len(halves(w["sq"].shape[0]))),
            *gather_semaphores(count, 4),
        ],
        compiler_params=pltpu.CompilerParams(collective_id=0, has_side_effects=True, vmem_limit_bytes=62 * MIB),
        name="open_layer",
    )(
        *[w[n] for n in names], small, inputs, jnp.asarray(np.ascontiguousarray(taps.transpose(0, 2, 1))), window, jnp.asarray(biased)
    )
    return dict(zip(names, outs), vec=outs[5], ub=outs[6]), outs[7], outs[8]


class Scatter:
    def __init__(self, place, view, order, sums, own, first, second, line, local_sem, send_sem, recv_sem):
        self.place, self.view = place, view
        self.by_y = order[0] == "y"
        self.late = order[2] == "z"
        self.sums, self.own, self.first, self.second, self.line = sums, own, first, second, line
        self.local_sem, self.send_sem, self.recv_sem = local_sem, send_sem, recv_sem
        self.f, self.g = (place.h, place.b) if self.by_y else (place.b, place.h)
        self.flips = (YFLIP, XFLIP) if self.by_y else (XFLIP, YFLIP)

    def index(self, f, g, a):
        return (f * 2 + g) * self.place.n + a

    def slot(self, f, g, a, c):
        h, b = (f, g) if self.by_y else (g, f)
        return h, self.place.seq_of(a, b, c)

    def remote(self, source, target, kind, send_at, recv_at):
        return pltpu.make_async_remote_copy(
            src_ref=source,
            dst_ref=target,
            send_sem=self.send_sem.at[send_at],
            recv_sem=self.recv_sem.at[recv_at],
            device_id=self.place.neighbour(kind),
            device_id_type=MESH,
        )

    def core_copy(self, i):
        return self.remote(self.sums.at[i], self.sums.at[i], CORE, i, i)

    def first_copy(self, g, a):
        n = self.place.n
        to = g * n + a
        return self.remote(self.sums.at[self.index(1 - self.f, g, a)], self.first.at[to], self.flips[0], 4 * n + to, 4 * n + to)

    def second_copy(self, a):
        n = self.place.n
        to = a if self.late else 0
        return self.remote(self.sums.at[self.index(self.f, 1 - self.g, a)], self.second.at[to], self.flips[1], 6 * n + to, 6 * n + to)

    def line_at(self, g, at):
        return at if self.late else g * (self.place.n + 1) + at

    def line_copy(self, kind, g, a):
        n = self.place.n
        to = self.line_at(g, a if kind == UP else jnp.where(a == self.place.a - 1, n, a))
        sent = 7 * n + (a if self.late else g * n + a)
        return self.remote(self.sums.at[self.index(self.f, g, a)], self.line.at[to], kind, sent, 7 * n + to)

    def line_wait(self, at):
        n = self.place.n
        self.remote(self.line.at[at], self.line.at[at], CORE, 7 * n, 7 * n + at).wait_recv()

    def piece(self, part, i):
        return (self.f if part >= 2 else 1 - self.f, self.g if part % 2 else 1 - self.g, self.place.along(i))

    def trade(self, part, i):
        f, g, a = self.piece(part, i)
        at = self.index(f, g, a)
        source = self.view(*self.slot(f, g, a, 1 - self.place.c))
        self.remote(source, self.sums.at[at], CORE, at, at).start()

    def load(self, part, i):
        source = self.view(*self.slot(*self.piece(part, i), self.place.c))
        return pltpu.make_async_copy(source, self.own.at[i % 4], self.local_sem.at[i % 4])

    def absorb(self, part, i):
        n = self.place.n
        f, g, a = self.piece(part, i)
        at = self.index(f, g, a)
        self.load(part, i).wait()
        self.core_copy(at).wait_recv()
        self.add(at, [(self.own, i % 4)])

        @pl.when(i + 4 < n)
        def _():
            self.load(part, i + 4).start()

        if part < 3:
            @pl.when(i + 4 >= n)
            def _():
                self.load(part + 1, i + 4 - n).start()

        if part < 2:
            self.first_copy(g, a).start()

    def after_first(self, g, a):
        self.first_copy(g, a).wait_recv()
        return self.index(self.f, g, a), [(self.first, g * self.place.n + a)]

    def add(self, i, refs):
        total = self.sums[i].astype(F32)
        for ref, at in refs:
            total = total + ref[at].astype(F32)
        self.sums[i] = total.astype(BF)

    def add_line(self, i, g):
        p = self.place
        for fed, at in ((p.a > 0, p.a), (p.a < p.n - 1, p.n)):
            @pl.when(fed)
            def _(at=self.line_at(g, at)):
                self.line_wait(at)
                self.add(i, [(self.line, at)])

    def flip_second(self, a):
        i, refs = self.after_first(1 - self.g, a)
        self.add(i, refs)
        if not self.late:
            self.add_line(i, 1 - self.g)
        self.second_copy(a).start()

    def move(self, g, d):
        p = self.place
        for kind, a, inside, fed in (
            (UP, p.a + d, p.a + d <= p.n - 1, p.a > 0),
            (DOWN, p.a - d, p.a - d >= 0, p.a < p.n - 1),
        ):
            @pl.when(inside)
            def _(kind=kind, a=a, fed=fed):
                i, refs = self.after_first(g, a)
                if self.late:
                    self.second_copy(a).wait_recv()
                    refs.append((self.second, a))
                self.add(i, refs)

                @pl.when(fed)
                def _():
                    at = self.line_at(g, a)
                    self.line_wait(at)
                    self.add(i, [(self.line, at)])

                self.line_copy(kind, g, a).start()

    def finish(self, store):
        p = self.place
        n = p.n
        i, refs = self.after_first(self.g, p.a)
        to = p.a if self.late else 0
        self.second_copy(p.a).wait_recv()
        self.add(i, refs + [(self.second, to)])
        self.add_line(i, self.g)
        store(self.sums[i].astype(F32))
        repeat(4 * n, lambda i: self.core_copy(i).wait_send())
        repeat(2 * n, lambda i: self.first_copy(i // n, i % n).wait_send())
        if self.late:
            repeat(n, lambda a: self.second_copy(a).wait_send())
        else:
            self.second_copy(p.a).wait_send()

        def line_done(a):
            for kind, inside in ((UP, a > p.a), (DOWN, a < p.a)):
                @pl.when(inside)
                def _(kind=kind):
                    for g in (self.g,) if self.late else (0, 1):
                        self.line_copy(kind, g, a).wait_send()

        repeat(n, line_done)


def scatter_scratch(count, shape, order):
    n = count // 4
    late = order[2] == "z"
    lines = n + 1 if late else 2 * n + 2
    return [
        *[pltpu.VMEM((k, *shape), BF) for k in (4 * n, 4, 2 * n, n if late else 1, lines)],
        pltpu.SemaphoreType.DMA((4,)),
        pltpu.SemaphoreType.DMA((9 * n,)),
        pltpu.SemaphoreType.DMA((7 * n + lines,)),
    ]


SCATTER_ORDERS = ("yzx", "xzy", "yxz", "xyz")


def block_scatters(rows, first):
    return [(at, size, SCATTER_ORDERS[(first + i) % 4]) for i, (at, size) in enumerate(halves(rows))]


def block_pairs(ref, rows, at, size, count):
    def view(h, s):
        return ref.at[pl.ds(pl.multiple_of((h * count + s) * rows + at, size), size)]

    return view


def square_pairs(ref, r, w):
    def view(h, s):
        return ref.at[pl.ds(pl.multiple_of(s * r, r), r), pl.ds(pl.multiple_of(h * w, w), w)]

    return view


def scatter_steps(place, units, stores, between=lambda at: None):
    n = place.n
    middle = [u for u in units if not u.late]
    late = [u for u in units if u.late]

    def each(run, some=units):
        def one(i):
            for unit in some:
                run(unit, i)

        return one

    def begin():
        for part in range(4):
            repeat(n, each(lambda u, i, part=part: u.trade(part, i)))
            if part == 0:
                repeat(4, each(lambda u, i: u.load(0, i).start()))
        between(0)

    def absorb(part):
        repeat(n, each(lambda u, i: u.absorb(part, i), middle + late))

    def second(d):
        for u in middle:
            u.move(1 - u.g, d)
        for u in late:
            u.flip_second(place.along(n - 1 - d))

    def third(d):
        for u in middle:
            u.move(u.g, d)

    def fourth():
        between(1)
        for u in late:
            u.flip_second(place.along(n - 1))
        for u in middle:
            u.flip_second(place.a)
        between(2)

    def fifth(d):
        for u in late:
            u.move(u.g, d)

    def finish():
        between(3)
        for unit, store in zip(units, stores):
            unit.finish(store)
        between(4)

    far = range(n - 1, 0, -1)
    return (
        [begin]
        + [functools.partial(absorb, part) for part in range(4)]
        + [functools.partial(second, d) for d in far]
        + [functools.partial(third, d) for d in far]
        + [fourth]
        + [functools.partial(fifth, d) for d in far]
        + [finish]
    )


def store_into(out):
    def store(value):
        out[...] = value

    return store


def scatter_dense_units(place, count, grads, outs, scratch):
    units, stores = [], []
    for ref, out, first in zip(grads, outs, (0, 2, 1)):
        rows = out.shape[0]
        for at, size, order in block_scatters(rows, first):
            units.append(Scatter(place, block_pairs(ref, rows, at, size, count), order, *scratch[:8]))
            stores.append(store_into(out.at[pl.ds(at, size)]))
            scratch = scratch[8:]
    return units, stores


def scatter_dense_scratch(count, shapes):
    scratch = []
    for (rows, width), first in zip(shapes, (0, 2, 1)):
        for at, size, order in block_scatters(rows, first):
            scratch += scatter_scratch(count, (size, width), order)
    return scratch


CLOSE_PLAN = (
    *("m0", ":load", "m1", "m2", ":wait", "c0", "m3", "c1", "m4", "c2", "l0"),
    *("m5", "l1", "l2", "l3", "l4", "m6", ":memory", "l5", ":out", "m7", "l6", "m8", "l7", ":rows", "l8", "m9", "l9"),
)


def close_kernel(
    count, gq, gk, gv, gp, sqw, dcb, dpb, dsb, vec, dub, dmade, dmem, dcur, dbl, masked, window, taps, outputs,
    q_out, k_out, v_out, p_out, sq_out, vec_out, ub_out, dx_out, rows_out,
    sums, parts, vec_send, vec_recv, returned, from_next, gsq, sq_scr, dcur_scr, dbl_scr, masked_scr, taps_scr,
    spread, dmasked, load_sem, row_send, row_recv, out_sem, out_send, out_recv, *scratch,
):
    place = Place(count)
    place.barrier(True)
    r, w = q_out.shape
    rows, width = spread.shape
    half = rows // 2
    units, stores = [], []
    for ref, out, order in zip((gq, gk, gv, gp), (q_out, k_out, v_out, p_out), SCATTER_ORDERS):
        units.append(Scatter(place, square_pairs(ref, r, w), order, *scratch[:8]))
        stores.append(store_into(out))
        scratch = scratch[8:]
    low_units, low_stores = [], []
    wide = sq_out.shape[0]
    for at, size, order in block_scatters(wide, 0):
        low_units.append(Scatter(place, block_pairs(gsq, wide, at, size, count), order, *scratch[:8]))
        low_stores.append(store_into(sq_out.at[pl.ds(at, size)]))
        scratch = scratch[8:]

    loads = [
        pltpu.make_async_copy(source, target, load_sem.at[i])
        for i, (source, target) in enumerate(
            (
                (taps, taps_scr), (masked.at[place.h], masked_scr), (sqw, sq_scr), (dcur, dcur_scr), (dbl, dbl_scr),
            )
        )
    ]

    pad = dmade.shape[0] // 3

    def rows_copy(i):
        here = pl.ds(i * pad, pad)
        return pltpu.make_async_remote_copy(
            src_ref=dmade.at[here] if i < 3 else dmem,
            dst_ref=returned.at[here] if i < 3 else from_next,
            send_sem=row_send.at[i],
            recv_sem=row_recv.at[i],
            device_id=(place.h, place.s + (i - 4 if i < 3 else -1)),
            device_id_type=MESH,
        )

    def exchange(i, source, target, wait=False):
        own = pltpu.make_async_copy(source.at[pl.ds(pl.multiple_of(place.h * half, half), half)], target.at[place.h], out_sem.at[i])
        other = pltpu.make_async_remote_copy(
            src_ref=source.at[pl.ds(pl.multiple_of((1 - place.h) * half, half), half)],
            dst_ref=target.at[place.h],
            send_sem=out_send.at[i],
            recv_sem=out_recv.at[i],
            device_id=place.neighbour(YFLIP),
            device_id_type=MESH,
        )
        if wait:
            own.wait()
            other.wait()
        else:
            other.start()
            own.start()

    def vec_copy(kind):
        return pltpu.make_async_remote_copy(
            src_ref=sums.at[kind],
            dst_ref=parts.at[kind],
            send_sem=vec_send.at[kind],
            recv_sem=vec_recv.at[kind],
            device_id=place.neighbour(kind),
            device_id_type=MESH,
        )

    def between(at):
        kinds = (CORE, XFLIP, YFLIP)
        if at == 0:
            sums[CORE, 0:16] = vec[...]
            sums[CORE, 0:1] = dcb[...]
            sums[CORE, 1:2] = dpb[...]
            sums[CORE, 2:3] = dsb[...]
            for i in range(4):
                sums[CORE, 12 + i : 13 + i] = dub[:, i * width : (i + 1) * width]
            vec_copy(CORE).start()
        elif at < 3:
            vec_copy(kinds[at - 1]).wait_recv()
            sums[kinds[at]] = sums[kinds[at - 1]] + parts[kinds[at - 1]]
            vec_copy(kinds[at]).start()
        elif at == 3:
            vec_copy(YFLIP).wait_recv()
            total = sums[YFLIP] + parts[YFLIP]
            ends = (place.a > 0, place.a < place.n - 1)
            sums[UP] = total
            sums[DOWN] = total
            for kind, fed in ((UP, ends[0]), (DOWN, ends[1])):
                @pl.when(fed)
                def _(kind=kind):
                    vec_copy(kind).wait_recv()
                    sums[kind] = sums[kind] + parts[kind]

                @place.when(kind)
                def _(kind=kind):
                    vec_copy(kind).start()
        else:
            total = sums[UP] + sums[DOWN] - (sums[YFLIP] + parts[YFLIP])
            both = vec_out.shape[1]
            k = place.h * count + place.s
            mine = pltpu.roll(total, lax.rem(width - k * both, width), 1)
            vec_out[...] = mine[:, :both]
            wide = ub_out.shape[1]
            flat = k * wide
            lanes = lax.rem(flat, width)
            mine = pltpu.roll(total, lax.rem(width - lanes, width), 1)[:, :wide]
            row = lax.broadcasted_iota(jnp.int32, mine.shape, 0)
            ub_out[...] = jnp.sum(jnp.where(row == 12 + flat // width, mine, 0.0), axis=0, keepdims=True)
            for kind in range(5):
                @place.when(kind)
                def _(kind=kind):
                    vec_copy(kind).wait_send()

    main = scatter_steps(place, units, stores, between)
    low = scatter_steps(place, low_units, low_stores)
    far = place.n - 1

    def give(i):
        @pl.when(place.inside(i - 4 if i < 3 else -1))
        def _():
            rows_copy(i).start()

        @pl.when(jnp.logical_not(place.inside(4 - i if i < 3 else 1)))
        def _():
            if i < 3:
                returned[i * pad : (i + 1) * pad] = jnp.zeros((pad, width), BF)
            else:
                from_next[...] = jnp.zeros_like(from_next)

    for i in range(3):
        give(i)

    def compressed(tap):
        cols = slice(tap * width, (tap + 1) * width)
        spread[...] = mm(taps_scr[tap], returned[...]).astype(BF)
        more = mm(spread[...], sq_scr[:, cols])
        if tap:
            more = more + dmasked[...]
        dmasked[...] = more
        gsq[:, cols] = mm_tn(spread[...], masked_scr[...]).astype(BF)

    def run(steps):
        for step in steps:
            step()

    def part(steps, k):
        cuts = [0, 1, 2, 3, 4, 5, 5 + far, 5 + 2 * far, 6 + 2 * far, 6 + 3 * far, 7 + 3 * far]
        run(steps[cuts[k] : cuts[k + 1]])

    def load_all():
        for load in loads:
            load.start()

    def wait_all():
        for load in loads:
            load.wait()
        masked_scr[...] = kept_rows(masked_scr[...], window)
        for i in range(3):
            @pl.when(place.inside(4 - i))
            def _(i=i):
                rows_copy(i).wait_recv()

    def send_rows():
        @pl.when(place.inside(1))
        def _():
            rows_copy(3).wait_recv()

        spread[...] = (dbl_scr[...] + dcur_scr[...] + from_next[...].astype(F32) + kept_rows(dmasked[...], window)).astype(BF)
        exchange(1, spread, dx_out)

    for item in CLOSE_PLAN:
        if item[0] == "m":
            part(main, int(item[1:]))
        elif item[0] == "l":
            part(low, int(item[1:]))
        elif item[0] == "c":
            compressed(int(item[1:]))
        else:
            {"load": load_all, "wait": wait_all, "rows": send_rows, "out": lambda: exchange(0, outputs, rows_out), "memory": lambda: give(3)}[item[1:]]()
    for i in range(4):
        @pl.when(place.inside(i - 4 if i < 3 else -1))
        def _(i=i):
            rows_copy(i).wait_send()
    exchange(0, outputs, rows_out, True)
    exchange(1, spread, dx_out, True)


def close_layer(g, w, layout, dmade, dmem, dcur, dbl, masked, window, outputs):
    pad, taps, collect, biased = layout
    count = lax.axis_size("seq")
    rows, width = dbl.shape
    both = width // (2 * count)
    square = (width // count, width // 2)
    tall = w["sq"].shape[1]
    scratch = []
    for order in SCATTER_ORDERS:
        scratch += scatter_scratch(count, square, order)
    for at, size, order in block_scatters(both, 0):
        scratch += scatter_scratch(count, (size, tall), order)
    vmem = pl.BlockSpec(memory_space=pltpu.VMEM)
    any_spec = pl.BlockSpec(memory_space=pl.ANY)
    outs = pl.pallas_call(
        functools.partial(close_kernel, count),
        in_specs=[any_spec] * 5 + [vmem] * 5 + [any_spec] * 5 + [pl.BlockSpec(memory_space=pltpu.SMEM)] + [any_spec] * 2,
        out_specs=[vmem] * 7 + [any_spec] * 2,
        out_shape=[jax.ShapeDtypeStruct(square, F32)] * 4
        + [jax.ShapeDtypeStruct(s, F32) for s in ((both, tall), (16, both), (1, 4 * both))]
        + [jax.ShapeDtypeStruct((2, rows // 2, width), BF)] * 2,
        scratch_shapes=[
            pltpu.VMEM((5, 16, width), F32),
            pltpu.VMEM((5, 16, width), F32),
            pltpu.SemaphoreType.DMA((5,)),
            pltpu.SemaphoreType.DMA((5,)),
            pltpu.VMEM((3 * pad, width), BF),
            pltpu.VMEM((rows, width), BF),
            pltpu.VMEM((width, tall), BF),
            pltpu.VMEM((width, tall), BF),
            pltpu.VMEM((rows, width), F32),
            pltpu.VMEM((rows, width), F32),
            pltpu.VMEM((rows, width), BF),
            pltpu.VMEM((3, rows, 3 * pad), BF),
            pltpu.VMEM((rows, width), BF),
            pltpu.VMEM((rows, width), F32),
            pltpu.SemaphoreType.DMA((5,)),
            *[pltpu.SemaphoreType.DMA((4,))] * 2,
            *[pltpu.SemaphoreType.DMA((2,))] * 3,
            *scratch,
        ],
        compiler_params=pltpu.CompilerParams(collective_id=2, has_side_effects=True, vmem_limit_bytes=62 * MIB),
        name="close_layer",
    )(
        g["q"], g["k"], g["v"], g["p"], w["sq"], g["cb"], g["pb"], g["sb"], g["sums"], g["ub"],
        dmade, dmem, dcur, dbl, masked, window, jnp.asarray(taps), outputs,
    )
    final = dict(zip(("q", "k", "v", "p", "sq"), outs[:5]))
    final.update({n: outs[5][i] for i, n in enumerate(VECTORS)})
    final["ub"] = outs[6].reshape(4 * both)
    return final, outs[7], outs[8]


FORWARD_SHARE = 0.25


def attend_forward_kernel(
    count, window, vec_ref, in1_ref, both, table_ref, wq_ref, wk_ref, wv_ref, wp_ref,
    collect, made, up, down, o,
    out_ref, p_ref, cq_ref, pq_ref, k_ref, v_ref, pl_ref, in_t_ref, up_f, down_f, o_f,
    s_scr, x_scr, arriving, in0_ref, in2_ref, bias_ref, in_sem, row_send, row_recv, *sems,
):
    turn, turns = pl.program_id(0), pl.num_programs(0)
    place = Place(count)
    units = []
    for shard, full, first in ((up, up_f, 0), (down, down_f, 2), (o, o_f, 1)):
        units += block_units(shard, full, count, first)
    gather = Gather(place, units, *sems)
    first, *steps, last = gather.steps()
    heads = cq_ref.shape[1] // HD
    rows, keys = cq_ref.shape[0], k_ref.shape[0]
    width = in2_ref.shape[1]
    pad = arriving.shape[0] // 3
    scale = HD ** (-0.5)
    points = 2 + heads
    ahead = int(len(steps) * FORWARD_SHARE)
    early = spread_steps(steps[:ahead], 4)
    plan = [[]] * 2 + spread_steps(steps[ahead:], turns * points - 3) + [[]]

    def run(chosen):
        for step in chosen:
            step()

    def point(k):
        for t in range(turns):
            if t * points + k and plan[t * points + k - 1]:
                @pl.when(turn == t)
                def _(chosen=plan[t * points + k - 1]):
                    run(chosen)

    def rows_copy(i):
        here = pl.ds(i * pad, pad)
        return pltpu.make_async_remote_copy(
            src_ref=made.at[here],
            dst_ref=arriving.at[here],
            send_sem=row_send.at[i],
            recv_sem=row_recv.at[i],
            device_id=(place.h, place.s + 4 - i),
            device_id_type=MESH,
        )

    @pl.when(turn == 0)
    def _():
        load = pltpu.make_async_copy(both.at[place.h], in2_ref, in_sem)
        load.start()
        place.barrier(True)
        for i in range(3):
            @pl.when(place.inside(4 - i))
            def _(i=i):
                rows_copy(i).start()

            @pl.when(jnp.logical_not(place.inside(i - 4)))
            def _(i=i):
                arriving[i * pad : (i + 1) * pad] = jnp.zeros((pad, width), BF)

        first()
        bias_ref[...] = key_bias(rows, window)
        load.wait()

    point(0)
    query = mm(in2_ref[...], wq_ref[...])
    cq_ref[...] = ((query + vec_ref[0:1]) * scale).astype(BF)
    pq_ref[...] = ((query + vec_ref[1:2]) * scale).astype(BF)

    def project(i, source):
        here = slice(i * rows, (i + 1) * rows)
        k_ref[here] = mm(source[...], wk_ref[...]).astype(BF)
        v_ref[here] = mm(source[...], wv_ref[...]).astype(BF)

    def ahead_of_rows(k):
        @pl.when(turn == 0)
        def _():
            run(early[k])

    project(1, in1_ref)
    ahead_of_rows(0)
    project(2, in2_ref)
    ahead_of_rows(1)
    for i in range(3):
        here = slice(i * rows, (i + 1) * rows)
        pl_ref[here] = mm(table_ref[here], wp_ref[...]).astype(BF)
    ahead_of_rows(2)
    point(1)

    @pl.when(turn == 0)
    def _():
        run(early[3])
        for i in range(3):
            @pl.when(place.inside(i - 4))
            def _(i=i):
                rows_copy(i).wait_recv()
        in0_ref[...] = mm(collect[...], arriving[...]).astype(BF)

    project(0, in0_ref)
    for i, source in enumerate((in0_ref, in1_ref, in2_ref)):
        @pl.when(turn == i + 1)
        def _(source=source, here=slice(i * rows, (i + 1) * rows)):
            in_t_ref[:, here] = source[...].T
    step = 32
    for head in range(heads):
        point(2 + head)
        cols = slice(head * HD, (head + 1) * HD)
        s_scr[...] = mm_nt(cq_ref[:, cols], k_ref[:, cols])
        x_scr[...] = mm_nt(pq_ref[:, cols], pl_ref[:, cols])
        for start in range(0, rows, step):
            here = slice(start, start + step)
            located = pltpu.roll(x_scr[here], (start + keys - rows + 1) % keys, 1, stride=1, stride_axis=0)
            scores = s_scr[here] + located + bias_ref[...]
            early, own = scores[:, : 2 * rows], scores[:, 2 * rows :]
            row = start + lax.broadcasted_iota(jnp.int32, own.shape, 0)
            col = lax.broadcasted_iota(jnp.int32, own.shape, 1)
            own = jnp.where(col <= row, own, -1e30)
            top = jnp.maximum(jnp.max(early, axis=1, keepdims=True), jnp.max(own, axis=1, keepdims=True))
            early, own = jnp.exp(early - top), jnp.exp(own - top)
            total = jnp.sum(early, axis=1, keepdims=True) + jnp.sum(own, axis=1, keepdims=True)
            share = 1.0 / total
            p_ref[head, here, : 2 * rows] = (early * share).astype(BF)
            p_ref[head, here, 2 * rows :] = (own * share).astype(BF)
        out_ref[:, cols] = mm(p_ref[head], v_ref[:, cols]).astype(BF)

    @pl.when(turn == turns - 1)
    def _():
        for i in range(3):
            @pl.when(place.inside(4 - i))
            def _(i=i):
                rows_copy(i).wait_send()
        last()


def attend_forward(window, memory, inputs, made, table, layout, w, shards):
    pad, taps, collect, biased = layout
    count = lax.axis_size("seq")
    rows, width = memory.shape
    keys = 3 * rows
    pair = 2 * HD
    names = ("up", "down", "o")

    def whole(shape):
        return pl.BlockSpec(shape, lambda t: (0,) * len(shape), pipeline_mode=pl.Buffered(1))

    def columns(height):
        return pl.BlockSpec((height, pair), lambda t: (0, t))

    any_spec = pl.BlockSpec(memory_space=pl.ANY)
    outs = pl.pallas_call(
        functools.partial(attend_forward_kernel, count),
        grid=(width // pair,),
        in_specs=[pl.BlockSpec(memory_space=pltpu.SMEM), columns(16), whole((rows, width)), any_spec, whole((keys, width))]
        + [columns(width)] * 4
        + [whole((rows, 3 * pad))]
        + [any_spec] * 4,
        out_specs=[columns(rows), pl.BlockSpec((2, rows, keys), lambda t: (t, 0, 0))]
        + [columns(rows)] * 2
        + [columns(keys)] * 3
        + [pl.BlockSpec((width, keys), lambda t: (0, 0))]
        + [any_spec] * 3,
        out_shape=[
            jax.ShapeDtypeStruct((rows, width), BF),
            jax.ShapeDtypeStruct((width // HD, rows, keys), BF),
            *[jax.ShapeDtypeStruct((rows, width), BF)] * 2,
            *[jax.ShapeDtypeStruct((keys, width), BF)] * 3,
            jax.ShapeDtypeStruct((width, keys), BF),
            *[jax.ShapeDtypeStruct((shards[n].shape[0] * 2 * count, width), BF) for n in names],
        ],
        scratch_shapes=[
            pltpu.VMEM((rows, keys), F32),
            pltpu.VMEM((rows, keys), F32),
            pltpu.VMEM((3 * pad, width), BF),
            *[pltpu.VMEM((rows, width), BF)] * 2,
            pltpu.VMEM((1, keys), F32),
            pltpu.SemaphoreType.DMA,
            pltpu.SemaphoreType.DMA((3,)),
            pltpu.SemaphoreType.DMA((3,)),
            *gather_semaphores(count, sum(len(halves(shards[n].shape[0])) for n in names)),
        ],
        compiler_params=pltpu.CompilerParams(collective_id=3, has_side_effects=True, vmem_limit_bytes=62 * MIB),
        name="attend_forward",
    )(
        window, w["vec"], memory, inputs, table, w["q"], w["k"], w["v"], w["p"],
        jnp.asarray(collect), made, *[shards[n] for n in names],
    )
    return outs[:8], dict(zip(names, outs[8:]))


BACKWARD_PLAN = (
    (0, 0), (0, 1), (0, 2), (1, 1), (1, 2),
    (3, 0), (3, 3), (4, 1),
    (4, 2), (5, 1), (5, 3),
    (6, 0),
    (6, 2), (7, 0), (7, 3),
)


def attend_backward_kernel(
    count, cq_ref, pq_ref, k_ref, v_ref, pl_ref, p_ref, do_ref, in_t_ref, table_t_ref, wq_ref, wk_ref, wv_ref, collect_t, up, down, o,
    dcb_ref, dpb_ref, gq_ref, gk_ref, gv_ref, gp_ref, dsb_ref, dmade_ref, up_out, down_out, o_out, dmem_out, dcur_out,
    dp_scr, ds_scr, dq_scr, dk_scr, dv_scr, dpl_scr, total, out_sem, *scratch,
):
    head, heads = pl.program_id(0), pl.num_programs(0)
    place = Place(count)
    units, stores = scatter_dense_units(place, count, (up, down, o), (up_out, down_out, o_out), scratch)
    first, *steps, last = scatter_steps(place, units, stores)
    plan = {at: [] for at in BACKWARD_PLAN}
    plan[BACKWARD_PLAN[0]] = [place.barrier, first]
    for i, step in enumerate(steps):
        plan[BACKWARD_PLAN[min(1 + i * (len(BACKWARD_PLAN) - 1) // len(steps), len(BACKWARD_PLAN) - 1)]].append(step)

    def point(k):
        for (t, at), chosen in plan.items():
            if at == k:
                @pl.when(head == t)
                def _(chosen=chosen):
                    for step in chosen:
                        step()

    rows, keys = cq_ref.shape[0], k_ref.shape[0]
    scale = HD ** (-0.5)
    block = 128
    flip = (
        lax.broadcasted_iota(jnp.int32, (block, block), 0)
        + lax.broadcasted_iota(jnp.int32, (block, block), 1)
        == block - 1
    ).astype(BF)
    point(0)
    dp_scr[...] = mm_nt(do_ref[...], v_ref[...])
    step = 32
    for start in range(0, rows, step):
        here = slice(start, start + step)
        prob = p_ref[0, here].astype(F32)
        dprob = dp_scr[here]
        delta = jnp.sum(prob * dprob, axis=1, keepdims=True)
        ds_scr[here] = (prob * (dprob - delta)).astype(BF)
    point(1)
    side = head % 2
    dv_scr[side] = mm_tn(do_ref[...], p_ref[0]).T.astype(BF)
    dk_scr[side] = mm_tn(cq_ref[...], ds_scr[...]).T.astype(BF)
    dcq = mm(ds_scr[...], k_ref[...]) * scale
    flipped = []
    for start in range(0, rows, block):
        here = slice(start, start + block)
        dp_scr[here] = mm(flip, ds_scr[here])
        flipped.append(mm(flip, pq_ref[here]).astype(BF))
        ds_scr[here] = pltpu.roll(dp_scr[here], rows - block - start, 1, stride=1, stride_axis=0).astype(BF)
    dpl_scr[side] = mm_tn(jnp.concatenate(flipped, axis=0), ds_scr[...]).T.astype(BF)
    dpq_flipped = mm(ds_scr[...], pl_ref[...]) * scale
    dpq = []
    for start in range(0, rows, block):
        piece = dpq_flipped[start : start + block]
        high = piece.astype(BF)
        dpq.append(mm(flip, high) + mm(flip, (piece - high.astype(F32)).astype(BF)))
    dpq = jnp.concatenate(dpq, axis=0)
    dq_scr[side] = (dcq + dpq).astype(BF)
    dcb_ref[...] = jnp.sum(dcq, axis=0, keepdims=True)
    dpb_ref[...] = jnp.sum(dpq, axis=0, keepdims=True)
    point(2)

    @pl.when(side == 1)
    def _():
        dq, dk, dv, dpl = (jnp.concatenate([ref[0], ref[1]], axis=1) for ref in (dq_scr, dk_scr, dv_scr, dpl_scr))
        gk_ref[...] = mm(in_t_ref[...], dk).astype(BF)
        gv_ref[...] = mm(in_t_ref[...], dv).astype(BF)
        gp_ref[...] = mm(table_t_ref[...], dpl).astype(BF)
        gq_ref[...] = mm(in_t_ref[:, 2 * rows :], dq).astype(BF)
        point(3)

        @pl.when(head == 1)
        def _():
            total[...] = jnp.zeros_like(total)

        for start in range(0, keys, rows):
            here = slice(start, start + rows)
            more = mm_nt(dk[here], wk_ref[...]) + mm_nt(dv[here], wv_ref[...])
            if start == 2 * rows:
                more = more + mm_nt(dq, wq_ref[...])
            total[here] += more

    width = total.shape[1]

    @pl.when(head == heads - 1)
    def _():
        own = pltpu.make_async_copy(total.at[pl.ds(2 * rows, rows)], dcur_out, out_sem.at[0])
        own.start()
        ds_scr[:, :width] = total[rows : 2 * rows].astype(BF)
        back = pltpu.make_async_copy(ds_scr.at[:, pl.ds(0, width)], dmem_out, out_sem.at[1])
        back.start()
        dsq = total[:rows].astype(BF)
        dsb_ref[...] = jnp.sum(dsq.astype(F32), axis=0, keepdims=True)
        dmade_ref[...] = mm(collect_t[...], dsq).astype(BF)
        last()
        own.wait()
        back.wait()


def attend_backward(saved, probs, d_out, inputs_t, table_t, layout, w, dense):
    pad, taps, collect, biased = layout
    count = lax.axis_size("seq")
    rows, width = d_out.shape
    keys = inputs_t.shape[1]
    heads = width // HD
    names = ("up", "down", "o")
    shapes = [(dense[n].shape[0] // (2 * count), width) for n in names]

    def whole(shape):
        return pl.BlockSpec(shape, lambda h: (0,) * len(shape), pipeline_mode=pl.Buffered(1))

    def columns(height):
        return pl.BlockSpec((height, HD), lambda h: (0, h))

    pair = pl.BlockSpec((width, 2 * HD), lambda h: (0, h // 2))
    any_spec = pl.BlockSpec(memory_space=pl.ANY)
    vmem = pl.BlockSpec(memory_space=pltpu.VMEM)
    outs = pl.pallas_call(
        functools.partial(attend_backward_kernel, count),
        grid=(heads,),
        in_specs=[columns(rows)] * 2
        + [columns(keys)] * 3
        + [pl.BlockSpec((1, rows, keys), lambda h: (h, 0, 0)), columns(rows), whole((width, keys)), whole((width, keys))]
        + [pair] * 3
        + [whole((3 * pad, rows))]
        + [any_spec] * 3,
        out_specs=[columns(1)] * 2 + [pair] * 4 + [pl.BlockSpec((1, width), lambda h: (0, 0)), vmem] + [vmem] * 3 + [any_spec] * 2,
        out_shape=[
            *[jax.ShapeDtypeStruct((1, width), F32)] * 2,
            *[jax.ShapeDtypeStruct((width, width), BF)] * 4,
            jax.ShapeDtypeStruct((1, width), F32),
            jax.ShapeDtypeStruct((3 * pad, width), BF),
            *[jax.ShapeDtypeStruct(shape, F32) for shape in shapes],
            jax.ShapeDtypeStruct((rows, width), BF),
            jax.ShapeDtypeStruct((rows, width), F32),
        ],
        scratch_shapes=[
            pltpu.VMEM((rows, keys), F32),
            pltpu.VMEM((rows, keys), BF),
            pltpu.VMEM((2, rows, HD), BF),
            *[pltpu.VMEM((2, keys, HD), BF)] * 3,
            pltpu.VMEM((keys, width), F32),
            pltpu.SemaphoreType.DMA((2,)),
            *scatter_dense_scratch(count, shapes),
        ],
        compiler_params=pltpu.CompilerParams(collective_id=1, has_side_effects=True, vmem_limit_bytes=62 * MIB),
        name="attend_backward",
    )(
        *saved, probs, d_out, inputs_t, table_t, w["q"], w["k"], w["v"],
        jnp.asarray(np.ascontiguousarray(collect.T)), *[dense[n] for n in names],
    )
    grads = dict(zip(("cb", "pb", "q", "k", "v", "p", "sb"), outs))
    return grads, dict(zip(names, outs[8:11])), (outs[7], *outs[11:])


def normalize(values):
    centre = values - jnp.mean(values, axis=-1, keepdims=True)
    spread = jnp.mean(centre * centre, axis=-1, keepdims=True)
    scale = lax.rsqrt(spread + epsilon)
    return centre * scale, scale


def normalize_back(grad, gain, unit, scale):
    pulled = grad * gain
    return scale * (
        pulled
        - jnp.mean(pulled, axis=-1, keepdims=True)
        - unit * jnp.mean(pulled * unit, axis=-1, keepdims=True)
    )


def gelu_parts(u):
    root = np.float32(np.sqrt(2.0 / np.pi))
    square = u * u
    tanh = jnp.tanh(u * (root + (root * 0.044715) * square))
    half = 0.5 * u
    value = half + half * tanh
    slope = 0.5 + 0.5 * tanh + half * (1.0 - tanh * tanh) * (root + (3 * 0.044715 * root) * square)
    return value, slope


VECTORS = ("cb", "pb", "sb", "ob", "g1", "s1", "db", "g2", "s2")


def feed_kernel(
    att_ref, x_all, ct_all, wo_ref, up_ref, down_ref, ub_ref, vec_ref,
    out_ref, gup_ref, gdown_ref, go_ref, dub_ref, sums_ref, dbl_ref, datt_ref,
    unit, scale, normed, acc, hidden, slope, dy, dy_low, x_ref, ct_ref, load_sem,
):
    turn = pl.program_id(0)
    chunks = pl.num_programs(0) // 2
    rows = att_ref.shape[0]
    at = {name: slice(i, i + 1) for i, name in enumerate(VECTORS)}

    def by_rows(run):
        repeat(rows // 128, lambda k: run(pl.ds(pl.multiple_of(k * 128, 128), 128)))

    def tally(name, values):
        sums_ref[at[name]] += jnp.sum(values, axis=0, keepdims=True)

    book = lax.axis_index("head")
    x_load = pltpu.make_async_copy(x_all.at[book], x_ref, load_sem.at[0])
    ct_load = pltpu.make_async_copy(ct_all.at[book], ct_ref, load_sem.at[1])

    @pl.when(turn == 0)
    def _():
        x_load.start()
        ct_load.start()
        sums_ref[...] = jnp.zeros_like(sums_ref)
        acc[...] = mm(att_ref[...], wo_ref[...])
        x_load.wait()

        def first(here):
            unit[here], scale[here] = normalize(x_ref[here].astype(F32) + acc[here] + vec_ref[at["ob"]])
            normed[here] = (unit[here] * vec_ref[at["g1"]] + vec_ref[at["s1"]]).astype(BF)
            acc[here] = jnp.zeros_like(acc[here])

        by_rows(first)

    @pl.when(turn < chunks)
    def _():
        value, slope_here = gelu_parts(mm_nt(normed[...], up_ref[...]) + ub_ref[...])
        hidden[turn] = value.astype(BF)
        slope[turn] = slope_here.astype(BF)
        acc[...] += mm(hidden[turn], down_ref[...])

    @pl.when(turn == chunks - 1)
    def _():
        ct_load.wait()

        def second(here):
            unit2, scale2 = normalize(normed[here].astype(F32) + acc[here] + vec_ref[at["db"]])
            out_ref[here] = (unit2 * vec_ref[at["g2"]] + vec_ref[at["s2"]]).astype(BF)
            ct = ct_ref[here].astype(F32)
            tally("g2", ct * unit2)
            tally("s2", ct)
            dy[here] = normalize_back(ct, vec_ref[at["g2"]], unit2, scale2)
            tally("db", dy[here])
            dy_low[here] = dy[here].astype(BF)
            acc[here] = jnp.zeros_like(acc[here])

        by_rows(second)

    @pl.when(turn >= chunks)
    def _():
        j = 2 * chunks - 1 - turn
        gdown_ref[...] = mm_tn(hidden[j], dy_low[...]).astype(BF)
        du = (mm_nt(dy_low[...], down_ref[...]) * slope[j].astype(F32)).astype(BF)
        dub_ref[...] = jnp.sum(du.astype(F32), axis=0, keepdims=True)
        gup_ref[...] = mm_tn(du, normed[...]).astype(BF)
        acc[...] += mm(du, up_ref[...])

    @pl.when(turn == 2 * chunks - 1)
    def _():
        def third(here):
            dnormed = dy[here] + acc[here]
            tally("g1", dnormed * unit[here])
            tally("s1", dnormed)
            dbl = normalize_back(dnormed, vec_ref[at["g1"]], unit[here], scale[here])
            tally("ob", dbl)
            dbl_ref[here] = dbl
            dy_low[here] = dbl.astype(BF)

        by_rows(third)
        go_ref[...] = mm_tn(att_ref[...], dy_low[...]).astype(BF)
        datt_ref[...] = mm_nt(dy_low[...], wo_ref[...]).astype(BF)


def feed(attended, x, ct, w):
    rows, width = attended.shape
    hidden = w["up"].shape[0]
    size = 1024
    chunks = hidden // size

    def whole(shape):
        return pl.BlockSpec(shape, lambda t: (0,) * len(shape), pipeline_mode=pl.Buffered(1))

    def kept(shape):
        return pl.BlockSpec(shape, lambda t: (0,) * len(shape))

    def weight(t):
        return jnp.where(t < chunks, t, 2 * chunks - 1 - t)

    def grad(t):
        return jnp.where(t < chunks, chunks - 1, 2 * chunks - 1 - t)

    outs = pl.pallas_call(
        feed_kernel,
        grid=(2 * chunks,),
        in_specs=[whole((rows, width))]
        + [pl.BlockSpec(memory_space=pl.ANY)] * 2
        + [whole((width, width))]
        + [pl.BlockSpec((size, width), lambda t: (weight(t), 0))] * 2
        + [pl.BlockSpec((1, size), lambda t: (0, weight(t))), whole((16, width))],
        out_specs=[kept((rows, width))]
        + [pl.BlockSpec((size, width), lambda t: (grad(t), 0))] * 2
        + [kept((width, width)), pl.BlockSpec((1, size), lambda t: (0, grad(t))), kept((16, width))]
        + [kept((rows, width))] * 2,
        out_shape=[
            jax.ShapeDtypeStruct((rows, width), BF),
            *[jax.ShapeDtypeStruct((hidden, width), BF)] * 2,
            jax.ShapeDtypeStruct((width, width), BF),
            jax.ShapeDtypeStruct((1, hidden), F32),
            jax.ShapeDtypeStruct((16, width), F32),
            jax.ShapeDtypeStruct((rows, width), F32),
            jax.ShapeDtypeStruct((rows, width), BF),
        ],
        scratch_shapes=[
            pltpu.VMEM((rows, width), F32),
            pltpu.VMEM((rows, 1), F32),
            pltpu.VMEM((rows, width), BF),
            pltpu.VMEM((rows, width), F32),
            pltpu.VMEM((chunks, rows, size), BF),
            pltpu.VMEM((chunks, rows, size), BF),
            pltpu.VMEM((rows, width), F32),
            *[pltpu.VMEM((rows, width), BF)] * 3,
            pltpu.SemaphoreType.DMA((2,)),
        ],
        compiler_params=pltpu.CompilerParams(vmem_limit_bytes=62 * MIB),
        name="feed",
    )(attended, x, ct, w["o"], w["up"], w["down"], w["ub"], w["vec"])
    outputs, gup, gdown, go, dub, sums, dbl, datt = outs
    return outputs, dict(up=gup, down=gdown, o=go, ub=dub, sums=sums), dbl, datt


def results_kernel(*refs):
    count = (len(refs) - 2) // 3
    sources, targets, blocks = (refs[i * count : (i + 1) * count] for i in range(3))
    turned, sem = refs[3 * count :]
    for i in range(count):
        pltpu.make_async_copy(sources[i], blocks[i], sem.at[i]).start()
    for i in range(count):
        pltpu.make_async_copy(sources[i], blocks[i], sem.at[i]).wait()
        if not i:
            turned[...] = blocks[0][...].T
        pltpu.make_async_copy(blocks[i] if i else turned, targets[i], sem.at[i]).start()
    for i in range(count):
        pltpu.make_async_copy(blocks[i] if i else turned, targets[i], sem.at[i]).wait()


def results(first, rest):
    any_spec = pl.BlockSpec(memory_space=pl.ANY)
    arrays = [first, *rest]
    shapes = [first.shape[::-1], *[a.shape for a in rest]]
    return pl.pallas_call(
        results_kernel,
        in_specs=[any_spec] * len(arrays),
        out_specs=[any_spec] * len(arrays),
        out_shape=[jax.ShapeDtypeStruct(shape, a.dtype) for shape, a in zip(shapes, arrays)],
        scratch_shapes=[
            *[pltpu.VMEM(a.shape, a.dtype) for a in arrays],
            pltpu.VMEM(first.shape[::-1], first.dtype),
            pltpu.SemaphoreType.DMA((len(arrays),)),
        ],
        compiler_params=pltpu.CompilerParams(vmem_limit_bytes=62 * MIB),
        name="results",
    )(*arrays)


def body(
    inputs, lengths,
    query_weight, key_weight, value_weight, position_weight, content_bias, position_bias,
    output_weight, output_bias, first_gain, first_shift, up_weight, up_bias, down_weight, down_bias,
    second_gain, second_shift, squeeze_weight, squeeze_bias, cotangent,
):
    seq = lax.axis_index("seq")
    head = lax.axis_index("head")
    rows, width = inputs.shape[2:]

    book_lengths = lax.dynamic_index_in_dim(lengths, head, 0, keepdims=False)
    padded_lengths = jnp.concatenate([jnp.zeros((4,), jnp.int32), book_lengths])
    window = lax.dynamic_slice_in_dim(padded_lengths, seq, 5, 0)
    x = inputs[:, 0]
    layout = squeeze_layout(rows)
    shards = dict(
        q=query_weight, k=key_weight, v=value_weight, p=position_weight,
        o=output_weight, up=up_weight.T, down=down_weight, sq=squeeze_weight.T,
        cb=content_bias, pb=position_bias, ob=output_bias, g1=first_gain, s1=first_shift, ub=up_bias,
        db=down_bias, g2=second_gain, s2=second_shift, sb=squeeze_bias,
    )
    w, made, memory = open_layer(shards, x, window, layout)

    table = table_rows(width, 3 * rows)
    (attended, probs, *saved, keys_in_t), dense = attend_forward(
        window, memory, x, made, jnp.asarray(table), layout, w, shards
    )
    w.update(dense)

    outputs, grads, dblended, dattended = feed(attended, x, cotangent[:, 0], w)

    more, final, (dmade, dmemory, dcurrent) = attend_backward(
        saved, probs, dattended, keys_in_t, jnp.asarray(np.ascontiguousarray(table.T)), layout, w, grads
    )
    more, input_rows, output_rows = close_layer(
        {**grads, **more}, w, layout, dmade, dmemory, dcurrent, dblended, x, window, outputs
    )
    final.update(more)
    names = ("down", "o", "q", "k", "v", "p", "sq")
    final["up"], output_rows, input_rows, *rest = results(final["up"], [output_rows, input_rows, *[final[n] for n in names]])
    final.update(zip(names, rest))
    return (
        output_rows[:, None], input_rows[:, None],
        final["q"], final["k"], final["v"], final["p"], final["cb"], final["pb"],
        final["o"], final["ob"], final["g1"], final["s1"], final["up"], final["ub"],
        final["down"], final["db"], final["g2"], final["s2"], final["sq"].T, final["sb"],
    )


def solution(mesh):
    both = ("head", "seq")
    matrix = P("seq", "head")
    in_specs = (
        P(None, "seq", None, None), P(), matrix, matrix, matrix, matrix, P(both), P(both),
        P(both, None), P("seq"), P("seq"), P("seq"), P(None, both), P(both), P(both, None), P("seq"),
        P("seq"), P("seq"), P(None, both), P(both), P(None, "seq", None, None),
    )
    rows = P(None, "seq", "head", None)
    out_specs = (
        rows, rows, matrix, matrix, matrix, matrix, P(both), P(both),
        P(both, None), P(both), P(both), P(both), P(None, both), P(both), P(both, None), P(both),
        P(both), P(both), P(None, both), P(both),
    )
    return jax.shard_map(body, mesh=mesh, in_specs=in_specs, out_specs=out_specs, check_vma=False)
```

```python
import functools

import jax
import jax.numpy as jnp
import numpy as np
from jax import lax
from jax.experimental import pallas as pl
from jax.experimental.pallas import tpu as pltpu
from jax.sharding import PartitionSpec as P

HD = 128
BF = jnp.bfloat16
F32 = jnp.float32
epsilon = 1e-05
MIB = 1024 * 1024


def mm(left, right, contract=((1,), (0,)), out=F32):
    return lax.dot_general(left, right, (contract, ((), ())), preferred_element_type=F32).astype(out)


def mm_nt(left, right, out=F32):
    return mm(left, right, ((1,), (1,)), out)


def mm_tn(left, right, out=F32):
    return mm(left, right, ((0,), (0,)), out)


def table_rows(width, count):
    distance = np.arange(count - 1, -1, -1).astype(np.float32)[:, None]
    exponent = -np.arange(0, width, 2).astype(np.float32) / np.float32(width)
    frequency = np.power(np.float32(10000.0), exponent).astype(np.float32)
    angles = (distance * frequency[None, :]).astype(np.float32)
    return np.concatenate([np.sin(angles), np.cos(angles)], axis=1).astype(BF)


def squeeze_layout(rows):
    pad = -(-(rows // 3 + 2) // 16) * 16
    taps = np.zeros((3, rows, 3 * pad), np.float32)
    collect = np.zeros((rows, 3 * pad), np.float32)
    biased = np.zeros((3 * pad, 1), np.float32)
    for role in range(3):
        first = role * rows // 3
        for i in range(rows):
            flat = role * rows + i
            taps[flat % 3, i, role * pad + flat // 3 - first] = 1.0
            collect[flat // 3, role * pad + flat // 3 - first] = 1.0
        for c in range(first, ((role + 1) * rows - 1) // 3 + 1):
            if role == 0 or 3 * c >= role * rows:
                biased[role * pad + c - first] = 1.0
    return pad, taps.astype(BF), collect.astype(BF), biased


MESH = pl.DeviceIdType.MESH
CORE, XFLIP, YFLIP, UP, DOWN = range(5)


def repeat(count, run):
    def body(i, carry):
        run(i)
        return carry

    lax.fori_loop(0, count, body, 0)


class Place:
    def __init__(self, count):
        self.count = count
        self.n = count // 4
        self.h = lax.axis_index("head")
        self.s = lax.axis_index("seq")
        self.a = self.s // 4
        self.b = (self.s // 2) % 2
        self.c = self.s % 2

    def seq_of(self, a, b, c):
        return a * 4 + b * 2 + c

    def neighbour(self, kind):
        s, h = self.s, self.h
        if kind == CORE:
            return (h, s + 1 - 2 * self.c)
        if kind == XFLIP:
            return (h, s + 2 - 4 * self.b)
        if kind == YFLIP:
            return (1 - h, s)
        return (h, s + 4) if kind == UP else (h, s - 4)

    def when(self, kind):
        if kind == UP:
            return pl.when(self.a < self.n - 1)
        if kind == DOWN:
            return pl.when(self.a > 0)
        return lambda run: run()

    def far(self):
        s, count = self.s, self.count
        for by, other in ((1, self.c == 1), (-1, self.c == 0), (2, self.b == 1), (-2, self.b == 0), (3, None), (-3, None)):
            inside = self.inside(by)
            yield by, inside if other is None else jnp.logical_and(inside, other)

    def inside(self, by):
        return self.s + by < self.count if by > 0 else self.s + by >= 0

    def barrier(self, shifts=False):
        barrier = pltpu.get_barrier_semaphore()
        for kind in range(5):
            @self.when(kind)
            def _(kind=kind):
                pl.semaphore_signal(barrier, inc=1, device_id=self.neighbour(kind), device_id_type=MESH)
        peers = 5 - jnp.where(self.a == 0, 1, 0) - jnp.where(self.a == self.n - 1, 1, 0)
        if shifts:
            for by, there in self.far():
                @pl.when(there)
                def _(by=by):
                    pl.semaphore_signal(barrier, inc=1, device_id=(self.h, self.s + by), device_id_type=MESH)
                peers = peers + jnp.where(there, 1, 0)
        pl.semaphore_wait(barrier, peers)

    def along(self, i):
        return (self.a + self.n // 2 + i) % self.n


class Gather:
    def __init__(self, place, units, local_sem, send_sem, recv_sem):
        self.place, self.units = place, units
        self.local_sem, self.send_sem, self.recv_sem = local_sem, send_sem, recv_sem

    def view(self, u, h, s):
        shard, full, view, order = self.units[u]
        return view(full, h, s)

    def copy(self, u, kind, h, s, own=False):
        n = self.place.n
        a, b = s // 4, (s // 2) % 2
        order = self.units[u][3]
        other = b if order.index("x") < order.index("z") else h
        sent = {
            UP: other * n + a,
            DOWN: (2 + other) * n + a,
            XFLIP: (4 + h) * n + a,
            YFLIP: (6 + b) * n + a,
            CORE: (8 + h * 2 + b) * n + a,
        }[kind]
        there = self.view(u, h, s)
        return pltpu.make_async_remote_copy(
            src_ref=self.units[u][0] if own else there,
            dst_ref=there,
            send_sem=self.send_sem.at[u, sent],
            recv_sem=self.recv_sem.at[u, h * self.place.count + s],
            device_id=self.place.neighbour(kind),
            device_id_type=MESH,
        )

    def local(self, u):
        return pltpu.make_async_copy(self.units[u][0], self.view(u, self.place.h, self.place.s), self.local_sem.at[u])

    def sources(self):
        found = []
        for t in range(self.place.n):
            for sign in ((1, -1) if t else (0,)):
                for x in (0, 1):
                    for y in (0, 1):
                        if t or x or y:
                            found.append((t, sign, x, y))
        return sorted(found, key=lambda e: e[0] + 2 * (e[2] + e[3]))

    def onward(self, u, sign, x, y):
        order = self.units[u][3]
        moved = {"x": x, "y": y, "z": sign}
        last = max([i for i in range(3) if moved[order[i]]], default=-1)
        kinds = []
        if last >= 0 and order[last] == "z":
            kinds.append(UP if sign > 0 else DOWN)
        for dim in order[last + 1 :]:
            kinds += {"x": [XFLIP], "y": [YFLIP], "z": [UP, DOWN]}[dim]
        return kinds + [CORE]

    def send(self, u, kind, h, s, own, wait):
        @self.place.when(kind)
        def _():
            copy = self.copy(u, kind, h, s, own)
            if wait:
                copy.wait_send()
            else:
                copy.start()

    def begin(self, wait=False):
        p = self.place
        for u in range(len(self.units)):
            for kind in self.onward(u, 0, 0, 0):
                self.send(u, kind, p.h, p.s, True, wait)
        if not wait:
            for u in range(len(self.units)):
                self.local(u).start()

    def pass_on(self, entry, wait=False):
        p = self.place
        t, sign, x, y = entry
        a = p.a - sign * t
        h = 1 - p.h if y else p.h
        s = p.seq_of(a, 1 - p.b if x else p.b, p.c)

        def run():
            for u in range(len(self.units)):
                if not wait:
                    self.copy(u, CORE, h, s).wait_recv()
                for kind in self.onward(u, sign, x, y):
                    self.send(u, kind, h, s, False, wait)

        if t:
            pl.when(jnp.logical_and(a >= 0, a <= p.n - 1))(run)
        else:
            run()

    def arrived(self):
        p = self.place

        def core(i):
            h, a, b = i // (2 * p.n), i // 2 % p.n, i % 2
            for u in range(len(self.units)):
                self.copy(u, CORE, h, p.seq_of(a, b, 1 - p.c)).wait_recv()

        repeat(4 * p.n, core)
        for u in range(len(self.units)):
            self.local(u).wait()

    def sent(self):
        self.begin(True)
        for entry in self.sources():
            self.pass_on(entry, True)

    def finish(self):
        self.arrived()
        self.sent()

    def steps(self):
        return [self.begin] + [functools.partial(self.pass_on, entry) for entry in self.sources()] + [self.finish]


GATHER_ORDERS = ("yzx", "xzy", "zxy", "zyx")


def halves(rows):
    return [(0, rows // 2), (rows // 2, rows // 2)] if rows % 32 == 0 else [(0, rows)]


def block_units(shard, full, count, first):
    rows = shard.shape[0]
    units = []
    for i, (at, size) in enumerate(halves(rows)):
        def view(ref, h, s, at=at, size=size):
            return ref.at[pl.ds(pl.multiple_of((h * count + s) * rows + at, size), size)]

        units.append((shard.at[pl.ds(at, size)], full, view, GATHER_ORDERS[(first + i) % 4]))
    return units


def square_unit(shard, full, order):
    r, w = shard.shape

    def view(ref, h, s):
        return ref.at[pl.ds(pl.multiple_of(s * r, r), r), pl.ds(pl.multiple_of(h * w, w), w)]

    return (shard, full, view, order)


def kept_rows(rows, window):
    at = lax.broadcasted_iota(jnp.int32, rows.shape, 0)
    return jnp.where(at < window[4], rows.astype(F32), 0.0).astype(rows.dtype)


def key_bias(rows, window):
    key = lax.broadcasted_iota(jnp.int32, (1, 3 * rows), 1)
    flat = 3 * key
    source = jnp.where(flat >= 2 * rows, 2, jnp.where(flat >= rows, 1, 0))
    source = jnp.where(key >= 2 * rows, 4, jnp.where(key >= rows, 3, source))
    first = jnp.where(key >= 2 * rows, 2 * rows, jnp.where(key >= rows, rows, source * rows))
    limit = sum(jnp.where(source == i, window[i], 0) for i in range(5))
    return jnp.where(jnp.where(key < rows, flat, key) - first < limit, 0.0, -1e30)


def open_kernel(
    count, small_names, q, k, v, p, sq, small, both, taps_t, window, biased,
    q_f, k_f, v_f, p_f, sq_f, vec, vec_up, made_out, memory,
    small_f, taps_scr, x_scr, sq_scr, grouped, made, load_sem, row_send, row_recv, *sems,
):
    place = Place(count)
    place.barrier(True)
    rows, width = x_scr.shape
    x = both.at[place.h]

    def small_view(ref, h, s):
        return ref.at[pl.ds(pl.multiple_of((h * count + s) * 8, 8), 8)]

    early = Gather(place, block_units(sq, sq_f, count, 0) + [(small, small_f, small_view, "zxy")], *sems[:3])
    late = Gather(
        place, [square_unit(*pair, GATHER_ORDERS[i]) for i, pair in enumerate(((q, q_f), (k, k_f), (v, v_f), (p, p_f)))], *sems[3:]
    )
    rows_copy = pltpu.make_async_remote_copy(
        src_ref=x,
        dst_ref=memory,
        send_sem=row_send,
        recv_sem=row_recv,
        device_id=(place.h, place.s + 1),
        device_id_type=MESH,
    )
    loads = [
        pltpu.make_async_copy(source, target, load_sem.at[i])
        for i, (source, target) in enumerate(((taps_t, taps_scr), (x, x_scr), (sq_f, sq_scr)))
    ]
    early.begin()
    late.begin()

    @pl.when(place.inside(1))
    def _():
        rows_copy.start()

    loads[0].start()
    loads[1].start()
    blank = pltpu.make_async_copy(made_out.at[pl.ds(0, rows)], memory, load_sem.at[3])

    @pl.when(place.s == 0)
    def _():
        made_out[...] = jnp.zeros_like(made_out)
        blank.start()
        blank.wait()

    loads[0].wait()
    loads[1].wait()
    x_scr[...] = kept_rows(x_scr[...], window)
    entries = early.sources()

    def group(tap):
        grouped[tap] = mm(taps_scr[tap], x_scr[...]).astype(BF)

    def square(tap):
        more = mm_nt(grouped[tap], sq_scr[:, tap * width : (tap + 1) * width])
        if tap:
            made[...] += more
        else:
            made[...] = more + biased[...] * vec[2:3]

    def unpack():
        for slot in range(2 * count):
            for name, row, at, size, target in small_names:
                if size * 2 * count > vec.shape[1] * (4 if name == "ub" else 1) and slot >= count:
                    continue
                ref = vec_up if name == "ub" else vec
                ref[target : target + 1, slot * size : (slot + 1) * size] = small_f[slot * 8 + row : slot * 8 + row + 1, at : at + size]

    lag = len(entries) // OPEN_LAG
    for i, entry in enumerate(entries):
        early.pass_on(entry)
        if i >= lag:
            late.pass_on(entries[i - lag])
        if i < 3:
            group(i)
    early.arrived()
    loads[2].start()
    unpack()
    loads[2].wait()
    rest = spread_steps([functools.partial(late.pass_on, entry) for entry in entries[len(entries) - lag :]], 3)
    for tap in range(3):
        for step in rest[tap]:
            step()
        square(tap)
    made_out[...] = made[...].astype(BF)
    late.arrived()

    @pl.when(place.inside(-1))
    def _():
        rows_copy.wait_recv()

    @pl.when(place.inside(1))
    def _():
        rows_copy.wait_send()

    early.sent()
    late.sent()


def spread_steps(steps, points):
    out = [[] for _ in range(points)]
    for i, step in enumerate(steps):
        out[i * points // len(steps)].append(step)
    return out


OPEN_LAG = 2


def gather_semaphores(count, units):
    return [
        pltpu.SemaphoreType.DMA((units,)),
        pltpu.SemaphoreType.DMA((units, 12 * (count // 4))),
        pltpu.SemaphoreType.DMA((units, 2 * count)),
    ]


def small_layout(both, seq):
    names = []
    for i, name in enumerate(("cb", "pb", "sb")):
        names.append((name, 0, i * both, both, i))
    names.append(("ub", 1, 0, 4 * both, 0))
    for i, name in enumerate(("ob", "g1", "s1", "db", "g2", "s2")):
        names.append((name, 2 + i // 2, (i % 2) * seq, seq, 3 + i))
    return names


def open_layer(w, inputs, window, layout):
    pad, taps, collect, biased = layout
    count = lax.axis_size("seq")
    both, seq = w["cb"].shape[0], w["ob"].shape[0]
    rows, width = inputs.shape[1:]
    layout = small_layout(both, seq)
    lines = [[] for _ in range(8)]
    for name, row, at, size, target in layout:
        lines[row].append(w[name].astype(F32))
    lines = [jnp.concatenate(parts) if parts else jnp.zeros((128,), F32) for parts in lines]
    small = jnp.stack([jnp.pad(line, (0, 128 - line.shape[0])) for line in lines])
    names = ("q", "k", "v", "p", "sq")
    any_spec = pl.BlockSpec(memory_space=pl.ANY)
    vmem_spec = pl.BlockSpec(memory_space=pltpu.VMEM)
    outs = pl.pallas_call(
        functools.partial(open_kernel, count, layout),
        in_specs=[any_spec] * 8 + [pl.BlockSpec(memory_space=pltpu.SMEM), vmem_spec],
        out_specs=[any_spec] * 5 + [vmem_spec] * 3 + [any_spec],
        out_shape=[
            *[jax.ShapeDtypeStruct((width, width), BF) for _ in range(4)],
            jax.ShapeDtypeStruct((width, w["sq"].shape[1]), BF),
            jax.ShapeDtypeStruct((16, width), F32),
            jax.ShapeDtypeStruct((1, 4 * width), F32),
            jax.ShapeDtypeStruct((3 * pad, width), BF),
            jax.ShapeDtypeStruct((rows, width), BF),
        ],
        scratch_shapes=[
            pltpu.VMEM((8 * 2 * count, 128), F32),
            pltpu.VMEM((3, 3 * pad, rows), BF),
            pltpu.VMEM((rows, width), BF),
            pltpu.VMEM((width, w["sq"].shape[1]), BF),
            pltpu.VMEM((3, 3 * pad, width), BF),
            pltpu.VMEM((3 * pad, width), F32),
            pltpu.SemaphoreType.DMA((4,)),
            *[pltpu.SemaphoreType.DMA] * 2,
            *gather_semaphores(count, 1 + len(halves(w["sq"].shape[0]))),
            *gather_semaphores(count, 4),
        ],
        compiler_params=pltpu.CompilerParams(collective_id=0, has_side_effects=True, vmem_limit_bytes=62 * MIB),
        name="open_layer",
    )(
        *[w[n] for n in names], small, inputs, jnp.asarray(np.ascontiguousarray(taps.transpose(0, 2, 1))), window, jnp.asarray(biased)
    )
    return dict(zip(names, outs), vec=outs[5], ub=outs[6]), outs[7], outs[8]


class Scatter:
    def __init__(self, place, view, order, sums, own, first, second, line, local_sem, send_sem, recv_sem):
        self.place, self.view = place, view
        self.by_y = order[0] == "y"
        self.late = order[2] == "z"
        self.sums, self.own, self.first, self.second, self.line = sums, own, first, second, line
        self.local_sem, self.send_sem, self.recv_sem = local_sem, send_sem, recv_sem
        self.f, self.g = (place.h, place.b) if self.by_y else (place.b, place.h)
        self.flips = (YFLIP, XFLIP) if self.by_y else (XFLIP, YFLIP)

    def index(self, f, g, a):
        return (f * 2 + g) * self.place.n + a

    def slot(self, f, g, a, c):
        h, b = (f, g) if self.by_y else (g, f)
        return h, self.place.seq_of(a, b, c)

    def remote(self, source, target, kind, send_at, recv_at):
        return pltpu.make_async_remote_copy(
            src_ref=source,
            dst_ref=target,
            send_sem=self.send_sem.at[send_at],
            recv_sem=self.recv_sem.at[recv_at],
            device_id=self.place.neighbour(kind),
            device_id_type=MESH,
        )

    def core_copy(self, i):
        return self.remote(self.sums.at[i], self.sums.at[i], CORE, i, i)

    def first_copy(self, g, a):
        n = self.place.n
        to = g * n + a
        return self.remote(self.sums.at[self.index(1 - self.f, g, a)], self.first.at[to], self.flips[0], 4 * n + to, 4 * n + to)

    def second_copy(self, a):
        n = self.place.n
        to = a if self.late else 0
        return self.remote(self.sums.at[self.index(self.f, 1 - self.g, a)], self.second.at[to], self.flips[1], 6 * n + to, 6 * n + to)

    def line_at(self, g, at):
        return at if self.late else g * (self.place.n + 1) + at

    def line_copy(self, kind, g, a):
        n = self.place.n
        to = self.line_at(g, a if kind == UP else jnp.where(a == self.place.a - 1, n, a))
        sent = 7 * n + (a if self.late else g * n + a)
        return self.remote(self.sums.at[self.index(self.f, g, a)], self.line.at[to], kind, sent, 7 * n + to)

    def line_wait(self, at):
        n = self.place.n
        self.remote(self.line.at[at], self.line.at[at], CORE, 7 * n, 7 * n + at).wait_recv()

    def piece(self, part, i):
        return (self.f if part >= 2 else 1 - self.f, self.g if part % 2 else 1 - self.g, self.place.along(i))

    def trade(self, part, i):
        f, g, a = self.piece(part, i)
        at = self.index(f, g, a)
        source = self.view(*self.slot(f, g, a, 1 - self.place.c))
        self.remote(source, self.sums.at[at], CORE, at, at).start()

    def load(self, part, i):
        source = self.view(*self.slot(*self.piece(part, i), self.place.c))
        return pltpu.make_async_copy(source, self.own.at[i % 4], self.local_sem.at[i % 4])

    def absorb(self, part, i):
        n = self.place.n
        f, g, a = self.piece(part, i)
        at = self.index(f, g, a)
        self.load(part, i).wait()
        self.core_copy(at).wait_recv()
        self.add(at, [(self.own, i % 4)])

        @pl.when(i + 4 < n)
        def _():
            self.load(part, i + 4).start()

        if part < 3:
            @pl.when(i + 4 >= n)
            def _():
                self.load(part + 1, i + 4 - n).start()

        if part < 2:
            self.first_copy(g, a).start()

    def after_first(self, g, a):
        self.first_copy(g, a).wait_recv()
        return self.index(self.f, g, a), [(self.first, g * self.place.n + a)]

    def add(self, i, refs):
        total = self.sums[i].astype(F32)
        for ref, at in refs:
            total = total + ref[at].astype(F32)
        self.sums[i] = total.astype(BF)

    def add_line(self, i, g):
        p = self.place
        for fed, at in ((p.a > 0, p.a), (p.a < p.n - 1, p.n)):
            @pl.when(fed)
            def _(at=self.line_at(g, at)):
                self.line_wait(at)
                self.add(i, [(self.line, at)])

    def flip_second(self, a):
        i, refs = self.after_first(1 - self.g, a)
        self.add(i, refs)
        if not self.late:
            self.add_line(i, 1 - self.g)
        self.second_copy(a).start()

    def move(self, g, d):
        p = self.place
        for kind, a, inside, fed in (
            (UP, p.a + d, p.a + d <= p.n - 1, p.a > 0),
            (DOWN, p.a - d, p.a - d >= 0, p.a < p.n - 1),
        ):
            @pl.when(inside)
            def _(kind=kind, a=a, fed=fed):
                i, refs = self.after_first(g, a)
                if self.late:
                    self.second_copy(a).wait_recv()
                    refs.append((self.second, a))
                self.add(i, refs)

                @pl.when(fed)
                def _():
                    at = self.line_at(g, a)
                    self.line_wait(at)
                    self.add(i, [(self.line, at)])

                self.line_copy(kind, g, a).start()

    def finish(self, store):
        p = self.place
        n = p.n
        i, refs = self.after_first(self.g, p.a)
        to = p.a if self.late else 0
        self.second_copy(p.a).wait_recv()
        self.add(i, refs + [(self.second, to)])
        self.add_line(i, self.g)
        store(self.sums[i].astype(F32))
        repeat(4 * n, lambda i: self.core_copy(i).wait_send())
        repeat(2 * n, lambda i: self.first_copy(i // n, i % n).wait_send())
        if self.late:
            repeat(n, lambda a: self.second_copy(a).wait_send())
        else:
            self.second_copy(p.a).wait_send()

        def line_done(a):
            for kind, inside in ((UP, a > p.a), (DOWN, a < p.a)):
                @pl.when(inside)
                def _(kind=kind):
                    for g in (self.g,) if self.late else (0, 1):
                        self.line_copy(kind, g, a).wait_send()

        repeat(n, line_done)


def scatter_scratch(count, shape, order):
    n = count // 4
    late = order[2] == "z"
    lines = n + 1 if late else 2 * n + 2
    return [
        *[pltpu.VMEM((k, *shape), BF) for k in (4 * n, 4, 2 * n, n if late else 1, lines)],
        pltpu.SemaphoreType.DMA((4,)),
        pltpu.SemaphoreType.DMA((9 * n,)),
        pltpu.SemaphoreType.DMA((7 * n + lines,)),
    ]


SCATTER_ORDERS = ("yzx", "xzy", "yxz", "xyz")


def block_scatters(rows, first):
    return [(at, size, SCATTER_ORDERS[(first + i) % 4]) for i, (at, size) in enumerate(halves(rows))]


def block_pairs(ref, rows, at, size, count):
    def view(h, s):
        return ref.at[pl.ds(pl.multiple_of((h * count + s) * rows + at, size), size)]

    return view


def square_pairs(ref, r, w):
    def view(h, s):
        return ref.at[pl.ds(pl.multiple_of(s * r, r), r), pl.ds(pl.multiple_of(h * w, w), w)]

    return view


def scatter_steps(place, units, stores, between=lambda at: None):
    n = place.n
    middle = [u for u in units if not u.late]
    late = [u for u in units if u.late]

    def each(run, some=units):
        def one(i):
            for unit in some:
                run(unit, i)

        return one

    def begin():
        for part in range(4):
            repeat(n, each(lambda u, i, part=part: u.trade(part, i)))
            if part == 0:
                repeat(4, each(lambda u, i: u.load(0, i).start()))
        between(0)

    def absorb(part):
        repeat(n, each(lambda u, i: u.absorb(part, i), middle + late))

    def second(d):
        for u in middle:
            u.move(1 - u.g, d)
        for u in late:
            u.flip_second(place.along(n - 1 - d))

    def third(d):
        for u in middle:
            u.move(u.g, d)

    def fourth():
        between(1)
        for u in late:
            u.flip_second(place.along(n - 1))
        for u in middle:
            u.flip_second(place.a)
        between(2)

    def fifth(d):
        for u in late:
            u.move(u.g, d)

    def finish():
        between(3)
        for unit, store in zip(units, stores):
            unit.finish(store)
        between(4)

    far = range(n - 1, 0, -1)
    return (
        [begin]
        + [functools.partial(absorb, part) for part in range(4)]
        + [functools.partial(second, d) for d in far]
        + [functools.partial(third, d) for d in far]
        + [fourth]
        + [functools.partial(fifth, d) for d in far]
        + [finish]
    )


def store_into(out):
    def store(value):
        out[...] = value

    return store


def scatter_dense_units(place, count, grads, outs, scratch):
    units, stores = [], []
    for ref, out, first in zip(grads, outs, (0, 2, 1)):
        rows = out.shape[0]
        for at, size, order in block_scatters(rows, first):
            units.append(Scatter(place, block_pairs(ref, rows, at, size, count), order, *scratch[:8]))
            stores.append(store_into(out.at[pl.ds(at, size)]))
            scratch = scratch[8:]
    return units, stores


def scatter_dense_scratch(count, shapes):
    scratch = []
    for (rows, width), first in zip(shapes, (0, 2, 1)):
        for at, size, order in block_scatters(rows, first):
            scratch += scatter_scratch(count, (size, width), order)
    return scratch


CLOSE_PLAN = (
    *(":memory", "m0", ":load", "m1", "m2", ":wait", "c0", "m3", "c1", "m4", "c2", "l0"),
    *("m5", "l1", "l2", "l3", "l4", "m6", "l5", ":out", "m7", "l6", "m8", "l7", ":rows", "l8", "m9", "l9"),
)


def close_kernel(
    count, gq, gk, gv, gp, sqw, dcb, dpb, dsb, vec, dub, dmade, dmem, dcur, dbl, masked, window, taps, outputs,
    q_out, k_out, v_out, p_out, sq_out, vec_out, ub_out, dx_out, rows_out,
    sums, parts, vec_send, vec_recv, returned, from_next, gsq, sq_scr, dcur_scr, dbl_scr, masked_scr, taps_scr,
    spread, dmasked, load_sem, row_send, row_recv, out_sem, out_send, out_recv, *scratch,
):
    place = Place(count)
    place.barrier(True)
    r, w = q_out.shape
    rows, width = spread.shape
    half = rows // 2
    units, stores = [], []
    for ref, out, order in zip((gq, gk, gv, gp), (q_out, k_out, v_out, p_out), SCATTER_ORDERS):
        units.append(Scatter(place, square_pairs(ref, r, w), order, *scratch[:8]))
        stores.append(store_into(out))
        scratch = scratch[8:]
    low_units, low_stores = [], []
    wide = sq_out.shape[0]
    for at, size, order in block_scatters(wide, 0):
        low_units.append(Scatter(place, block_pairs(gsq, wide, at, size, count), order, *scratch[:8]))
        low_stores.append(store_into(sq_out.at[pl.ds(at, size)]))
        scratch = scratch[8:]

    loads = [
        pltpu.make_async_copy(source, target, load_sem.at[i])
        for i, (source, target) in enumerate(
            (
                (taps, taps_scr), (masked.at[place.h], masked_scr), (sqw, sq_scr), (dcur, dcur_scr), (dbl, dbl_scr),
            )
        )
    ]

    pad = dmade.shape[0] // 3

    def rows_copy(i):
        here = pl.ds(i * pad, pad)
        return pltpu.make_async_remote_copy(
            src_ref=dmade.at[here] if i < 3 else dmem,
            dst_ref=returned.at[here] if i < 3 else from_next,
            send_sem=row_send.at[i],
            recv_sem=row_recv.at[i],
            device_id=(place.h, place.s + (i - 4 if i < 3 else -1)),
            device_id_type=MESH,
        )

    def exchange(i, source, target, wait=False):
        own = pltpu.make_async_copy(source.at[pl.ds(pl.multiple_of(place.h * half, half), half)], target.at[place.h], out_sem.at[i])
        other = pltpu.make_async_remote_copy(
            src_ref=source.at[pl.ds(pl.multiple_of((1 - place.h) * half, half), half)],
            dst_ref=target.at[place.h],
            send_sem=out_send.at[i],
            recv_sem=out_recv.at[i],
            device_id=place.neighbour(YFLIP),
            device_id_type=MESH,
        )
        if wait:
            own.wait()
            other.wait()
        else:
            other.start()
            own.start()

    def vec_copy(kind):
        return pltpu.make_async_remote_copy(
            src_ref=sums.at[kind],
            dst_ref=parts.at[kind],
            send_sem=vec_send.at[kind],
            recv_sem=vec_recv.at[kind],
            device_id=place.neighbour(kind),
            device_id_type=MESH,
        )

    def between(at):
        kinds = (CORE, XFLIP, YFLIP)
        if at == 0:
            sums[CORE, 0:16] = vec[...]
            sums[CORE, 0:1] = dcb[...]
            sums[CORE, 1:2] = dpb[...]
            sums[CORE, 2:3] = dsb[...]
            for i in range(4):
                sums[CORE, 12 + i : 13 + i] = dub[:, i * width : (i + 1) * width]
            vec_copy(CORE).start()
        elif at < 3:
            vec_copy(kinds[at - 1]).wait_recv()
            sums[kinds[at]] = sums[kinds[at - 1]] + parts[kinds[at - 1]]
            vec_copy(kinds[at]).start()
        elif at == 3:
            vec_copy(YFLIP).wait_recv()
            total = sums[YFLIP] + parts[YFLIP]
            ends = (place.a > 0, place.a < place.n - 1)
            sums[UP] = total
            sums[DOWN] = total
            for kind, fed in ((UP, ends[0]), (DOWN, ends[1])):
                @pl.when(fed)
                def _(kind=kind):
                    vec_copy(kind).wait_recv()
                    sums[kind] = sums[kind] + parts[kind]

                @place.when(kind)
                def _(kind=kind):
                    vec_copy(kind).start()
        else:
            total = sums[UP] + sums[DOWN] - (sums[YFLIP] + parts[YFLIP])
            both = vec_out.shape[1]
            k = place.h * count + place.s
            mine = pltpu.roll(total, lax.rem(width - k * both, width), 1)
            vec_out[...] = mine[:, :both]
            wide = ub_out.shape[1]
            flat = k * wide
            lanes = lax.rem(flat, width)
            mine = pltpu.roll(total, lax.rem(width - lanes, width), 1)[:, :wide]
            row = lax.broadcasted_iota(jnp.int32, mine.shape, 0)
            ub_out[...] = jnp.sum(jnp.where(row == 12 + flat // width, mine, 0.0), axis=0, keepdims=True)
            for kind in range(5):
                @place.when(kind)
                def _(kind=kind):
                    vec_copy(kind).wait_send()

    main = scatter_steps(place, units, stores, between)
    low = scatter_steps(place, low_units, low_stores)
    far = place.n - 1

    def give(i):
        @pl.when(place.inside(i - 4 if i < 3 else -1))
        def _():
            rows_copy(i).start()

        @pl.when(jnp.logical_not(place.inside(4 - i if i < 3 else 1)))
        def _():
            if i < 3:
                returned[i * pad : (i + 1) * pad] = jnp.zeros((pad, width), BF)
            else:
                from_next[...] = jnp.zeros_like(from_next)

    for i in range(3):
        give(i)

    def compressed(tap):
        cols = slice(tap * width, (tap + 1) * width)
        spread[...] = mm(taps_scr[tap], returned[...]).astype(BF)
        more = mm(spread[...], sq_scr[:, cols])
        if tap:
            more = more + dmasked[...]
        dmasked[...] = more
        gsq[:, cols] = mm_tn(spread[...], masked_scr[...]).astype(BF)

    def run(steps):
        for step in steps:
            step()

    def part(steps, k):
        cuts = [0, 1, 2, 3, 4, 5, 5 + far, 5 + 2 * far, 6 + 2 * far, 6 + 3 * far, 7 + 3 * far]
        run(steps[cuts[k] : cuts[k + 1]])

    def load_all():
        for load in loads:
            load.start()

    def wait_all():
        for load in loads:
            load.wait()
        masked_scr[...] = kept_rows(masked_scr[...], window)
        for i in range(3):
            @pl.when(place.inside(4 - i))
            def _(i=i):
                rows_copy(i).wait_recv()

    def send_rows():
        @pl.when(place.inside(1))
        def _():
            rows_copy(3).wait_recv()

        spread[...] = (dbl_scr[...] + dcur_scr[...] + from_next[...].astype(F32) + kept_rows(dmasked[...], window)).astype(BF)
        exchange(1, spread, dx_out)

    for item in CLOSE_PLAN:
        if item[0] == "m":
            part(main, int(item[1:]))
        elif item[0] == "l":
            part(low, int(item[1:]))
        elif item[0] == "c":
            compressed(int(item[1:]))
        else:
            {"load": load_all, "wait": wait_all, "rows": send_rows, "out": lambda: exchange(0, outputs, rows_out), "memory": lambda: give(3)}[item[1:]]()
    for i in range(4):
        @pl.when(place.inside(i - 4 if i < 3 else -1))
        def _(i=i):
            rows_copy(i).wait_send()
    exchange(0, outputs, rows_out, True)
    exchange(1, spread, dx_out, True)


def close_layer(g, w, layout, dmade, dmem, dcur, dbl, masked, window, outputs):
    pad, taps, collect, biased = layout
    count = lax.axis_size("seq")
    rows, width = dbl.shape
    both = width // (2 * count)
    square = (width // count, width // 2)
    tall = w["sq"].shape[1]
    scratch = []
    for order in SCATTER_ORDERS:
        scratch += scatter_scratch(count, square, order)
    for at, size, order in block_scatters(both, 0):
        scratch += scatter_scratch(count, (size, tall), order)
    vmem = pl.BlockSpec(memory_space=pltpu.VMEM)
    any_spec = pl.BlockSpec(memory_space=pl.ANY)
    outs = pl.pallas_call(
        functools.partial(close_kernel, count),
        in_specs=[any_spec] * 5 + [vmem] * 5 + [any_spec] * 5 + [pl.BlockSpec(memory_space=pltpu.SMEM)] + [any_spec] * 2,
        out_specs=[vmem] * 7 + [any_spec] * 2,
        out_shape=[jax.ShapeDtypeStruct(square, F32)] * 4
        + [jax.ShapeDtypeStruct(s, F32) for s in ((both, tall), (16, both), (1, 4 * both))]
        + [jax.ShapeDtypeStruct((2, rows // 2, width), BF)] * 2,
        scratch_shapes=[
            pltpu.VMEM((5, 16, width), F32),
            pltpu.VMEM((5, 16, width), F32),
            pltpu.SemaphoreType.DMA((5,)),
            pltpu.SemaphoreType.DMA((5,)),
            pltpu.VMEM((3 * pad, width), BF),
            pltpu.VMEM((rows, width), BF),
            pltpu.VMEM((width, tall), BF),
            pltpu.VMEM((width, tall), BF),
            pltpu.VMEM((rows, width), F32),
            pltpu.VMEM((rows, width), F32),
            pltpu.VMEM((rows, width), BF),
            pltpu.VMEM((3, rows, 3 * pad), BF),
            pltpu.VMEM((rows, width), BF),
            pltpu.VMEM((rows, width), F32),
            pltpu.SemaphoreType.DMA((5,)),
            *[pltpu.SemaphoreType.DMA((4,))] * 2,
            *[pltpu.SemaphoreType.DMA((2,))] * 3,
            *scratch,
        ],
        compiler_params=pltpu.CompilerParams(collective_id=2, has_side_effects=True, vmem_limit_bytes=62 * MIB),
        name="close_layer",
    )(
        g["q"], g["k"], g["v"], g["p"], w["sq"], g["cb"], g["pb"], g["sb"], g["sums"], g["ub"],
        dmade, dmem, dcur, dbl, masked, window, jnp.asarray(taps), outputs,
    )
    final = dict(zip(("q", "k", "v", "p", "sq"), outs[:5]))
    final.update({n: outs[5][i] for i, n in enumerate(VECTORS)})
    final["ub"] = outs[6].reshape(4 * both)
    return final, outs[7], outs[8]


FORWARD_SHARE = 0.25


def attend_forward_kernel(
    count, window, vec_ref, in1_ref, both, table_ref, wq_ref, wk_ref, wv_ref, wp_ref,
    collect, made, up, down, o,
    out_ref, p_ref, cq_ref, pq_ref, k_ref, v_ref, pl_ref, in_t_ref, up_f, down_f, o_f,
    s_scr, x_scr, arriving, in0_ref, in2_ref, bias_ref, in_sem, row_send, row_recv, *sems,
):
    turn, turns = pl.program_id(0), pl.num_programs(0)
    place = Place(count)
    units = []
    for shard, full, first in ((up, up_f, 0), (down, down_f, 2), (o, o_f, 1)):
        units += block_units(shard, full, count, first)
    gather = Gather(place, units, *sems)
    first, *steps, last = gather.steps()
    heads = cq_ref.shape[1] // HD
    rows, keys = cq_ref.shape[0], k_ref.shape[0]
    width = in2_ref.shape[1]
    pad = arriving.shape[0] // 3
    scale = HD ** (-0.5)
    points = 2 + heads
    ahead = int(len(steps) * FORWARD_SHARE)
    early = spread_steps(steps[:ahead], 4)
    plan = [[]] * 2 + spread_steps(steps[ahead:], turns * points - 3) + [[]]

    def run(chosen):
        for step in chosen:
            step()

    def point(k):
        for t in range(turns):
            if t * points + k and plan[t * points + k - 1]:
                @pl.when(turn == t)
                def _(chosen=plan[t * points + k - 1]):
                    run(chosen)

    def rows_copy(i):
        here = pl.ds(i * pad, pad)
        return pltpu.make_async_remote_copy(
            src_ref=made.at[here],
            dst_ref=arriving.at[here],
            send_sem=row_send.at[i],
            recv_sem=row_recv.at[i],
            device_id=(place.h, place.s + 4 - i),
            device_id_type=MESH,
        )

    @pl.when(turn == 0)
    def _():
        load = pltpu.make_async_copy(both.at[place.h], in2_ref, in_sem)
        load.start()
        place.barrier(True)
        for i in range(3):
            @pl.when(place.inside(4 - i))
            def _(i=i):
                rows_copy(i).start()

            @pl.when(jnp.logical_not(place.inside(i - 4)))
            def _(i=i):
                arriving[i * pad : (i + 1) * pad] = jnp.zeros((pad, width), BF)

        first()
        bias_ref[...] = key_bias(rows, window)
        load.wait()

    point(0)
    query = mm(in2_ref[...], wq_ref[...])
    cq_ref[...] = ((query + vec_ref[0:1]) * scale).astype(BF)
    pq_ref[...] = ((query + vec_ref[1:2]) * scale).astype(BF)

    def project(i, source):
        here = slice(i * rows, (i + 1) * rows)
        k_ref[here] = mm(source[...], wk_ref[...]).astype(BF)
        v_ref[here] = mm(source[...], wv_ref[...]).astype(BF)

    def ahead_of_rows(k):
        @pl.when(turn == 0)
        def _():
            run(early[k])

    project(1, in1_ref)
    ahead_of_rows(0)
    project(2, in2_ref)
    ahead_of_rows(1)
    for i in range(3):
        here = slice(i * rows, (i + 1) * rows)
        pl_ref[here] = mm(table_ref[here], wp_ref[...]).astype(BF)
    ahead_of_rows(2)
    point(1)

    @pl.when(turn == 0)
    def _():
        run(early[3])
        for i in range(3):
            @pl.when(place.inside(i - 4))
            def _(i=i):
                rows_copy(i).wait_recv()
        in0_ref[...] = mm(collect[...], arriving[...]).astype(BF)

    project(0, in0_ref)
    for i, source in enumerate((in0_ref, in1_ref, in2_ref)):
        @pl.when(turn == i + 1)
        def _(source=source, here=slice(i * rows, (i + 1) * rows)):
            in_t_ref[:, here] = source[...].T
    step = 32
    for head in range(heads):
        point(2 + head)
        cols = slice(head * HD, (head + 1) * HD)
        s_scr[...] = mm_nt(cq_ref[:, cols], k_ref[:, cols])
        x_scr[...] = mm_nt(pq_ref[:, cols], pl_ref[:, cols])
        for start in range(0, rows, step):
            here = slice(start, start + step)
            located = pltpu.roll(x_scr[here], (start + keys - rows + 1) % keys, 1, stride=1, stride_axis=0)
            scores = s_scr[here] + located + bias_ref[...]
            early, own = scores[:, : 2 * rows], scores[:, 2 * rows :]
            row = start + lax.broadcasted_iota(jnp.int32, own.shape, 0)
            col = lax.broadcasted_iota(jnp.int32, own.shape, 1)
            own = jnp.where(col <= row, own, -1e30)
            top = jnp.maximum(jnp.max(early, axis=1, keepdims=True), jnp.max(own, axis=1, keepdims=True))
            early, own = jnp.exp(early - top), jnp.exp(own - top)
            total = jnp.sum(early, axis=1, keepdims=True) + jnp.sum(own, axis=1, keepdims=True)
            share = 1.0 / total
            p_ref[head, here, : 2 * rows] = (early * share).astype(BF)
            p_ref[head, here, 2 * rows :] = (own * share).astype(BF)
        out_ref[:, cols] = mm(p_ref[head], v_ref[:, cols]).astype(BF)

    @pl.when(turn == turns - 1)
    def _():
        for i in range(3):
            @pl.when(place.inside(4 - i))
            def _(i=i):
                rows_copy(i).wait_send()
        last()


def attend_forward(window, memory, inputs, made, table, layout, w, shards):
    pad, taps, collect, biased = layout
    count = lax.axis_size("seq")
    rows, width = memory.shape
    keys = 3 * rows
    pair = 2 * HD
    names = ("up", "down", "o")

    def whole(shape):
        return pl.BlockSpec(shape, lambda t: (0,) * len(shape), pipeline_mode=pl.Buffered(1))

    def columns(height):
        return pl.BlockSpec((height, pair), lambda t: (0, t))

    any_spec = pl.BlockSpec(memory_space=pl.ANY)
    outs = pl.pallas_call(
        functools.partial(attend_forward_kernel, count),
        grid=(width // pair,),
        in_specs=[pl.BlockSpec(memory_space=pltpu.SMEM), columns(16), whole((rows, width)), any_spec, whole((keys, width))]
        + [columns(width)] * 4
        + [whole((rows, 3 * pad))]
        + [any_spec] * 4,
        out_specs=[columns(rows), pl.BlockSpec((2, rows, keys), lambda t: (t, 0, 0))]
        + [columns(rows)] * 2
        + [columns(keys)] * 3
        + [pl.BlockSpec((width, keys), lambda t: (0, 0))]
        + [any_spec] * 3,
        out_shape=[
            jax.ShapeDtypeStruct((rows, width), BF),
            jax.ShapeDtypeStruct((width // HD, rows, keys), BF),
            *[jax.ShapeDtypeStruct((rows, width), BF)] * 2,
            *[jax.ShapeDtypeStruct((keys, width), BF)] * 3,
            jax.ShapeDtypeStruct((width, keys), BF),
            *[jax.ShapeDtypeStruct((shards[n].shape[0] * 2 * count, width), BF) for n in names],
        ],
        scratch_shapes=[
            pltpu.VMEM((rows, keys), F32),
            pltpu.VMEM((rows, keys), F32),
            pltpu.VMEM((3 * pad, width), BF),
            *[pltpu.VMEM((rows, width), BF)] * 2,
            pltpu.VMEM((1, keys), F32),
            pltpu.SemaphoreType.DMA,
            pltpu.SemaphoreType.DMA((3,)),
            pltpu.SemaphoreType.DMA((3,)),
            *gather_semaphores(count, sum(len(halves(shards[n].shape[0])) for n in names)),
        ],
        compiler_params=pltpu.CompilerParams(collective_id=3, has_side_effects=True, vmem_limit_bytes=62 * MIB),
        name="attend_forward",
    )(
        window, w["vec"], memory, inputs, table, w["q"], w["k"], w["v"], w["p"],
        jnp.asarray(collect), made, *[shards[n] for n in names],
    )
    return outs[:8], dict(zip(names, outs[8:]))


BACKWARD_PLAN = (
    (0, 0), (0, 1), (0, 2), (1, 1), (1, 2),
    (3, 0), (3, 3), (4, 1),
    (5, 0), (5, 2), (5, 3),
    (6, 1),
    (7, 0), (7, 1), (7, 3),
)


def attend_backward_kernel(
    count, cq_ref, pq_ref, k_ref, v_ref, pl_ref, p_ref, do_ref, in_t_ref, table_t_ref, wq_ref, wk_ref, wv_ref, collect_t, up, down, o,
    dcb_ref, dpb_ref, gq_ref, gk_ref, gv_ref, gp_ref, dsb_ref, dmade_ref, up_out, down_out, o_out, dmem_out, dcur_out,
    dp_scr, ds_scr, dq_scr, dk_scr, dv_scr, dpl_scr, total, out_sem, *scratch,
):
    head, heads = pl.program_id(0), pl.num_programs(0)
    place = Place(count)
    units, stores = scatter_dense_units(place, count, (up, down, o), (up_out, down_out, o_out), scratch)
    first, *steps, last = scatter_steps(place, units, stores)
    plan = {at: [] for at in BACKWARD_PLAN}
    plan[BACKWARD_PLAN[0]] = [place.barrier, first]
    for i, step in enumerate(steps):
        plan[BACKWARD_PLAN[min(1 + i * (len(BACKWARD_PLAN) - 1) // len(steps), len(BACKWARD_PLAN) - 1)]].append(step)

    def point(k):
        for (t, at), chosen in plan.items():
            if at == k:
                @pl.when(head == t)
                def _(chosen=chosen):
                    for step in chosen:
                        step()

    rows, keys = cq_ref.shape[0], k_ref.shape[0]
    scale = HD ** (-0.5)
    block = 128
    flip = (
        lax.broadcasted_iota(jnp.int32, (block, block), 0)
        + lax.broadcasted_iota(jnp.int32, (block, block), 1)
        == block - 1
    ).astype(BF)
    point(0)
    dp_scr[...] = mm_nt(do_ref[...], v_ref[...])
    step = 32
    for start in range(0, rows, step):
        here = slice(start, start + step)
        prob = p_ref[0, here].astype(F32)
        dprob = dp_scr[here]
        delta = jnp.sum(prob * dprob, axis=1, keepdims=True)
        ds_scr[here] = (prob * (dprob - delta)).astype(BF)
    point(1)
    side = head % 2
    dv_scr[side] = mm_tn(do_ref[...], p_ref[0]).T.astype(BF)
    dk_scr[side] = mm_tn(cq_ref[...], ds_scr[...]).T.astype(BF)
    dcq = mm(ds_scr[...], k_ref[...]) * scale
    flipped = []
    for start in range(0, rows, block):
        here = slice(start, start + block)
        dp_scr[here] = mm(flip, ds_scr[here])
        flipped.append(mm(flip, pq_ref[here]).astype(BF))
        ds_scr[here] = pltpu.roll(dp_scr[here], rows - block - start, 1, stride=1, stride_axis=0).astype(BF)
    dpl_scr[side] = mm_tn(jnp.concatenate(flipped, axis=0), ds_scr[...]).T.astype(BF)
    dpq_flipped = mm(ds_scr[...], pl_ref[...]) * scale
    dpq = []
    for start in range(0, rows, block):
        piece = dpq_flipped[start : start + block]
        high = piece.astype(BF)
        dpq.append(mm(flip, high) + mm(flip, (piece - high.astype(F32)).astype(BF)))
    dpq = jnp.concatenate(dpq, axis=0)
    dq_scr[side] = (dcq + dpq).astype(BF)
    dcb_ref[...] = jnp.sum(dcq, axis=0, keepdims=True)
    dpb_ref[...] = jnp.sum(dpq, axis=0, keepdims=True)
    point(2)

    @pl.when(side == 1)
    def _():
        dq, dk, dv, dpl = (jnp.concatenate([ref[0], ref[1]], axis=1) for ref in (dq_scr, dk_scr, dv_scr, dpl_scr))
        gk_ref[...] = mm(in_t_ref[...], dk).astype(BF)
        gv_ref[...] = mm(in_t_ref[...], dv).astype(BF)
        gp_ref[...] = mm(table_t_ref[...], dpl).astype(BF)
        gq_ref[...] = mm(in_t_ref[:, 2 * rows :], dq).astype(BF)
        point(3)

        @pl.when(head == 1)
        def _():
            total[...] = jnp.zeros_like(total)

        for start in range(0, keys, rows):
            here = slice(start, start + rows)
            more = mm_nt(dk[here], wk_ref[...]) + mm_nt(dv[here], wv_ref[...])
            if start == 2 * rows:
                more = more + mm_nt(dq, wq_ref[...])
            total[here] += more

    width = total.shape[1]

    @pl.when(head == heads - 1)
    def _():
        own = pltpu.make_async_copy(total.at[pl.ds(2 * rows, rows)], dcur_out, out_sem.at[0])
        own.start()
        ds_scr[:, :width] = total[rows : 2 * rows].astype(BF)
        back = pltpu.make_async_copy(ds_scr.at[:, pl.ds(0, width)], dmem_out, out_sem.at[1])
        back.start()
        dsq = total[:rows].astype(BF)
        dsb_ref[...] = jnp.sum(dsq.astype(F32), axis=0, keepdims=True)
        dmade_ref[...] = mm(collect_t[...], dsq).astype(BF)
        last()
        own.wait()
        back.wait()


def attend_backward(saved, probs, d_out, inputs_t, table_t, layout, w, dense):
    pad, taps, collect, biased = layout
    count = lax.axis_size("seq")
    rows, width = d_out.shape
    keys = inputs_t.shape[1]
    heads = width // HD
    names = ("up", "down", "o")
    shapes = [(dense[n].shape[0] // (2 * count), width) for n in names]

    def whole(shape):
        return pl.BlockSpec(shape, lambda h: (0,) * len(shape), pipeline_mode=pl.Buffered(1))

    def columns(height):
        return pl.BlockSpec((height, HD), lambda h: (0, h))

    pair = pl.BlockSpec((width, 2 * HD), lambda h: (0, h // 2))
    any_spec = pl.BlockSpec(memory_space=pl.ANY)
    vmem = pl.BlockSpec(memory_space=pltpu.VMEM)
    outs = pl.pallas_call(
        functools.partial(attend_backward_kernel, count),
        grid=(heads,),
        in_specs=[columns(rows)] * 2
        + [columns(keys)] * 3
        + [pl.BlockSpec((1, rows, keys), lambda h: (h, 0, 0)), columns(rows), whole((width, keys)), whole((width, keys))]
        + [pair] * 3
        + [whole((3 * pad, rows))]
        + [any_spec] * 3,
        out_specs=[columns(1)] * 2 + [pair] * 4 + [pl.BlockSpec((1, width), lambda h: (0, 0)), vmem] + [vmem] * 3 + [any_spec] * 2,
        out_shape=[
            *[jax.ShapeDtypeStruct((1, width), F32)] * 2,
            *[jax.ShapeDtypeStruct((width, width), BF)] * 4,
            jax.ShapeDtypeStruct((1, width), F32),
            jax.ShapeDtypeStruct((3 * pad, width), BF),
            *[jax.ShapeDtypeStruct(shape, F32) for shape in shapes],
            jax.ShapeDtypeStruct((rows, width), BF),
            jax.ShapeDtypeStruct((rows, width), F32),
        ],
        scratch_shapes=[
            pltpu.VMEM((rows, keys), F32),
            pltpu.VMEM((rows, keys), BF),
            pltpu.VMEM((2, rows, HD), BF),
            *[pltpu.VMEM((2, keys, HD), BF)] * 3,
            pltpu.VMEM((keys, width), F32),
            pltpu.SemaphoreType.DMA((2,)),
            *scatter_dense_scratch(count, shapes),
        ],
        compiler_params=pltpu.CompilerParams(collective_id=1, has_side_effects=True, vmem_limit_bytes=62 * MIB),
        name="attend_backward",
    )(
        *saved, probs, d_out, inputs_t, table_t, w["q"], w["k"], w["v"],
        jnp.asarray(np.ascontiguousarray(collect.T)), *[dense[n] for n in names],
    )
    grads = dict(zip(("cb", "pb", "q", "k", "v", "p", "sb"), outs))
    return grads, dict(zip(names, outs[8:11])), (outs[7], *outs[11:])


def normalize(values):
    centre = values - jnp.mean(values, axis=-1, keepdims=True)
    spread = jnp.mean(centre * centre, axis=-1, keepdims=True)
    scale = lax.rsqrt(spread + epsilon)
    return centre * scale, scale


def normalize_back(grad, gain, unit, scale):
    pulled = grad * gain
    return scale * (
        pulled
        - jnp.mean(pulled, axis=-1, keepdims=True)
        - unit * jnp.mean(pulled * unit, axis=-1, keepdims=True)
    )


def gelu_parts(u):
    root = np.float32(np.sqrt(2.0 / np.pi))
    square = u * u
    tanh = jnp.tanh(u * (root + (root * 0.044715) * square))
    half = 0.5 * u
    value = half + half * tanh
    slope = 0.5 + 0.5 * tanh + half * (1.0 - tanh * tanh) * (root + (3 * 0.044715 * root) * square)
    return value, slope


VECTORS = ("cb", "pb", "sb", "ob", "g1", "s1", "db", "g2", "s2")


def feed_kernel(
    att_ref, x_all, ct_all, wo_ref, up_ref, down_ref, ub_ref, vec_ref,
    out_ref, gup_ref, gdown_ref, go_ref, dub_ref, sums_ref, dbl_ref, datt_ref,
    unit, scale, normed, acc, hidden, slope, dy, dy_low, x_ref, ct_ref, load_sem,
):
    turn = pl.program_id(0)
    chunks = pl.num_programs(0) // 2
    rows = att_ref.shape[0]
    at = {name: slice(i, i + 1) for i, name in enumerate(VECTORS)}

    def by_rows(run):
        repeat(rows // 128, lambda k: run(pl.ds(pl.multiple_of(k * 128, 128), 128)))

    def tally(name, values):
        sums_ref[at[name]] += jnp.sum(values, axis=0, keepdims=True)

    book = lax.axis_index("head")
    x_load = pltpu.make_async_copy(x_all.at[book], x_ref, load_sem.at[0])
    ct_load = pltpu.make_async_copy(ct_all.at[book], ct_ref, load_sem.at[1])

    @pl.when(turn == 0)
    def _():
        x_load.start()
        ct_load.start()
        sums_ref[...] = jnp.zeros_like(sums_ref)
        acc[...] = mm(att_ref[...], wo_ref[...])
        x_load.wait()

        def first(here):
            unit[here], scale[here] = normalize(x_ref[here].astype(F32) + acc[here] + vec_ref[at["ob"]])
            normed[here] = (unit[here] * vec_ref[at["g1"]] + vec_ref[at["s1"]]).astype(BF)
            acc[here] = jnp.zeros_like(acc[here])

        by_rows(first)

    @pl.when(turn < chunks)
    def _():
        value, slope_here = gelu_parts(mm_nt(normed[...], up_ref[...]) + ub_ref[...])
        hidden[turn] = value.astype(BF)
        slope[turn] = slope_here.astype(BF)
        acc[...] += mm(hidden[turn], down_ref[...])

    @pl.when(turn == chunks - 1)
    def _():
        ct_load.wait()

        def second(here):
            unit2, scale2 = normalize(normed[here].astype(F32) + acc[here] + vec_ref[at["db"]])
            out_ref[here] = (unit2 * vec_ref[at["g2"]] + vec_ref[at["s2"]]).astype(BF)
            ct = ct_ref[here].astype(F32)
            tally("g2", ct * unit2)
            tally("s2", ct)
            dy[here] = normalize_back(ct, vec_ref[at["g2"]], unit2, scale2)
            tally("db", dy[here])
            dy_low[here] = dy[here].astype(BF)
            acc[here] = jnp.zeros_like(acc[here])

        by_rows(second)

    @pl.when(turn >= chunks)
    def _():
        j = 2 * chunks - 1 - turn
        gdown_ref[...] = mm_tn(hidden[j], dy_low[...]).astype(BF)
        du = (mm_nt(dy_low[...], down_ref[...]) * slope[j].astype(F32)).astype(BF)
        dub_ref[...] = jnp.sum(du.astype(F32), axis=0, keepdims=True)
        gup_ref[...] = mm_tn(du, normed[...]).astype(BF)
        acc[...] += mm(du, up_ref[...])

    @pl.when(turn == 2 * chunks - 1)
    def _():
        def third(here):
            dnormed = dy[here] + acc[here]
            tally("g1", dnormed * unit[here])
            tally("s1", dnormed)
            dbl = normalize_back(dnormed, vec_ref[at["g1"]], unit[here], scale[here])
            tally("ob", dbl)
            dbl_ref[here] = dbl
            dy_low[here] = dbl.astype(BF)

        by_rows(third)
        go_ref[...] = mm_tn(att_ref[...], dy_low[...]).astype(BF)
        datt_ref[...] = mm_nt(dy_low[...], wo_ref[...]).astype(BF)


def feed(attended, x, ct, w):
    rows, width = attended.shape
    hidden = w["up"].shape[0]
    size = 1024
    chunks = hidden // size

    def whole(shape):
        return pl.BlockSpec(shape, lambda t: (0,) * len(shape), pipeline_mode=pl.Buffered(1))

    def kept(shape):
        return pl.BlockSpec(shape, lambda t: (0,) * len(shape))

    def weight(t):
        return jnp.where(t < chunks, t, 2 * chunks - 1 - t)

    def grad(t):
        return jnp.where(t < chunks, chunks - 1, 2 * chunks - 1 - t)

    outs = pl.pallas_call(
        feed_kernel,
        grid=(2 * chunks,),
        in_specs=[whole((rows, width))]
        + [pl.BlockSpec(memory_space=pl.ANY)] * 2
        + [whole((width, width))]
        + [pl.BlockSpec((size, width), lambda t: (weight(t), 0))] * 2
        + [pl.BlockSpec((1, size), lambda t: (0, weight(t))), whole((16, width))],
        out_specs=[kept((rows, width))]
        + [pl.BlockSpec((size, width), lambda t: (grad(t), 0))] * 2
        + [kept((width, width)), pl.BlockSpec((1, size), lambda t: (0, grad(t))), kept((16, width))]
        + [kept((rows, width))] * 2,
        out_shape=[
            jax.ShapeDtypeStruct((rows, width), BF),
            *[jax.ShapeDtypeStruct((hidden, width), BF)] * 2,
            jax.ShapeDtypeStruct((width, width), BF),
            jax.ShapeDtypeStruct((1, hidden), F32),
            jax.ShapeDtypeStruct((16, width), F32),
            jax.ShapeDtypeStruct((rows, width), F32),
            jax.ShapeDtypeStruct((rows, width), BF),
        ],
        scratch_shapes=[
            pltpu.VMEM((rows, width), F32),
            pltpu.VMEM((rows, 1), F32),
            pltpu.VMEM((rows, width), BF),
            pltpu.VMEM((rows, width), F32),
            pltpu.VMEM((chunks, rows, size), BF),
            pltpu.VMEM((chunks, rows, size), BF),
            pltpu.VMEM((rows, width), F32),
            *[pltpu.VMEM((rows, width), BF)] * 3,
            pltpu.SemaphoreType.DMA((2,)),
        ],
        compiler_params=pltpu.CompilerParams(vmem_limit_bytes=62 * MIB),
        name="feed",
    )(attended, x, ct, w["o"], w["up"], w["down"], w["ub"], w["vec"])
    outputs, gup, gdown, go, dub, sums, dbl, datt = outs
    return outputs, dict(up=gup, down=gdown, o=go, ub=dub, sums=sums), dbl, datt


def results_kernel(*refs):
    count = (len(refs) - 2) // 3
    sources, targets, blocks = (refs[i * count : (i + 1) * count] for i in range(3))
    turned, sem = refs[3 * count :]
    for i in range(count):
        pltpu.make_async_copy(sources[i], blocks[i], sem.at[i]).start()
    for i in range(count):
        pltpu.make_async_copy(sources[i], blocks[i], sem.at[i]).wait()
        if not i:
            turned[...] = blocks[0][...].T
        pltpu.make_async_copy(blocks[i] if i else turned, targets[i], sem.at[i]).start()
    for i in range(count):
        pltpu.make_async_copy(blocks[i] if i else turned, targets[i], sem.at[i]).wait()


def results(first, rest):
    any_spec = pl.BlockSpec(memory_space=pl.ANY)
    arrays = [first, *rest]
    shapes = [first.shape[::-1], *[a.shape for a in rest]]
    return pl.pallas_call(
        results_kernel,
        in_specs=[any_spec] * len(arrays),
        out_specs=[any_spec] * len(arrays),
        out_shape=[jax.ShapeDtypeStruct(shape, a.dtype) for shape, a in zip(shapes, arrays)],
        scratch_shapes=[
            *[pltpu.VMEM(a.shape, a.dtype) for a in arrays],
            pltpu.VMEM(first.shape[::-1], first.dtype),
            pltpu.SemaphoreType.DMA((len(arrays),)),
        ],
        compiler_params=pltpu.CompilerParams(vmem_limit_bytes=62 * MIB),
        name="results",
    )(*arrays)


def body(
    inputs, lengths,
    query_weight, key_weight, value_weight, position_weight, content_bias, position_bias,
    output_weight, output_bias, first_gain, first_shift, up_weight, up_bias, down_weight, down_bias,
    second_gain, second_shift, squeeze_weight, squeeze_bias, cotangent,
):
    seq = lax.axis_index("seq")
    head = lax.axis_index("head")
    rows, width = inputs.shape[2:]

    book_lengths = lax.dynamic_index_in_dim(lengths, head, 0, keepdims=False)
    padded_lengths = jnp.concatenate([jnp.zeros((4,), jnp.int32), book_lengths])
    window = lax.dynamic_slice_in_dim(padded_lengths, seq, 5, 0)
    x = inputs[:, 0]
    layout = squeeze_layout(rows)
    shards = dict(
        q=query_weight, k=key_weight, v=value_weight, p=position_weight,
        o=output_weight, up=up_weight.T, down=down_weight, sq=squeeze_weight.T,
        cb=content_bias, pb=position_bias, ob=output_bias, g1=first_gain, s1=first_shift, ub=up_bias,
        db=down_bias, g2=second_gain, s2=second_shift, sb=squeeze_bias,
    )
    w, made, memory = open_layer(shards, x, window, layout)

    table = table_rows(width, 3 * rows)
    (attended, probs, *saved, keys_in_t), dense = attend_forward(
        window, memory, x, made, jnp.asarray(table), layout, w, shards
    )
    w.update(dense)

    outputs, grads, dblended, dattended = feed(attended, x, cotangent[:, 0], w)

    more, final, (dmade, dmemory, dcurrent) = attend_backward(
        saved, probs, dattended, keys_in_t, jnp.asarray(np.ascontiguousarray(table.T)), layout, w, grads
    )
    more, input_rows, output_rows = close_layer(
        {**grads, **more}, w, layout, dmade, dmemory, dcurrent, dblended, x, window, outputs
    )
    final.update(more)
    names = ("down", "o", "q", "k", "v", "p", "sq")
    final["up"], output_rows, input_rows, *rest = results(final["up"], [output_rows, input_rows, *[final[n] for n in names]])
    final.update(zip(names, rest))
    return (
        output_rows[:, None], input_rows[:, None],
        final["q"], final["k"], final["v"], final["p"], final["cb"], final["pb"],
        final["o"], final["ob"], final["g1"], final["s1"], final["up"], final["ub"],
        final["down"], final["db"], final["g2"], final["s2"], final["sq"].T, final["sb"],
    )


def solution(mesh):
    both = ("head", "seq")
    matrix = P("seq", "head")
    in_specs = (
        P(None, "seq", None, None), P(), matrix, matrix, matrix, matrix, P(both), P(both),
        P(both, None), P("seq"), P("seq"), P("seq"), P(None, both), P(both), P(both, None), P("seq"),
        P("seq"), P("seq"), P(None, both), P(both), P(None, "seq", None, None),
    )
    rows = P(None, "seq", "head", None)
    out_specs = (
        rows, rows, matrix, matrix, matrix, matrix, P(both), P(both),
        P(both, None), P(both), P(both), P(both), P(None, both), P(both), P(both, None), P(both),
        P(both), P(both), P(None, both), P(both),
    )
    return jax.shard_map(body, mesh=mesh, in_specs=in_specs, out_specs=out_specs, check_vma=False)
```
